128 devices in a mesh: group: 4 (over z), dev: 32 (over y, x, core).
Axes of the slice: x: 4, y: 4, z: 4, core: 2. Of those that a mesh axis runs over, the one named last changes fastest.
Arguments:
- query_hidden: bfloat16 [256, 32, 768], P(('group', 'dev')), may hold values from -6 to 6
- passage_hidden: bfloat16 [16384, 48, 768], P(('group', 'dev')), may hold values from -6 to 6
- head_weight: bfloat16 [768, 128], replicated, may hold values from -0.21875 to 0.21875
- teacher: float32 [256, 64], P(('group', 'dev')), may hold values from -9 to 9
- candidates: int32 [256, 64], P(('group', 'dev')), may hold values from 0 to 4095, as said below
- storage: int32 [4, 4096], P('group'), may hold values from 0 to 4095, as said below
- lengths: int32 [4, 4096], P('group'), may hold values from 12 to 48
Outputs:
- query_loss: float32 [256], P(('group', 'dev'))
- head_grad: float32 [768, 128], replicated
- query_grad: bfloat16 [256, 32, 768], P(('group', 'dev'))
- passage_grad: bfloat16 [16384, 48, 768], P(('group', 'dev'))
The draws below stay inside these ranges and needn't reach their ends.
Inputs may be any that keep to these rules, and one draw needn't show every extreme that they name: Of the candidates of the 2 queries on one device, at most 12 have a storage position on any one device of the group (storage position // 128); in every group one device stores exactly 12 of the candidates of every device of that group. Each row is a permutation: row g gives each passage of group g its storage position within the group.
All inputs are finite; a program needn't handle non-finite values.
Results may differ from the reference program's by a relative error of at most 0.0082.
Values may be sent and summed in bfloat16 or wider, within the bound.
No kernel may reach another device: no remote copies, remote signals or barrier semaphores. Data moves between devices by JAX's collectives and lax.ppermute only.
A program may use at most 128 MiB of HBM per device.

```python
import jax
import jax.numpy as jnp
from jax import lax

D = 768
DIM = 128
QLEN = 32
PLEN = 48
CAND = 64
Q_DEV = 2
P_DEV = 128
REQ_DEV = 128
CAP = 12
PG = 4096
QUERIES = 256
PASSAGES = 16384
N_GROUP = 4
N_DEV = 32


def layout_perm(key):
    group_keys = jax.random.split(key, N_GROUP)
    return jax.vmap(lambda one_key: jax.random.permutation(one_key, PG))(group_keys)


def draw_storage(key, part):
    return layout_perm(key).astype(jnp.int32)


def draw_candidates(key, part):
    storage_perm = layout_perm(key)
    key = jax.random.fold_in(key, 7)
    hot_key, shift_key, slot_key, mix_key = jax.random.split(key, 4)
    devices_all = N_GROUP * N_DEV
    hot_owner = jax.random.randint(hot_key, (N_GROUP,), 0, N_DEV)
    group_of = jnp.arange(devices_all, dtype=jnp.int32) // N_DEV
    hot_rows = hot_owner[group_of][:, None]
    offsets = jax.random.randint(shift_key, (devices_all, 1), 0, N_DEV - 1)
    request_order = jnp.arange(REQ_DEV, dtype=jnp.int32)[None, :]
    spread = (hot_rows + 1 + (request_order - CAP + offsets) % (N_DEV - 1)) % N_DEV
    owner_dev = jnp.where(request_order < CAP, hot_rows, spread)
    slot_index = jax.random.randint(slot_key, (devices_all, REQ_DEV), 0, P_DEV)
    position = owner_dev * P_DEV + slot_index
    mix_keys = jax.random.split(mix_key, devices_all)
    shuffled = jax.vmap(lambda one_key, row_values: jax.random.permutation(one_key, row_values))(mix_keys, position)
    inverse_perm = jnp.argsort(storage_perm, axis=1)
    chosen = inverse_perm[group_of[:, None], shuffled]
    return chosen.reshape(devices_all * Q_DEV, CAND).astype(jnp.int32)


def touch_ends(drawn, own_key, smallest, high):
    index_at = [jax.random.randint(jax.random.fold_in(own_key, axis), (), 0, length) for axis, length in enumerate(drawn.shape)]
    main_axis = drawn.shape.index(max(drawn.shape))
    beside = index_at[:main_axis] + [(index_at[main_axis] + 1) % drawn.shape[main_axis]] + index_at[main_axis + 1:]
    return drawn.at[tuple(index_at)].set(smallest).at[tuple(beside)].set(high)


def shard_levels(stream_key, shape, shards, smallest, top_value):
    def one(dim, blocks):
        heights = jax.random.uniform(jax.random.fold_in(jax.random.fold_in(stream_key, 6), dim), (blocks,), jnp.float32, smallest / len(shards), top_value / len(shards))
        return jnp.repeat(jnp.exp(heights), shape[dim] // blocks).reshape((-1,) + (1,) * (len(shape) - dim - 1))

    loudness = one(*shards[0])
    for cut in shards[1:]:
        loudness = loudness * one(*cut)
    return loudness


def noise(key, shape, width, bound, cuts=(), kind=jnp.bfloat16):
    factor_of = shard_levels(key, shape, cuts, -0.22, 0.18) if cuts else 1.0
    values = jax.random.normal(key, shape, jnp.float32) * width * factor_of
    return jnp.minimum(jnp.maximum(values, -bound), bound).astype(kind)


def setup_inputs(seed: int = 0) -> dict:
    key_list = jax.random.split(jax.random.key(seed), 8)
    return {
        "query_hidden": noise(key_list[0], (QUERIES, QLEN, D), 1.0, 6.0, ((0, 128),)),
        "passage_hidden": noise(key_list[1], (PASSAGES, PLEN, D), 1.0, 6.0, ((0, 128),)),
        "head_weight": noise(key_list[2], (D, DIM), D ** -0.5, 0.21875),
        "teacher": noise(key_list[3], (QUERIES, CAND), 3.0, 9.0, ((0, 128),), jnp.float32),
        "candidates": draw_candidates(jax.random.fold_in(key_list[7], 71), 0),
        "storage": draw_storage(jax.random.fold_in(key_list[7], 71), 0),
        "lengths": touch_ends(jax.random.randint(key_list[6], (N_GROUP, PG), PLEN // 4, PLEN + 1), jax.random.fold_in(key_list[6], 1), PLEN // 4, PLEN).astype(jnp.int32),
    }


TAU = 0.0625
LOSS_SCALE = 32768.0
EPS = 1e-06

def normalize(hidden, weight):
    projected = jnp.dot(hidden, weight, preferred_element_type=jnp.float32)
    inverse = lax.rsqrt(lax.optimization_barrier(jnp.sum(projected * projected, axis=-1, keepdims=True)) + EPS)
    return (projected * inverse, inverse)

def unnormalize(upstream, unit_rows, inverse):
    radial = lax.optimization_barrier(jnp.sum(unit_rows * upstream, axis=-1, keepdims=True))
    return ((upstream - unit_rows * radial) * inverse).astype(jnp.bfloat16)

def soft_scores(queries, passages, valid_mask):
    similar = jnp.einsum('...ik,...jk->...ij', queries.astype(jnp.float32), passages.astype(jnp.float32))
    exponent = jnp.exp(similar / TAU) * valid_mask[..., None, :].astype(jnp.float32)
    denominator = lax.optimization_barrier(jnp.sum(exponent, axis=-1))
    return (TAU * lax.optimization_barrier(jnp.sum(jnp.log(denominator), axis=-1)), exponent / denominator[..., None])

def distill(scores, teacher):
    teach_log = teacher - jnp.log(lax.optimization_barrier(jnp.sum(jnp.exp(teacher), axis=-1, keepdims=True)))
    student_log = scores - jnp.log(lax.optimization_barrier(jnp.sum(jnp.exp(scores), axis=-1, keepdims=True)))
    teach_prob = jnp.exp(teach_log)
    query_loss = lax.optimization_barrier(jnp.sum(teach_prob * (teach_log - student_log), axis=-1))
    return (query_loss, LOSS_SCALE * (jnp.exp(student_log) - teach_prob))

def reference(query_hidden, passage_hidden, head_weight, teacher, candidates, storage, lengths):
    slabs = passage_hidden.reshape(PASSAGES // P_DEV, P_DEV * PLEN, D)

    def encode_slab(slab_rows):
        unit_rows, _ = normalize(slab_rows, head_weight)
        return unit_rows.astype(jnp.bfloat16)
    encoded = lax.map(encode_slab, slabs).reshape(PASSAGES, PLEN, DIM)
    query_flat = query_hidden.reshape(QUERIES * QLEN, D)
    query_unit, query_inverse = normalize(query_flat, head_weight)
    query_enc = query_unit.astype(jnp.bfloat16).reshape(QUERIES, QLEN, DIM)
    group_of = jnp.arange(QUERIES, dtype=jnp.int32) // (Q_DEV * N_DEV)
    stored_at = (storage[group_of[:, None], candidates] + group_of[:, None] * PG).astype(jnp.int32)
    valid_all = jnp.arange(PLEN, dtype=jnp.int32)[None, :] < lengths.reshape(-1)[:, None]

    def forward(entries):
        query_one, stored = entries
        score_row, _ = soft_scores(query_one[None], encoded[stored], valid_all[stored])
        return score_row
    scores = lax.map(forward, (query_enc, stored_at))
    query_loss, score_pull = distill(scores, teacher)

    def backward(accum, entries):
        query_one, stored, pull_row = entries
        cand_embed = encoded[stored]
        _, weights = soft_scores(query_one[None], cand_embed, valid_all[stored])
        mixed = (pull_row[:, None, None] * weights).astype(jnp.bfloat16).astype(jnp.float32)
        query_delta = jnp.einsum('cij,cjk->ik', mixed, cand_embed.astype(jnp.float32))
        cand_delta = jnp.einsum('cij,ik->cjk', mixed, query_one.astype(jnp.float32)).astype(jnp.bfloat16)
        accum = accum.at[stored].add(cand_delta.astype(jnp.float32))
        return (accum, query_delta)
    empty_grad = jnp.zeros((PASSAGES, PLEN, DIM), jnp.float32)
    passage_delta, query_delta = lax.scan(backward, empty_grad, (query_enc, stored_at, score_pull))
    contraction = (((0,), (0,)), ((), ()))
    transposed = (((1,), (1,)), ((), ()))

    def passage_back(entries):
        slab_rows, upstream = entries
        unit_rows, inverse = normalize(slab_rows, head_weight)
        preact = unnormalize(upstream, unit_rows, inverse)
        hidden_delta = lax.dot_general(preact, head_weight, transposed, preferred_element_type=jnp.float32)
        head_delta = lax.dot_general(slab_rows, preact, contraction, preferred_element_type=jnp.float32)
        return (hidden_delta.astype(jnp.bfloat16), head_delta)
    passage_grad, head_parts = lax.map(passage_back, (slabs, passage_delta.reshape(PASSAGES // P_DEV, P_DEV * PLEN, DIM)))
    query_preact = unnormalize(query_delta.reshape(QUERIES * QLEN, DIM), query_unit, query_inverse)
    query_grad = lax.dot_general(query_preact, head_weight, transposed, preferred_element_type=jnp.float32)
    head_grad = lax.optimization_barrier(jnp.sum(head_parts, axis=0)) + lax.dot_general(query_flat, query_preact, contraction, preferred_element_type=jnp.float32)
    return (query_loss, head_grad, query_grad.astype(jnp.bfloat16).reshape(QUERIES, QLEN, D), passage_grad.reshape(PASSAGES, PLEN, D))
```

```python
import jax
import jax.numpy as jnp
from jax import lax
from jax.experimental import pallas as pl
from jax.experimental.pallas import tpu as pltpu
from jax.sharding import PartitionSpec as P

TAU = 0.0625
LOSS_SCALE = 32768.0
EPS = 1e-06

N_DEV = 32
N_ALL = 128
STORED = 128
PLEN = 48
QLEN = 32
D = 768
DIM = 128
PER_QUERY = 64
CAP = 12
SLOTS = 16
WIDE = CAP * PLEN
QROWS = 2 * QLEN
META = 16
CHUNK = 4
BLOCK = 768
STEPS = STORED * PLEN // BLOCK
HEAD_TILES = D // 8

BF = jnp.bfloat16
F32 = jnp.float32
ROWS_ROWS = (((0,), (0,)), ((), ()))
COLS_COLS = (((1,), (1,)), ((), ()))
VMEM = pl.BlockSpec(memory_space=pltpu.VMEM)
SMEM = pl.BlockSpec(memory_space=pltpu.SMEM)


def params():
    return pltpu.CompilerParams(vmem_limit_bytes=50 * 1024 * 1024)


def dot(a, b, dims=(((1,), (0,)), ((), ()))):
    return lax.dot_general(a, b, dims, preferred_element_type=F32)


def iota(shape, axis):
    return lax.broadcasted_iota(jnp.int32, shape, axis)


def split3(x):
    hi = x.astype(BF).astype(F32)
    mid = (x - hi).astype(BF).astype(F32)
    return hi, mid, (x - hi - mid)


def expander(copies):
    row = iota((DIM, WIDE), 0)
    slot = (row & (SLOTS - 1)) * PLEN
    lane = iota((DIM, WIDE), 1)
    hit = (lane >= slot) & (lane < slot + PLEN) & (row < copies * SLOTS)
    return jnp.where(hit, 1.0, 0.0)


def request_kernel(hidden_ref, weight_ref, teacher_ref, cand_ref, storage_ref, lengths_ref,
                   send_ref, proj_ref, const_ref, place_ref, length_ref):
    for i in range(N_DEV):
        place_ref[i : i + 1, :] = storage_ref[0:1, i * STORED : (i + 1) * STORED]
        length_ref[i : i + 1, :] = lengths_ref[0:1, i * STORED : (i + 1) * STORED]
    proj = dot(hidden_ref[...], weight_ref[...])
    proj_ref[...] = proj
    inverse = lax.rsqrt(jnp.sum(proj * proj, axis=-1, keepdims=True) + EPS)
    embed = (proj * inverse).astype(BF)

    teacher = teacher_ref[...]
    log_t = teacher - jnp.log(jnp.sum(jnp.exp(teacher), axis=-1, keepdims=True))
    prob = jnp.exp(log_t)
    const = jnp.sum(prob * log_t, axis=-1, keepdims=True)
    const_ref[...] = jnp.concatenate(
        [jnp.broadcast_to(const, (2, DIM)), jnp.zeros((6, DIM), F32)], axis=0
    )
    prob_row = jnp.concatenate([prob[0:1], prob[1:2]], axis=1)
    cand = cand_ref[...]
    cand_row = jnp.concatenate([cand[0:1], cand[1:2]], axis=1)

    place = place_ref[...]
    owner_table = (place >> 7).astype(F32).astype(BF)
    slot_table = (place & (STORED - 1)).astype(F32).astype(BF)
    length_table = length_ref[...].astype(F32).astype(BF)
    sub32 = iota((N_DEV, DIM), 0)
    sub128 = iota((DIM, DIM), 0)
    lane128 = iota((DIM, DIM), 1)
    high = jnp.where(sub32 == (cand_row >> 7), 1.0, 0.0).astype(BF)
    low = sub128 == (cand_row & (STORED - 1))
    owner = jnp.sum(jnp.where(low, dot(owner_table, high, ROWS_ROWS), 0.0), axis=0, keepdims=True)
    slot = jnp.sum(jnp.where(low, dot(slot_table, high, ROWS_ROWS), 0.0), axis=0, keepdims=True)
    match = jnp.where(sub32 == owner.astype(jnp.int32), 1.0, 0.0)
    match_bf = match.astype(BF)
    at_slot = sub128 == slot.astype(jnp.int32)
    length = jnp.sum(
        jnp.where(at_slot, dot(length_table, match_bf, ROWS_ROWS), 0.0), axis=0, keepdims=True
    )
    earlier = jnp.where(sub128 < lane128, 1.0, 0.0).astype(BF)
    rank = jnp.sum(match * dot(match_bf, earlier), axis=0, keepdims=True).astype(jnp.int32)
    t_hi, t_mid, t_lo = split3(prob_row)
    which = jnp.where(iota((1, DIM), 1) >= PER_QUERY, 1.0, 0.0)
    fields = (slot, which, length, t_hi, t_mid, t_lo, jnp.ones((1, DIM), F32))
    field_of = sub128 >> 4
    values = jnp.zeros((DIM, DIM), F32)
    for f, row in enumerate(fields):
        values = jnp.where(field_of == f, row, values)
    values = jnp.where((sub128 & (SLOTS - 1)) == rank, values, 0.0).astype(BF)
    meta = dot(match_bf, values, COLS_COLS)
    for s in range(N_DEV):
        send_ref[s, 0:QROWS, :] = embed
        send_ref[s, QROWS : QROWS + META, :] = jnp.broadcast_to(meta[s : s + 1], (META, DIM)).astype(BF)


def encode_kernel(hidden_ref, weight_ref, proj_ref, embed_ref):
    proj = dot(hidden_ref[...], weight_ref[...])
    proj_ref[...] = proj
    inverse = lax.rsqrt(jnp.sum(proj * proj, axis=-1, keepdims=True) + EPS)
    embed_ref[...] = (proj * inverse).astype(BF)


def stored_rows(embed_ref, place_ref, s):
    parts = []
    for k in range(CAP):
        start = pl.multiple_of(place_ref[s, k], 16)
        parts.append(embed_ref[pl.ds(start, PLEN), :])
    return jnp.concatenate(parts, axis=0)


def score_kernel(recv_ref, embed_ref, expo_ref, recip_ref, sums_ref, table_ref, second_ref, place_ref,
                 meta_ref, limit_ref, smem_ref, sem):
    for s in range(N_DEV):
        rows = recv_ref[s, QROWS : QROWS + META, :].astype(F32)
        meta_ref[s : s + 1, :] = rows[0:1, :]
    meta = meta_ref[...]
    place_ref[...] = meta.astype(jnp.int32) * PLEN
    copy = pltpu.make_async_copy(place_ref, smem_ref, sem)
    copy.start()
    meta_bf = meta.astype(BF)
    spread = expander(1)
    second_ref[...] = dot(pltpu.roll(meta, DIM - SLOTS, 1).astype(BF), spread.astype(BF))
    length = dot(pltpu.roll(meta, DIM - 2 * SLOTS, 1).astype(BF), spread.astype(BF))
    lane = iota((1, WIDE), 1)
    token = lane
    for k in range(1, CAP):
        token = token - jnp.where(lane >= k * PLEN, PLEN, 0)
    limit_ref[...] = jnp.where(token.astype(F32) < length, 1.0, 0.0)
    copy.wait()

    def chunk(i, carry):
        for u in range(CHUNK):
            s = i * CHUNK + u
            queries = recv_ref[s, 0:QROWS, :]
            sims = dot(queries, stored_rows(embed_ref, smem_ref, s), COLS_COLS)
            second = second_ref[pl.ds(s, 1), :]
            valid = limit_ref[pl.ds(s, 1), :]
            mine = jnp.where(second > 0.5, sims[QLEN:QROWS], sims[0:QLEN])
            expo = jnp.where(valid > 0.5, jnp.exp(mine * (1.0 / TAU)), 0.0)
            expo_ref[pl.ds(pl.multiple_of(s * QLEN, QLEN), QLEN), :] = expo.astype(BF)
        return carry

    lax.fori_loop(0, N_DEV // CHUNK, chunk, 0)
    total = dot(expo_ref[...], spread.astype(BF), COLS_COLS)
    total = jnp.where(total > 0.0, total, 1.0)
    recip_ref[...] = 1.0 / total
    scores = TAU * jnp.sum(jnp.log(total).reshape(N_DEV, QLEN, DIM), axis=1)
    lane = iota((N_DEV, DIM), 1)
    present = (pltpu.roll(meta, DIM - 6 * SLOTS, 1) > 0.5) & (lane < SLOTS)
    teach = (
        pltpu.roll(meta, DIM - 3 * SLOTS, 1)
        + pltpu.roll(meta, DIM - 4 * SLOTS, 1)
        + pltpu.roll(meta, DIM - 5 * SLOTS, 1)
    )
    teach = jnp.where(present, teach, 0.0)
    student = jnp.where(present, jnp.exp(scores), 0.0)
    which = pltpu.roll(meta, DIM - SLOTS, 1) > 0.5
    table_ref[0] = student
    table_ref[1] = teach
    table_ref[2] = jnp.where(which, 1.0, 0.0)
    gain = teach * scores
    columns = []
    for value in (student, gain):
        columns.append(jnp.sum(jnp.where(which, 0.0, value), axis=-1, keepdims=True))
        columns.append(jnp.sum(jnp.where(which, value, 0.0), axis=-1, keepdims=True))
    mixed = jnp.zeros((N_DEV, DIM), F32)
    for j, column in enumerate(columns):
        mixed = jnp.where(lane == j, column, mixed)
    mixed = jnp.concatenate([mixed, jnp.zeros((DIM - N_DEV, DIM), F32)], axis=0)
    part = jnp.transpose(mixed)[0:8, :]
    for s in range(N_DEV):
        sums_ref[s] = part


def query_kernel(sums_ref, const_ref, me_ref, table_ref, second_ref, expo_ref, recip_ref, embed_ref, place_ref,
                 send_ref, mixed_ref, loss_ref, pull_ref):
    sums = jnp.sum(sums_ref[...], axis=0)
    log_sum = jnp.log(jnp.where(sums > 0.0, sums, 1.0))
    loss = const_ref[0:2, :] + log_sum[0:2, :] - sums[2:4, :]
    picked = jnp.where(iota((2, DIM), 1) == me_ref[0], loss, 0.0)
    loss_ref[...] = jnp.broadcast_to(jnp.sum(picked, axis=-1, keepdims=True), (2, DIM))
    turned = jnp.transpose(jnp.concatenate([sums, jnp.zeros((DIM - 8, DIM), F32)], axis=0))[0:N_DEV, :]
    normal = jnp.where(table_ref[2] > 0.5, turned[:, 1:2], turned[:, 0:1])
    pull_ref[...] = LOSS_SCALE * (table_ref[0] / normal - table_ref[1])
    spread = expander(2).astype(BF)
    lane = iota((QLEN, DIM), 1)

    def chunk(i, carry):
        scaled = []
        for u in range(CHUNK):
            s = i * CHUNK + u
            rows = pl.ds(pl.multiple_of(s * QLEN, QLEN), QLEN)
            factor = recip_ref[rows, :] * pull_ref[pl.ds(s, 1), :]
            hi = factor.astype(BF).astype(F32)
            lo = factor - hi
            scaled.append(jnp.where(lane < SLOTS, hi, pltpu.roll(lo, SLOTS, 1)).astype(BF))
        wide = dot(jnp.concatenate(scaled, axis=0), spread)
        rows = pl.ds(pl.multiple_of(i * (CHUNK * QLEN), CHUNK * QLEN), CHUNK * QLEN)
        mixed = expo_ref[rows, :].astype(F32) * wide
        mixed_ref[rows, :] = mixed.astype(BF)
        for u in range(CHUNK):
            s = i * CHUNK + u
            one = mixed[u * QLEN : (u + 1) * QLEN]
            second = second_ref[pl.ds(s, 1), :] > 0.5
            both = jnp.concatenate(
                [jnp.where(second, 0.0, one).astype(BF), jnp.where(second, one, 0.0).astype(BF)], axis=0
            )
            send_ref[s] = dot(both, stored_rows(embed_ref, place_ref, s)).astype(BF)
        return carry

    lax.fori_loop(0, N_DEV // CHUNK, chunk, 0)


def stored_kernel(place_ref, hidden_ref, proj_ref, weight_ref, recv_ref, mixed_ref, second_ref,
                  grad_ref, head_ref, delta_ref, acc_ref):
    step = pl.program_id(0)

    @pl.when(step == 0)
    def _():
        delta_ref[...] = jnp.zeros_like(delta_ref)
        acc_ref[...] = jnp.zeros_like(acc_ref)

        def chunk(i, carry):
            for u in range(CHUNK):
                s = i * CHUNK + u
                one = mixed_ref[pl.ds(pl.multiple_of(s * QLEN, QLEN), QLEN), :].astype(F32)
                second = second_ref[pl.ds(s, 1), :] > 0.5
                both = jnp.concatenate(
                    [jnp.where(second, 0.0, one).astype(BF), jnp.where(second, one, 0.0).astype(BF)], axis=0
                )
                part = dot(both, recv_ref[s, 0:QROWS, :], ROWS_ROWS)
                for k in range(CAP):
                    at = pl.ds(pl.multiple_of(place_ref[s, k], 16), PLEN)
                    delta_ref[at, :] += part[k * PLEN : (k + 1) * PLEN]
            return carry

        lax.fori_loop(0, N_DEV // CHUNK, chunk, 0)

    proj = proj_ref[...]
    delta = delta_ref[pl.ds(pl.multiple_of(step * BLOCK, BLOCK), BLOCK), :]
    inverse = lax.rsqrt(jnp.sum(proj * proj, axis=-1, keepdims=True) + EPS)
    unit = proj * inverse
    radial = jnp.sum(unit * delta, axis=-1, keepdims=True)
    preact = ((delta - unit * radial) * inverse).astype(BF)
    grad_ref[...] = dot(preact, weight_ref[...], COLS_COLS).astype(BF)
    acc_ref[...] += dot(preact, hidden_ref[...], ROWS_ROWS)

    @pl.when(step == STEPS - 1)
    def _():
        head_ref[...] = jnp.transpose(acc_ref[...])


def finish_kernel(recv_ref, hidden_ref, weight_ref, proj_ref, head_ref, grad_ref, send_ref):
    delta = jnp.sum(recv_ref[...].astype(F32), axis=0)
    proj = proj_ref[...]
    inverse = lax.rsqrt(jnp.sum(proj * proj, axis=-1, keepdims=True) + EPS)
    unit = proj * inverse
    radial = jnp.sum(unit * delta, axis=-1, keepdims=True)
    preact = ((delta - unit * radial) * inverse).astype(BF)
    grad_ref[...] = dot(preact, weight_ref[...], COLS_COLS).astype(BF)
    head = head_ref[...] + dot(hidden_ref[...], preact, ROWS_ROWS)
    send_ref[0:HEAD_TILES] = head.reshape(HEAD_TILES, 8, DIM).astype(BF)
    send_ref[HEAD_TILES:N_ALL] = jnp.zeros((N_ALL - HEAD_TILES, 8, DIM), BF)


def reduce_kernel(recv_ref, send_ref):
    total = jnp.sum(recv_ref[...].astype(F32), axis=0).astype(BF)
    send_ref[...] = jnp.broadcast_to(total[None], (N_ALL, 8, DIM))


def shape(dims, kind):
    return jax.ShapeDtypeStruct(dims, kind)


def exchange(x, axes):
    return lax.all_to_all(x, axes, split_axis=0, concat_axis=0, tiled=True)


def on_device(query_hidden, passage_hidden, head_weight, teacher, candidates, storage, lengths):
    query_flat = query_hidden.reshape(QROWS, D)
    flat_hidden = passage_hidden.reshape(STORED * PLEN, D)
    send, query_proj, const = pl.pallas_call(
        request_kernel,
        out_shape=(
            shape((N_DEV, QROWS + META, DIM), BF),
            shape((QROWS, DIM), F32),
            shape((8, DIM), F32),
        ),
        in_specs=[VMEM] * 6,
        out_specs=(VMEM,) * 3,
        scratch_shapes=[pltpu.VMEM((N_DEV, DIM), jnp.int32)] * 2,
        compiler_params=params(),
        name="request",
    )(query_flat, head_weight, teacher, candidates, storage, lengths)
    recv = exchange(send, "dev")

    proj, embed = pl.pallas_call(
        encode_kernel,
        grid=(STEPS,),
        out_shape=(shape((STORED * PLEN, DIM), F32), shape((STORED * PLEN, DIM), BF)),
        in_specs=[
            pl.BlockSpec((BLOCK, D), lambda i: (i, 0)),
            pl.BlockSpec((D, DIM), lambda i: (0, 0)),
        ],
        out_specs=(
            pl.BlockSpec((BLOCK, DIM), lambda i: (i, 0)),
            pl.BlockSpec((BLOCK, DIM), lambda i: (i, 0)),
        ),
        cost_estimate=pl.CostEstimate(flops=2 * 6144 * D * DIM, bytes_accessed=15_000_000, transcendentals=0),
        compiler_params=params(),
        name="encode",
    )(flat_hidden, head_weight)

    expo, recip, sums, table, second, place = pl.pallas_call(
        score_kernel,
        out_shape=(
            shape((N_DEV * QLEN, WIDE), BF),
            shape((N_DEV * QLEN, DIM), F32),
            shape((N_DEV, 8, DIM), F32),
            shape((3, N_DEV, DIM), F32),
            shape((N_DEV, WIDE), F32),
            shape((N_DEV, DIM), jnp.int32),
        ),
        in_specs=[VMEM] * 2,
        out_specs=(VMEM,) * 6,
        scratch_shapes=[
            pltpu.VMEM((N_DEV, DIM), F32),
            pltpu.VMEM((N_DEV, WIDE), F32),
            pltpu.SMEM((N_DEV, DIM), jnp.int32),
            pltpu.SemaphoreType.DMA,
        ],
        compiler_params=params(),
        name="score",
    )(recv, embed)
    all_sums = exchange(sums, "dev")

    me = lax.axis_index("dev").astype(jnp.int32).reshape(1)
    send_delta, mixed, loss = pl.pallas_call(
        query_kernel,
        out_shape=(
            shape((N_DEV, QROWS, DIM), BF),
            shape((N_DEV * QLEN, WIDE), BF),
            shape((2, DIM), F32),
        ),
        in_specs=[VMEM, VMEM, SMEM, VMEM, VMEM, VMEM, VMEM, VMEM, SMEM],
        out_specs=(VMEM,) * 3,
        scratch_shapes=[pltpu.VMEM((N_DEV, DIM), F32)],
        compiler_params=params(),
        name="query",
    )(all_sums, const, me, table, second, expo, recip, embed, place)
    recv_delta = exchange(send_delta, "dev")

    whole = lambda *dims: pl.BlockSpec(dims, lambda i: (0,) * len(dims))
    passage_grad, head = pl.pallas_call(
        stored_kernel,
        grid=(STEPS,),
        out_shape=(shape((STORED * PLEN, D), BF), shape((D, DIM), F32)),
        in_specs=[
            SMEM,
            pl.BlockSpec((BLOCK, D), lambda i: (i, 0)),
            pl.BlockSpec((BLOCK, DIM), lambda i: (i, 0)),
            whole(D, DIM),
            whole(N_DEV, QROWS + META, DIM),
            whole(N_DEV * QLEN, WIDE),
            whole(N_DEV, WIDE),
        ],
        out_specs=(pl.BlockSpec((BLOCK, D), lambda i: (i, 0)), whole(D, DIM)),
        scratch_shapes=[pltpu.VMEM((STORED * PLEN, DIM), F32), pltpu.VMEM((DIM, D), F32)],
        cost_estimate=pl.CostEstimate(flops=6 * 6144 * D * DIM, bytes_accessed=24_000_000, transcendentals=0),
        compiler_params=params(),
        name="stored",
    )(place, flat_hidden, proj, head_weight, recv, mixed, second)

    query_grad, send_head = pl.pallas_call(
        finish_kernel,
        out_shape=(shape((QROWS, D), BF), shape((N_ALL, 8, DIM), BF)),
        in_specs=[VMEM] * 5,
        out_specs=(VMEM,) * 2,
        compiler_params=params(),
        name="finish",
    )(recv_delta, query_flat, head_weight, query_proj, head)
    recv_head = exchange(send_head, ("group", "dev"))
    send_total = pl.pallas_call(
        reduce_kernel,
        out_shape=shape((N_ALL, 8, DIM), BF),
        in_specs=[VMEM],
        out_specs=VMEM,
        compiler_params=params(),
        name="reduce",
    )(recv_head)
    head_all = exchange(send_total, ("group", "dev"))
    head_grad = head_all[:HEAD_TILES].reshape(D, DIM).astype(F32)
    return (
        loss[:, 0],
        head_grad,
        query_grad.reshape(2, QLEN, D),
        passage_grad.reshape(STORED, PLEN, D),
    )


def solution(mesh):
    return jax.shard_map(
        on_device,
        mesh=mesh,
        in_specs=(
            P(("group", "dev"), None, None),
            P(("group", "dev"), None, None),
            P(),
            P(("group", "dev"), None),
            P(("group", "dev"), None),
            P("group", None),
            P("group", None),
        ),
        out_specs=(
            P(("group", "dev")),
            P(),
            P(("group", "dev"), None, None),
            P(("group", "dev"), None, None),
        ),
        check_vma=False,
    )
```

```python
import jax
import jax.numpy as jnp
from jax import lax
from jax.experimental import pallas as pl
from jax.experimental.pallas import tpu as pltpu
from jax.sharding import PartitionSpec as P

TAU = 0.0625
LOSS_SCALE = 32768.0
EPS = 1e-06

N_DEV = 32
N_ALL = 128
STORED = 128
PLEN = 48
QLEN = 32
D = 768
DIM = 128
PER_QUERY = 64
CAP = 12
SLOTS = 16
WIDE = CAP * PLEN
QROWS = 2 * QLEN
META = 16
CHUNK = 4
TOKENS = STORED * PLEN
BLOCK = 1536
STEPS = TOKENS // BLOCK
LANES = 4
PART = 768
PARTS = TOKENS // PART
AHEAD = 3
HEAD_TILES = D // 8

BF = jnp.bfloat16
F32 = jnp.float32
ROWS_ROWS = (((0,), (0,)), ((), ()))
COLS_COLS = (((1,), (1,)), ((), ()))
VMEM = pl.BlockSpec(memory_space=pltpu.VMEM)
SMEM = pl.BlockSpec(memory_space=pltpu.SMEM)
HBM = pl.BlockSpec(memory_space=pltpu.HBM)


def params(mib):
    return pltpu.CompilerParams(vmem_limit_bytes=mib * 1024 * 1024)


def dot(a, b, dims=(((1,), (0,)), ((), ()))):
    return lax.dot_general(a, b, dims, preferred_element_type=F32)


def iota(shape, axis):
    return lax.broadcasted_iota(jnp.int32, shape, axis)


def start_copies(pairs, sems):
    copies = [pltpu.make_async_copy(a, b, sems.at[i]) for i, (a, b) in enumerate(pairs)]
    for copy in copies:
        copy.start()
    return copies


def wait_copies(copies):
    for copy in copies:
        copy.wait()


def split3(x):
    hi = x.astype(BF).astype(F32)
    mid = (x - hi).astype(BF).astype(F32)
    return hi, mid, (x - hi - mid)


def expander(copies):
    row = iota((DIM, WIDE), 0)
    slot = (row & (SLOTS - 1)) * PLEN
    lane = iota((DIM, WIDE), 1)
    hit = (lane >= slot) & (lane < slot + PLEN) & (row < copies * SLOTS)
    return jnp.where(hit, 1.0, 0.0)


def request_kernel(hidden_hbm, weight_hbm, teacher_hbm, cand_hbm, storage_hbm, lengths_hbm,
                   send_ref, proj_hbm, const_hbm,
                   hidden_ref, weight_ref, teacher_ref, cand_ref, storage_ref, lengths_ref,
                   place_ref, length_ref, proj_ref, const_ref, sems, out_sems):
    small = start_copies(
        (
            (cand_hbm, cand_ref),
            (storage_hbm, storage_ref),
            (lengths_hbm, lengths_ref),
            (teacher_hbm, teacher_ref),
            (weight_hbm, weight_ref),
            (hidden_hbm, hidden_ref),
        ),
        sems,
    )
    wait_copies(small)
    for i in range(N_DEV):
        place_ref[i : i + 1, :] = storage_ref[0:1, i * STORED : (i + 1) * STORED]
        length_ref[i : i + 1, :] = lengths_ref[0:1, i * STORED : (i + 1) * STORED]
    proj = dot(hidden_ref[...], weight_ref[...])
    proj_ref[...] = proj
    inverse = lax.rsqrt(jnp.sum(proj * proj, axis=-1, keepdims=True) + EPS)
    embed = (proj * inverse).astype(BF)

    teacher = teacher_ref[...]
    log_t = teacher - jnp.log(jnp.sum(jnp.exp(teacher), axis=-1, keepdims=True))
    prob = jnp.exp(log_t)
    const = jnp.sum(prob * log_t, axis=-1, keepdims=True)
    const_ref[...] = jnp.concatenate(
        [jnp.broadcast_to(const, (2, DIM)), jnp.zeros((6, DIM), F32)], axis=0
    )
    outs = start_copies(((proj_ref, proj_hbm), (const_ref, const_hbm)), out_sems)
    prob_row = jnp.concatenate([prob[0:1], prob[1:2]], axis=1)
    cand = cand_ref[...]
    cand_row = jnp.concatenate([cand[0:1], cand[1:2]], axis=1)

    place = place_ref[...]
    owner_table = (place >> 7).astype(F32).astype(BF)
    slot_table = (place & (STORED - 1)).astype(F32).astype(BF)
    length_table = length_ref[...].astype(F32).astype(BF)
    sub32 = iota((N_DEV, DIM), 0)
    sub128 = iota((DIM, DIM), 0)
    lane128 = iota((DIM, DIM), 1)
    high = jnp.where(sub32 == (cand_row >> 7), 1.0, 0.0).astype(BF)
    low = sub128 == (cand_row & (STORED - 1))
    owner = jnp.sum(jnp.where(low, dot(owner_table, high, ROWS_ROWS), 0.0), axis=0, keepdims=True)
    slot = jnp.sum(jnp.where(low, dot(slot_table, high, ROWS_ROWS), 0.0), axis=0, keepdims=True)
    match = jnp.where(sub32 == owner.astype(jnp.int32), 1.0, 0.0)
    match_bf = match.astype(BF)
    at_slot = sub128 == slot.astype(jnp.int32)
    length = jnp.sum(
        jnp.where(at_slot, dot(length_table, match_bf, ROWS_ROWS), 0.0), axis=0, keepdims=True
    )
    earlier = jnp.where(sub128 < lane128, 1.0, 0.0).astype(BF)
    rank = jnp.sum(match * dot(match_bf, earlier), axis=0, keepdims=True).astype(jnp.int32)
    t_hi, t_mid, t_lo = split3(prob_row)
    which = jnp.where(iota((1, DIM), 1) >= PER_QUERY, 1.0, 0.0)
    fields = (slot, which, length, t_hi, t_mid, t_lo, jnp.ones((1, DIM), F32))
    field_of = sub128 >> 4
    values = jnp.zeros((DIM, DIM), F32)
    for f, row in enumerate(fields):
        values = jnp.where(field_of == f, row, values)
    values = jnp.where((sub128 & (SLOTS - 1)) == rank, values, 0.0).astype(BF)
    meta = dot(match_bf, values, COLS_COLS)
    for s in range(N_DEV):
        send_ref[s, 0:QROWS, :] = embed
        send_ref[s, QROWS : QROWS + META, :] = jnp.broadcast_to(meta[s : s + 1], (META, DIM)).astype(BF)
    wait_copies(outs)


def token_copies(hidden_hbm, hidden_ref, sems):
    copies = []
    for i in range(PARTS):
        rows = pl.ds(i * PART, PART)
        copies.append(pltpu.make_async_copy(hidden_hbm.at[rows], hidden_ref.at[rows], sems.at[i]))
    return copies


def encode_kernel(hidden_hbm, weight_hbm, proj_hbm, embed_ref, hidden_ref, weight_ref, proj_ref, sems, out_sems):
    weight_copy = pltpu.make_async_copy(weight_hbm, weight_ref, sems.at[PARTS])
    weight_copy.start()
    copies = token_copies(hidden_hbm, hidden_ref, sems)
    for copy in copies[:AHEAD]:
        copy.start()
    weight_copy.wait()
    outs = []
    for i, copy in enumerate(copies):
        rows = pl.ds(i * PART, PART)
        copy.wait()
        if i + AHEAD < PARTS:
            copies[i + AHEAD].start()
        proj = dot(hidden_ref[rows, :], weight_ref[...])
        proj_ref[rows, :] = proj
        outs.append(pltpu.make_async_copy(proj_ref.at[rows], proj_hbm.at[rows], out_sems.at[i]))
        outs[-1].start()
        inverse = lax.rsqrt(jnp.sum(proj * proj, axis=-1, keepdims=True) + EPS)
        embed_ref[rows, :] = (proj * inverse).astype(BF)
    for out in outs:
        out.wait()


def stored_rows(embed_ref, place_ref, s):
    parts = []
    for k in range(CAP):
        start = pl.multiple_of(place_ref[s, k], 16)
        parts.append(embed_ref[pl.ds(start, PLEN), :])
    return jnp.concatenate(parts, axis=0)


def score_kernel(recv_ref, embed_ref, expo_hbm, recip_hbm, sums_ref, table_hbm, second_hbm, place_hbm,
                 recip_ref, table_ref, second_ref, place_ref, meta_ref, limit_ref, expo_ref, round_ref,
                 smem_ref, sem, expo_sems, out_sems):
    for s in range(N_DEV):
        rows = recv_ref[s, QROWS : QROWS + META, :].astype(F32)
        meta_ref[s : s + 1, :] = rows[0:1, :]
    meta = meta_ref[...]
    place_ref[...] = meta.astype(jnp.int32) * PLEN
    copy = pltpu.make_async_copy(place_ref, smem_ref, sem)
    copy.start()
    outs = start_copies(((place_ref, place_hbm),), out_sems)
    meta_bf = meta.astype(BF)
    spread = expander(1)
    second_ref[...] = dot(pltpu.roll(meta, DIM - SLOTS, 1).astype(BF), spread.astype(BF))
    length = dot(pltpu.roll(meta, DIM - 2 * SLOTS, 1).astype(BF), spread.astype(BF))
    lane = iota((1, WIDE), 1)
    token = lane
    for k in range(1, CAP):
        token = token - jnp.where(lane >= k * PLEN, PLEN, 0)
    limit_ref[...] = jnp.where(token.astype(F32) < length, 1.0, 0.0)
    outs += start_copies(((second_ref, second_hbm),), out_sems.at[pl.ds(1, 1)])
    copy.wait()

    def expo_copy(i):
        rows = pl.ds(i * (CHUNK * QLEN), CHUNK * QLEN)
        return pltpu.make_async_copy(expo_ref.at[rows], expo_hbm.at[rows], expo_sems.at[i])

    def chunk(i, carry):
        for u in range(CHUNK):
            s = i * CHUNK + u
            queries = recv_ref[s, 0:QROWS, :]
            sims = dot(queries, stored_rows(embed_ref, smem_ref, s), COLS_COLS)
            second = second_ref[pl.ds(s, 1), :]
            valid = limit_ref[pl.ds(s, 1), :]
            mine = jnp.where(second > 0.5, sims[QLEN:QROWS], sims[0:QLEN])
            expo = jnp.where(valid > 0.5, jnp.exp(mine * (1.0 / TAU)), 0.0)
            rows = pl.ds(pl.multiple_of(s * QLEN, QLEN), QLEN)
            expo_ref[rows, :] = expo
            round_ref[rows, :] = expo.astype(BF)
        expo_copy(i).start()
        return carry

    lax.fori_loop(0, N_DEV // CHUNK, chunk, 0)
    total = dot(round_ref[...], spread.astype(BF), COLS_COLS)
    total = jnp.where(total > 0.0, total, 1.0)
    recip_ref[...] = 1.0 / total
    outs += start_copies(((recip_ref, recip_hbm),), out_sems.at[pl.ds(2, 1)])
    scores = TAU * jnp.sum(jnp.log(total).reshape(N_DEV, QLEN, DIM), axis=1)
    lane = iota((N_DEV, DIM), 1)
    present = (pltpu.roll(meta, DIM - 6 * SLOTS, 1) > 0.5) & (lane < SLOTS)
    teach = (
        pltpu.roll(meta, DIM - 3 * SLOTS, 1)
        + pltpu.roll(meta, DIM - 4 * SLOTS, 1)
        + pltpu.roll(meta, DIM - 5 * SLOTS, 1)
    )
    teach = jnp.where(present, teach, 0.0)
    student = jnp.where(present, jnp.exp(scores), 0.0)
    which = pltpu.roll(meta, DIM - SLOTS, 1) > 0.5
    table_ref[0] = student
    table_ref[1] = teach
    table_ref[2] = jnp.where(which, 1.0, 0.0)
    outs += start_copies(((table_ref, table_hbm),), out_sems.at[pl.ds(3, 1)])
    gain = teach * scores
    columns = []
    for value in (student, gain):
        columns.append(jnp.sum(jnp.where(which, 0.0, value), axis=-1, keepdims=True))
        columns.append(jnp.sum(jnp.where(which, value, 0.0), axis=-1, keepdims=True))
    mixed = jnp.zeros((N_DEV, DIM), F32)
    for j, column in enumerate(columns):
        mixed = jnp.where(lane == j, column, mixed)
    mixed = jnp.concatenate([mixed, jnp.zeros((DIM - N_DEV, DIM), F32)], axis=0)
    part = jnp.transpose(mixed)[0:8, :]
    for s in range(N_DEV):
        sums_ref[s] = part
    wait_copies(outs)
    wait_copies([expo_copy(i) for i in range(N_DEV // CHUNK)])


def halves(one, second):
    return jnp.concatenate(
        [jnp.where(second, 0.0, one).astype(BF), jnp.where(second, one, 0.0).astype(BF)], axis=0
    )


def ahead_kernel(recv_ref, second_hbm, expo_hbm, recip_hbm, weights_ref, turned_hbm,
                 second_ref, recip_ref, expo_ref, turned_ref, small_sems, sems, out_sems):
    small = start_copies(((recip_hbm, recip_ref), (second_hbm, second_ref)), small_sems)
    steps = N_DEV // CHUNK
    span = CHUNK * QLEN
    fetch = []
    for i in range(steps):
        rows = pl.ds(i * span, span)
        fetch.append(pltpu.make_async_copy(expo_hbm.at[rows], expo_ref.at[rows], sems.at[i]))
        fetch[-1].start()
    spread = expander(2).astype(BF)
    lane = iota((span, DIM), 1)
    outs = []
    wait_copies(small)
    for i in range(steps):
        rows = pl.ds(i * span, span)
        recip = recip_ref[rows, :]
        hi = recip.astype(BF).astype(F32)
        lo = recip - hi
        factor = jnp.where(lane < SLOTS, hi, jnp.where(lane < 2 * SLOTS, pltpu.roll(lo, SLOTS, 1), 0.0))
        wide = dot(factor.astype(BF), spread)
        fetch[i].wait()
        weights = expo_ref[rows, :] * wide
        weights_ref[rows, :] = weights.astype(BF)
        for u in range(CHUNK):
            s = i * CHUNK + u
            second = second_ref[s : s + 1, :] > 0.5
            both = halves(weights[u * QLEN : (u + 1) * QLEN], second)
            turned_ref[s] = dot(both, recv_ref[s, 0:QROWS, :], ROWS_ROWS).astype(BF)
        part = pl.ds(i * CHUNK, CHUNK)
        outs.append(pltpu.make_async_copy(turned_ref.at[part], turned_hbm.at[part], out_sems.at[i]))
        outs[-1].start()
    for out in outs:
        out.wait()


def query_kernel(sums_ref, const_hbm, me_ref, table_hbm, second_hbm, weights_ref, embed_ref, place_hbm,
                 send_ref, pull_hbm, loss_hbm,
                 const_ref, table_ref, second_ref, pull_ref, loss_ref, wide_ref, smem_ref, sems, out_sems):
    small = start_copies(
        ((table_hbm, table_ref), (place_hbm, smem_ref), (const_hbm, const_ref), (second_hbm, second_ref)), sems
    )
    sums = jnp.sum(sums_ref[...], axis=0)
    log_sum = jnp.log(jnp.where(sums > 0.0, sums, 1.0))
    turned = jnp.transpose(jnp.concatenate([sums, jnp.zeros((DIM - 8, DIM), F32)], axis=0))[0:N_DEV, :]
    wait_copies(small)
    loss = const_ref[0:2, :] + log_sum[0:2, :] - sums[2:4, :]
    picked = jnp.where(iota((2, DIM), 1) == me_ref[0], loss, 0.0)
    loss_ref[...] = jnp.broadcast_to(jnp.sum(picked, axis=-1, keepdims=True), (2, DIM))
    normal = jnp.where(table_ref[2] > 0.5, turned[:, 1:2], turned[:, 0:1])
    pull = LOSS_SCALE * (table_ref[0] / normal - table_ref[1])
    pull_ref[...] = pull
    outs = start_copies(((pull_ref, pull_hbm), (loss_ref, loss_hbm)), out_sems)
    hi = pull.astype(BF).astype(F32)
    lo = pull - hi
    lane = iota((N_DEV, DIM), 1)
    factor = jnp.where(lane < SLOTS, hi, jnp.where(lane < 2 * SLOTS, pltpu.roll(lo, SLOTS, 1), 0.0))
    wide_ref[...] = dot(factor.astype(BF), expander(2).astype(BF))

    def chunk(i, carry):
        for u in range(CHUNK):
            s = i * CHUNK + u
            rows = pl.ds(pl.multiple_of(s * QLEN, QLEN), QLEN)
            mixed = weights_ref[rows, :].astype(F32) * wide_ref[pl.ds(s, 1), :]
            both = halves(mixed, second_ref[pl.ds(s, 1), :] > 0.5)
            send_ref[s] = dot(both, stored_rows(embed_ref, smem_ref, s)).astype(BF)
        return carry

    lax.fori_loop(0, N_DEV // CHUNK, chunk, 0)
    wait_copies(outs)


def stored_kernel(place_hbm, pull_hbm, hidden_hbm, proj_hbm, turned_hbm, preact_ref, head_ref,
                  hidden_ref, proj_ref, turned_ref, delta_ref, place_smem, pull_smem, smem_sems,
                  sems, turned_sems, proj_sem):
    steps = N_DEV // CHUNK
    scalars = start_copies(((place_hbm, place_smem), (pull_hbm, pull_smem)), smem_sems)
    fetch = []
    for i in range(steps):
        part = pl.ds(i * CHUNK, CHUNK)
        fetch.append(pltpu.make_async_copy(turned_hbm.at[part], turned_ref.at[part], turned_sems.at[i]))
        fetch[-1].start()
    proj_copy = pltpu.make_async_copy(proj_hbm, proj_ref, proj_sem)
    proj_copy.start()
    copies = token_copies(hidden_hbm, hidden_ref, sems)
    for copy in copies:
        copy.start()
    delta_ref[...] = jnp.zeros_like(delta_ref)
    wait_copies(scalars)

    def add(s, carry):
        for k in range(CAP):
            at = pl.ds(pl.multiple_of(place_smem[s, k], 16), PLEN)
            part = turned_ref[s, k * PLEN : (k + 1) * PLEN, :].astype(F32)
            delta_ref[k % LANES, at, :] += part * pull_smem[s, k]
        return carry

    for i in range(steps):
        fetch[i].wait()
        lax.fori_loop(i * CHUNK, (i + 1) * CHUNK, add, 0)
    proj_copy.wait()
    total = jnp.zeros((DIM, D), F32)
    for i in range(STEPS):
        rows = pl.ds(i * BLOCK, BLOCK)
        proj = proj_ref[rows, :]
        delta = jnp.sum(delta_ref[:, rows, :], axis=0)
        inverse = lax.rsqrt(jnp.sum(proj * proj, axis=-1, keepdims=True) + EPS)
        unit = proj * inverse
        radial = jnp.sum(unit * delta, axis=-1, keepdims=True)
        preact = ((delta - unit * radial) * inverse).astype(BF)
        preact_ref[rows, :] = preact
        for j in range(i * BLOCK // PART, (i + 1) * BLOCK // PART):
            copies[j].wait()
        total = total + dot(preact, hidden_ref[rows, :], ROWS_ROWS)
    head_ref[...] = jnp.transpose(total)


def back_kernel(preact_ref, weight_ref, grad_ref):
    grad_ref[...] = dot(preact_ref[...], weight_ref[...], COLS_COLS).astype(BF)


def finish_kernel(recv_ref, hidden_hbm, weight_hbm, proj_hbm, head_ref, grad_ref, send_ref,
                  hidden_ref, weight_ref, proj_ref, sems):
    copies = start_copies(((proj_hbm, proj_ref), (hidden_hbm, hidden_ref), (weight_hbm, weight_ref)), sems)
    delta = jnp.sum(recv_ref[...].astype(F32), axis=0)
    copies[0].wait()
    proj = proj_ref[...]
    inverse = lax.rsqrt(jnp.sum(proj * proj, axis=-1, keepdims=True) + EPS)
    unit = proj * inverse
    radial = jnp.sum(unit * delta, axis=-1, keepdims=True)
    preact = ((delta - unit * radial) * inverse).astype(BF)
    wait_copies(copies[1:])
    grad_ref[...] = dot(preact, weight_ref[...], COLS_COLS).astype(BF)
    head = head_ref[...] + dot(hidden_ref[...], preact, ROWS_ROWS)
    send_ref[0:HEAD_TILES] = head.reshape(HEAD_TILES, 8, DIM).astype(BF)
    send_ref[HEAD_TILES:N_ALL] = jnp.zeros((N_ALL - HEAD_TILES, 8, DIM), BF)


def reduce_kernel(recv_ref, send_ref):
    total = jnp.sum(recv_ref[...].astype(F32), axis=0).astype(BF)
    send_ref[...] = jnp.broadcast_to(total[None], (N_ALL, 8, DIM))


def shape(dims, kind):
    return jax.ShapeDtypeStruct(dims, kind)


def in_hbm(x):
    return pltpu.with_memory_space_constraint(x, pltpu.HBM)


def in_vmem(x):
    return pltpu.with_memory_space_constraint(x, pltpu.VMEM)


def exchange(x, axes):
    return lax.all_to_all(x, axes, split_axis=0, concat_axis=0, tiled=True)


def estimate(flops, size):
    return pl.CostEstimate(flops=flops, bytes_accessed=size, transcendentals=0)


def on_device(query_hidden, passage_hidden, head_weight, teacher, candidates, storage, lengths):
    query_flat = in_hbm(query_hidden.reshape(QROWS, D))
    flat_hidden = in_hbm(passage_hidden.reshape(TOKENS, D))
    head_weight = in_hbm(head_weight)
    send, query_proj, const = pl.pallas_call(
        request_kernel,
        out_shape=(
            shape((N_DEV, QROWS + META, DIM), BF),
            pltpu.HBM((QROWS, DIM), F32),
            pltpu.HBM((8, DIM), F32),
        ),
        in_specs=[HBM] * 6,
        out_specs=(VMEM, HBM, HBM),
        scratch_shapes=[
            pltpu.VMEM((QROWS, D), BF),
            pltpu.VMEM((D, DIM), BF),
            pltpu.VMEM((2, PER_QUERY), F32),
            pltpu.VMEM((2, PER_QUERY), jnp.int32),
            pltpu.VMEM((1, N_DEV * STORED), jnp.int32),
            pltpu.VMEM((1, N_DEV * STORED), jnp.int32),
            pltpu.VMEM((N_DEV, DIM), jnp.int32),
            pltpu.VMEM((N_DEV, DIM), jnp.int32),
            pltpu.VMEM((QROWS, DIM), F32),
            pltpu.VMEM((8, DIM), F32),
            pltpu.SemaphoreType.DMA((6,)),
            pltpu.SemaphoreType.DMA((2,)),
        ],
        compiler_params=params(4),
        name="request",
    )(query_flat, head_weight, in_hbm(teacher), in_hbm(candidates), in_hbm(storage), in_hbm(lengths))
    recv = exchange(send, "dev")

    proj, embed = pl.pallas_call(
        encode_kernel,
        out_shape=(pltpu.HBM((TOKENS, DIM), F32), pltpu.VMEM((TOKENS, DIM), BF)),
        in_specs=[HBM, HBM],
        out_specs=(HBM, VMEM),
        scratch_shapes=[
            pltpu.VMEM((TOKENS, D), BF),
            pltpu.VMEM((D, DIM), BF),
            pltpu.VMEM((TOKENS, DIM), F32),
            pltpu.SemaphoreType.DMA((PARTS + 1,)),
            pltpu.SemaphoreType.DMA((PARTS,)),
        ],
        cost_estimate=estimate(2 * TOKENS * D * DIM, 15_000_000),
        compiler_params=params(20),
        name="encode",
    )(flat_hidden, head_weight)

    expo, recip, sums, table, second, place = pl.pallas_call(
        score_kernel,
        out_shape=(
            pltpu.HBM((N_DEV * QLEN, WIDE), F32),
            pltpu.HBM((N_DEV * QLEN, DIM), F32),
            shape((N_DEV, 8, DIM), F32),
            pltpu.HBM((3, N_DEV, DIM), F32),
            pltpu.HBM((N_DEV, WIDE), F32),
            pltpu.HBM((N_DEV, DIM), jnp.int32),
        ),
        in_specs=[VMEM] * 2,
        out_specs=(HBM, HBM, VMEM, HBM, HBM, HBM),
        scratch_shapes=[
            pltpu.VMEM((N_DEV * QLEN, DIM), F32),
            pltpu.VMEM((3, N_DEV, DIM), F32),
            pltpu.VMEM((N_DEV, WIDE), F32),
            pltpu.VMEM((N_DEV, DIM), jnp.int32),
            pltpu.VMEM((N_DEV, DIM), F32),
            pltpu.VMEM((N_DEV, WIDE), F32),
            pltpu.VMEM((N_DEV * QLEN, WIDE), F32),
            pltpu.VMEM((N_DEV * QLEN, WIDE), BF),
            pltpu.SMEM((N_DEV, DIM), jnp.int32),
            pltpu.SemaphoreType.DMA,
            pltpu.SemaphoreType.DMA((N_DEV // CHUNK,)),
            pltpu.SemaphoreType.DMA((4,)),
        ],
        compiler_params=params(14),
        name="score",
    )(recv, in_vmem(embed))
    all_sums = exchange(sums, "dev")

    weights, turned = pl.pallas_call(
        ahead_kernel,
        out_shape=(pltpu.VMEM((N_DEV * QLEN, WIDE), BF), pltpu.HBM((N_DEV, WIDE, DIM), BF)),
        in_specs=[VMEM, HBM, HBM, HBM],
        out_specs=(VMEM, HBM),
        scratch_shapes=[
            pltpu.VMEM((N_DEV, WIDE), F32),
            pltpu.VMEM((N_DEV * QLEN, DIM), F32),
            pltpu.VMEM((N_DEV * QLEN, WIDE), F32),
            pltpu.VMEM((N_DEV, WIDE, DIM), BF),
            pltpu.SemaphoreType.DMA((2,)),
            pltpu.SemaphoreType.DMA((N_DEV // CHUNK,)),
            pltpu.SemaphoreType.DMA((N_DEV // CHUNK,)),
        ],
        cost_estimate=estimate(2 * TOKENS * D * DIM, 15_000_000),
        compiler_params=params(22),
        name="ahead",
    )(recv, in_hbm(second), in_hbm(expo), in_hbm(recip))

    me = lax.axis_index("dev").astype(jnp.int32).reshape(1)
    send_delta, pull, loss = pl.pallas_call(
        query_kernel,
        out_shape=(
            shape((N_DEV, QROWS, DIM), BF),
            pltpu.HBM((N_DEV, DIM), F32),
            pltpu.HBM((2, DIM), F32),
        ),
        in_specs=[VMEM, HBM, SMEM, HBM, HBM, VMEM, VMEM, HBM],
        out_specs=(VMEM, HBM, HBM),
        scratch_shapes=[
            pltpu.VMEM((8, DIM), F32),
            pltpu.VMEM((3, N_DEV, DIM), F32),
            pltpu.VMEM((N_DEV, WIDE), F32),
            pltpu.VMEM((N_DEV, DIM), F32),
            pltpu.VMEM((2, DIM), F32),
            pltpu.VMEM((N_DEV, WIDE), F32),
            pltpu.SMEM((N_DEV, DIM), jnp.int32),
            pltpu.SemaphoreType.DMA((4,)),
            pltpu.SemaphoreType.DMA((2,)),
        ],
        compiler_params=params(12),
        name="query",
    )(all_sums, in_hbm(const), me, in_hbm(table), in_hbm(second), in_vmem(weights), in_vmem(embed), in_hbm(place))
    recv_delta = exchange(send_delta, "dev")

    preact, head = pl.pallas_call(
        stored_kernel,
        out_shape=(pltpu.VMEM((TOKENS, DIM), BF), pltpu.VMEM((D, DIM), F32)),
        in_specs=[HBM] * 5,
        out_specs=(VMEM, VMEM),
        scratch_shapes=[
            pltpu.VMEM((TOKENS, D), BF),
            pltpu.VMEM((TOKENS, DIM), F32),
            pltpu.VMEM((N_DEV, WIDE, DIM), BF),
            pltpu.VMEM((LANES, TOKENS, DIM), F32),
            pltpu.SMEM((N_DEV, DIM), jnp.int32),
            pltpu.SMEM((N_DEV, DIM), F32),
            pltpu.SemaphoreType.DMA((2,)),
            pltpu.SemaphoreType.DMA((PARTS,)),
            pltpu.SemaphoreType.DMA((N_DEV // CHUNK,)),
            pltpu.SemaphoreType.DMA,
        ],
        cost_estimate=estimate(4 * TOKENS * D * DIM, 20_000_000),
        compiler_params=params(40),
        name="stored",
    )(in_hbm(place), in_hbm(pull), flat_hidden, in_hbm(proj), in_hbm(turned))

    query_grad, send_head = pl.pallas_call(
        finish_kernel,
        out_shape=(shape((QROWS, D), BF), shape((N_ALL, 8, DIM), BF)),
        in_specs=[VMEM, HBM, HBM, HBM, VMEM],
        out_specs=(VMEM,) * 2,
        scratch_shapes=[
            pltpu.VMEM((QROWS, D), BF),
            pltpu.VMEM((D, DIM), BF),
            pltpu.VMEM((QROWS, DIM), F32),
            pltpu.SemaphoreType.DMA((3,)),
        ],
        compiler_params=params(8),
        name="finish",
    )(recv_delta, query_flat, head_weight, in_hbm(query_proj), in_vmem(head))
    recv_head = exchange(send_head, ("group", "dev"))

    passage_grad = pl.pallas_call(
        back_kernel,
        grid=(STEPS,),
        out_shape=shape((TOKENS, D), BF),
        in_specs=[
            pl.BlockSpec((BLOCK, DIM), lambda i: (i, 0)),
            pl.BlockSpec((D, DIM), lambda i: (0, 0)),
        ],
        out_specs=pl.BlockSpec((BLOCK, D), lambda i: (i, 0)),
        cost_estimate=estimate(2 * TOKENS * D * DIM, 15_000_000),
        compiler_params=params(20),
        name="back",
    )(in_vmem(preact), head_weight)

    send_total = pl.pallas_call(
        reduce_kernel,
        out_shape=shape((N_ALL, 8, DIM), BF),
        in_specs=[VMEM],
        out_specs=VMEM,
        compiler_params=params(4),
        name="reduce",
    )(recv_head)
    head_all = exchange(send_total, ("group", "dev"))
    head_grad = head_all[:HEAD_TILES].reshape(D, DIM).astype(F32)
    return (
        loss[:, 0],
        head_grad,
        query_grad.reshape(2, QLEN, D),
        passage_grad.reshape(STORED, PLEN, D),
    )


def solution(mesh):
    return jax.shard_map(
        on_device,
        mesh=mesh,
        in_specs=(
            P(("group", "dev"), None, None),
            P(("group", "dev"), None, None),
            P(),
            P(("group", "dev"), None),
            P(("group", "dev"), None),
            P("group", None),
            P("group", None),
        ),
        out_specs=(
            P(("group", "dev")),
            P(),
            P(("group", "dev"), None, None),
            P(("group", "dev"), None, None),
        ),
        check_vma=False,
    )
```

```python
import jax
import jax.numpy as jnp
from jax import lax
from jax.experimental import pallas as pl
from jax.experimental.pallas import tpu as pltpu
from jax.sharding import PartitionSpec as P

TAU = 0.0625
LOSS_SCALE = 32768.0
EPS = 1e-06

N_DEV = 32
N_ALL = 128
STORED = 128
PLEN = 48
QLEN = 32
D = 768
DIM = 128
PER_QUERY = 64
CAP = 12
SLOTS = 16
WIDE = CAP * PLEN
QROWS = 2 * QLEN
META = 16
CHUNK = 16
GROUP = 16
TOKENS = STORED * PLEN
BLOCK = 1536
STEPS = TOKENS // BLOCK
LANES = 1
PART = 768
PARTS = TOKENS // PART
AHEAD = 3
HEAD_TILES = D // 8

BF = jnp.bfloat16
F32 = jnp.float32
ROWS_ROWS = (((0,), (0,)), ((), ()))
COLS_COLS = (((1,), (1,)), ((), ()))
VMEM = pl.BlockSpec(memory_space=pltpu.VMEM)
SMEM = pl.BlockSpec(memory_space=pltpu.SMEM)
HBM = pl.BlockSpec(memory_space=pltpu.HBM)


def params(mib):
    return pltpu.CompilerParams(vmem_limit_bytes=mib * 1024 * 1024)


def dot(a, b, dims=(((1,), (0,)), ((), ()))):
    return lax.dot_general(a, b, dims, preferred_element_type=F32)


def iota(shape, axis):
    return lax.broadcasted_iota(jnp.int32, shape, axis)


def start_copies(pairs, sems):
    copies = [pltpu.make_async_copy(a, b, sems.at[i]) for i, (a, b) in enumerate(pairs)]
    for copy in copies:
        copy.start()
    return copies


def wait_copies(copies):
    for copy in copies:
        copy.wait()


def split3(x):
    hi = x.astype(BF).astype(F32)
    mid = (x - hi).astype(BF).astype(F32)
    return hi, mid, (x - hi - mid)


def expander(copies):
    row = iota((DIM, WIDE), 0)
    slot = (row & (SLOTS - 1)) * PLEN
    lane = iota((DIM, WIDE), 1)
    hit = (lane >= slot) & (lane < slot + PLEN) & (row < copies * SLOTS)
    return jnp.where(hit, 1.0, 0.0)


def request_kernel(hidden_hbm, weight_hbm, teacher_hbm, cand_hbm, storage_hbm, lengths_hbm,
                   send_ref, proj_hbm, const_hbm,
                   hidden_ref, weight_ref, teacher_ref, cand_ref, storage_ref, lengths_ref,
                   place_ref, length_ref, proj_ref, const_ref, sems, out_sems):
    small = start_copies(
        (
            (cand_hbm, cand_ref),
            (storage_hbm, storage_ref),
            (lengths_hbm, lengths_ref),
            (teacher_hbm, teacher_ref),
            (weight_hbm, weight_ref),
            (hidden_hbm, hidden_ref),
        ),
        sems,
    )
    wait_copies(small)
    for i in range(N_DEV):
        place_ref[i : i + 1, :] = storage_ref[0:1, i * STORED : (i + 1) * STORED]
        length_ref[i : i + 1, :] = lengths_ref[0:1, i * STORED : (i + 1) * STORED]
    proj = dot(hidden_ref[...], weight_ref[...])
    proj_ref[...] = proj
    inverse = lax.rsqrt(jnp.sum(proj * proj, axis=-1, keepdims=True) + EPS)
    embed = (proj * inverse).astype(BF)

    teacher = teacher_ref[...]
    log_t = teacher - jnp.log(jnp.sum(jnp.exp(teacher), axis=-1, keepdims=True))
    prob = jnp.exp(log_t)
    const = jnp.sum(prob * log_t, axis=-1, keepdims=True)
    const_ref[...] = jnp.concatenate(
        [jnp.broadcast_to(const, (2, DIM)), jnp.zeros((6, DIM), F32)], axis=0
    )
    outs = start_copies(((proj_ref, proj_hbm), (const_ref, const_hbm)), out_sems)
    prob_row = jnp.concatenate([prob[0:1], prob[1:2]], axis=1)
    cand = cand_ref[...]
    cand_row = jnp.concatenate([cand[0:1], cand[1:2]], axis=1)

    place = place_ref[...]
    owner_table = (place >> 7).astype(F32).astype(BF)
    slot_table = (place & (STORED - 1)).astype(F32).astype(BF)
    length_table = length_ref[...].astype(F32).astype(BF)
    sub32 = iota((N_DEV, DIM), 0)
    sub128 = iota((DIM, DIM), 0)
    lane128 = iota((DIM, DIM), 1)
    high = jnp.where(sub32 == (cand_row >> 7), 1.0, 0.0).astype(BF)
    low = sub128 == (cand_row & (STORED - 1))
    owner = jnp.sum(jnp.where(low, dot(owner_table, high, ROWS_ROWS), 0.0), axis=0, keepdims=True)
    slot = jnp.sum(jnp.where(low, dot(slot_table, high, ROWS_ROWS), 0.0), axis=0, keepdims=True)
    match = jnp.where(sub32 == owner.astype(jnp.int32), 1.0, 0.0)
    match_bf = match.astype(BF)
    at_slot = sub128 == slot.astype(jnp.int32)
    length = jnp.sum(
        jnp.where(at_slot, dot(length_table, match_bf, ROWS_ROWS), 0.0), axis=0, keepdims=True
    )
    earlier = jnp.where(sub128 < lane128, 1.0, 0.0).astype(BF)
    rank = jnp.sum(match * dot(match_bf, earlier), axis=0, keepdims=True).astype(jnp.int32)
    t_hi, t_mid, t_lo = split3(prob_row)
    which = jnp.where(iota((1, DIM), 1) >= PER_QUERY, 1.0, 0.0)
    fields = (slot, which, length, t_hi, t_mid, t_lo, jnp.ones((1, DIM), F32))
    field_of = sub128 >> 4
    values = jnp.zeros((DIM, DIM), F32)
    for f, row in enumerate(fields):
        values = jnp.where(field_of == f, row, values)
    values = jnp.where((sub128 & (SLOTS - 1)) == rank, values, 0.0).astype(BF)
    meta = dot(match_bf, values, COLS_COLS)
    for s in range(N_DEV):
        send_ref[s, 0:QROWS, :] = embed
        send_ref[s, QROWS : QROWS + META, :] = jnp.broadcast_to(meta[s : s + 1], (META, DIM)).astype(BF)
    wait_copies(outs)


def token_copies(hidden_hbm, hidden_ref, sems):
    copies = []
    for i in range(PARTS):
        rows = pl.ds(i * PART, PART)
        copies.append(pltpu.make_async_copy(hidden_hbm.at[rows], hidden_ref.at[rows], sems.at[i]))
    return copies


def encode_kernel(hidden_hbm, weight_hbm, embed_ref, inverse_hbm, hidden_ref, weight_ref, inverse_ref, sems, out_sem):
    weight_copy = pltpu.make_async_copy(weight_hbm, weight_ref, sems.at[PARTS])
    weight_copy.start()
    copies = token_copies(hidden_hbm, hidden_ref, sems)
    for copy in copies[:AHEAD]:
        copy.start()
    weight_copy.wait()
    packed = jnp.zeros((DIM, DIM), F32)
    lane = iota((DIM, DIM), 1)
    for i, copy in enumerate(copies):
        rows = pl.ds(i * PART, PART)
        copy.wait()
        if i + AHEAD < PARTS:
            copies[i + AHEAD].start()
        proj = dot(hidden_ref[rows, :], weight_ref[...])
        inverse = lax.rsqrt(jnp.sum(proj * proj, axis=-1, keepdims=True) + EPS)
        embed_ref[rows, :] = (proj * inverse).astype(BF)
        for j in range(PART // DIM):
            packed = jnp.where(lane == i * (PART // DIM) + j, inverse[j * DIM : (j + 1) * DIM], packed)
    inverse_ref[...] = packed
    out = pltpu.make_async_copy(inverse_ref, inverse_hbm, out_sem)
    out.start()
    out.wait()


def stored_rows(embed_ref, place_ref, s):
    parts = []
    for k in range(CAP):
        start = pl.multiple_of(place_ref[s, k], 16)
        parts.append(embed_ref[pl.ds(start, PLEN), :])
    return jnp.concatenate(parts, axis=0)


def score_kernel(recv_ref, embed_ref, expo_hbm, recip_hbm, sums_ref, table_hbm, second_hbm, place_hbm, queries_hbm,
                 recip_ref, table_ref, second_ref, place_ref, meta_ref, limit_ref, expo_ref, round_ref,
                 smem_ref, sem, expo_sems, out_sems):
    outs = start_copies(((recv_ref.at[:, pl.ds(0, QROWS)], queries_hbm),), out_sems.at[pl.ds(4, 1)])
    for s in range(N_DEV):
        rows = recv_ref[s, QROWS : QROWS + META, :].astype(F32)
        meta_ref[s : s + 1, :] = rows[0:1, :]
    meta = meta_ref[...]
    place_ref[...] = meta.astype(jnp.int32) * PLEN
    copy = pltpu.make_async_copy(place_ref, smem_ref, sem)
    copy.start()
    outs += start_copies(((place_ref, place_hbm),), out_sems)
    meta_bf = meta.astype(BF)
    spread = expander(1)
    second_ref[...] = dot(pltpu.roll(meta, DIM - SLOTS, 1).astype(BF), spread.astype(BF))
    length = dot(pltpu.roll(meta, DIM - 2 * SLOTS, 1).astype(BF), spread.astype(BF))
    lane = iota((1, WIDE), 1)
    token = lane
    for k in range(1, CAP):
        token = token - jnp.where(lane >= k * PLEN, PLEN, 0)
    limit_ref[...] = jnp.where(token.astype(F32) < length, 1.0, 0.0)
    outs += start_copies(((second_ref, second_hbm),), out_sems.at[pl.ds(1, 1)])
    copy.wait()

    def expo_copy(i):
        rows = pl.ds(i * (CHUNK * QLEN), CHUNK * QLEN)
        return pltpu.make_async_copy(expo_ref.at[rows], expo_hbm.at[rows], expo_sems.at[i])

    def chunk(i, carry):
        for u in range(CHUNK):
            s = i * CHUNK + u
            queries = recv_ref[s, 0:QROWS, :]
            sims = dot(queries, stored_rows(embed_ref, smem_ref, s), COLS_COLS)
            second = second_ref[pl.ds(s, 1), :]
            valid = limit_ref[pl.ds(s, 1), :]
            mine = jnp.where(second > 0.5, sims[QLEN:QROWS], sims[0:QLEN])
            expo = jnp.where(valid > 0.5, jnp.exp(mine * (1.0 / TAU)), 0.0)
            rows = pl.ds(pl.multiple_of(s * QLEN, QLEN), QLEN)
            expo_ref[rows, :] = expo
            round_ref[rows, :] = expo.astype(BF)
        expo_copy(i).start()
        return carry

    lax.fori_loop(0, N_DEV // CHUNK, chunk, 0)
    total = dot(round_ref[...], spread.astype(BF), COLS_COLS)
    total = jnp.where(total > 0.0, total, 1.0)
    recip_ref[...] = 1.0 / total
    outs += start_copies(((recip_ref, recip_hbm),), out_sems.at[pl.ds(2, 1)])
    scores = TAU * jnp.sum(jnp.log(total).reshape(N_DEV, QLEN, DIM), axis=1)
    lane = iota((N_DEV, DIM), 1)
    present = (pltpu.roll(meta, DIM - 6 * SLOTS, 1) > 0.5) & (lane < SLOTS)
    teach = (
        pltpu.roll(meta, DIM - 3 * SLOTS, 1)
        + pltpu.roll(meta, DIM - 4 * SLOTS, 1)
        + pltpu.roll(meta, DIM - 5 * SLOTS, 1)
    )
    teach = jnp.where(present, teach, 0.0)
    student = jnp.where(present, jnp.exp(scores), 0.0)
    which = pltpu.roll(meta, DIM - SLOTS, 1) > 0.5
    table_ref[0] = student
    table_ref[1] = teach
    table_ref[2] = jnp.where(which, 1.0, 0.0)
    outs += start_copies(((table_ref, table_hbm),), out_sems.at[pl.ds(3, 1)])
    gain = teach * scores
    columns = []
    for value in (student, gain):
        columns.append(jnp.sum(jnp.where(which, 0.0, value), axis=-1, keepdims=True))
        columns.append(jnp.sum(jnp.where(which, value, 0.0), axis=-1, keepdims=True))
    mixed = jnp.zeros((N_DEV, DIM), F32)
    for j, column in enumerate(columns):
        mixed = jnp.where(lane == j, column, mixed)
    mixed = jnp.concatenate([mixed, jnp.zeros((DIM - N_DEV, DIM), F32)], axis=0)
    part = jnp.transpose(mixed)[0:8, :]
    for s in range(N_DEV):
        sums_ref[s] = part
    wait_copies(outs)
    wait_copies([expo_copy(i) for i in range(N_DEV // CHUNK)])


def halves(one, second):
    return jnp.concatenate(
        [jnp.where(second, 0.0, one).astype(BF), jnp.where(second, one, 0.0).astype(BF)], axis=0
    )


def ahead_kernel(expo_hbm, recip_hbm, weights_ref, recip_ref, expo_ref, sems):
    steps = N_DEV // GROUP
    span = GROUP * QLEN
    fetch = []
    for i in range(steps):
        rows = pl.ds(i * span, span)
        fetch.append(
            start_copies(
                ((recip_hbm.at[rows], recip_ref.at[rows]), (expo_hbm.at[rows], expo_ref.at[rows])), sems.at[i]
            )
        )
    spread = expander(2).astype(BF)
    lane = iota((span, DIM), 1)
    for i in range(steps):
        rows = pl.ds(i * span, span)
        wait_copies(fetch[i])
        recip = recip_ref[rows, :]
        hi = recip.astype(BF).astype(F32)
        lo = recip - hi
        factor = jnp.where(lane < SLOTS, hi, jnp.where(lane < 2 * SLOTS, pltpu.roll(lo, SLOTS, 1), 0.0))
        weights_ref[rows, :] = (expo_ref[rows, :] * dot(factor.astype(BF), spread)).astype(BF)


def query_kernel(sums_ref, const_hbm, me_ref, table_hbm, second_hbm, weights_ref, embed_ref, place_hbm,
                 send_hbm, mixed_hbm, loss_hbm,
                 const_ref, table_ref, second_ref, loss_ref, wide_ref, send_ref, mixed_ref, smem_ref,
                 sems, out_sems, part_sems):
    small = start_copies(
        ((table_hbm, table_ref), (place_hbm, smem_ref), (const_hbm, const_ref), (second_hbm, second_ref)), sems
    )
    sums = jnp.sum(sums_ref[...], axis=0)
    log_sum = jnp.log(jnp.where(sums > 0.0, sums, 1.0))
    turned = jnp.transpose(jnp.concatenate([sums, jnp.zeros((DIM - 8, DIM), F32)], axis=0))[0:N_DEV, :]
    wait_copies(small)
    loss = const_ref[0:2, :] + log_sum[0:2, :] - sums[2:4, :]
    picked = jnp.where(iota((2, DIM), 1) == me_ref[0], loss, 0.0)
    loss_ref[...] = jnp.broadcast_to(jnp.sum(picked, axis=-1, keepdims=True), (2, DIM))
    normal = jnp.where(table_ref[2] > 0.5, turned[:, 1:2], turned[:, 0:1])
    pull = LOSS_SCALE * (table_ref[0] / normal - table_ref[1])
    outs = start_copies(((loss_ref, loss_hbm),), out_sems)
    hi = pull.astype(BF).astype(F32)
    lo = pull - hi
    lane = iota((N_DEV, DIM), 1)
    factor = jnp.where(lane < SLOTS, hi, jnp.where(lane < 2 * SLOTS, pltpu.roll(lo, SLOTS, 1), 0.0))
    wide_ref[...] = dot(factor.astype(BF), expander(2).astype(BF))

    def part_copies(i):
        some = pl.ds(i * CHUNK, CHUNK)
        rows = pl.ds(i * (CHUNK * QLEN), CHUNK * QLEN)
        return [
            pltpu.make_async_copy(send_ref.at[some], send_hbm.at[some], part_sems.at[i, 0]),
            pltpu.make_async_copy(mixed_ref.at[rows], mixed_hbm.at[rows], part_sems.at[i, 1]),
        ]

    def chunk(i, carry):
        for u in range(CHUNK):
            s = i * CHUNK + u
            rows = pl.ds(pl.multiple_of(s * QLEN, QLEN), QLEN)
            mixed = weights_ref[rows, :].astype(F32) * wide_ref[pl.ds(s, 1), :]
            mixed_ref[rows, :] = mixed.astype(BF)
            both = halves(mixed, second_ref[pl.ds(s, 1), :] > 0.5)
            send_ref[s] = dot(both, stored_rows(embed_ref, smem_ref, s)).astype(BF)
        for copy in part_copies(i):
            copy.start()
        return carry

    lax.fori_loop(0, N_DEV // CHUNK, chunk, 0)
    wait_copies(outs)
    for i in range(N_DEV // CHUNK):
        wait_copies(part_copies(i))


def stored_kernel(place_hbm, queries_hbm, second_hbm, mixed_hbm, inverse_hbm, hidden_hbm, embed_ref,
                  preact_hbm, head_ref,
                  preact_ref, hidden_ref, queries_ref, second_ref, mixed_ref, inverse_ref, delta_ref, place_smem,
                  sems, small_sems, mixed_sems, out_sems):
    steps = N_DEV // GROUP
    small = start_copies(
        ((place_hbm, place_smem), (second_hbm, second_ref), (queries_hbm, queries_ref), (inverse_hbm, inverse_ref)),
        small_sems,
    )
    fetch = []
    for i in range(steps):
        rows = pl.ds(i * GROUP * QLEN, GROUP * QLEN)
        fetch += start_copies(((mixed_hbm.at[rows], mixed_ref.at[rows]),), mixed_sems.at[pl.ds(i, 1)])
    copies = token_copies(hidden_hbm, hidden_ref, sems)
    delta_ref[...] = jnp.zeros_like(delta_ref)
    wait_copies(small)

    for i in range(steps):
        fetch[i].wait()
        for copy in copies[i * PARTS // steps : (i + 1) * PARTS // steps]:
            copy.start()
        for s in range(i * GROUP, (i + 1) * GROUP):
            both = halves(mixed_ref[s * QLEN : (s + 1) * QLEN, :].astype(F32), second_ref[s : s + 1, :] > 0.5)
            part = dot(both, queries_ref[s], ROWS_ROWS)
            for k in range(CAP):
                at = pl.ds(pl.multiple_of(place_smem[s, k], 16), PLEN)
                delta_ref[k % LANES, at, :] += part[k * PLEN : (k + 1) * PLEN]
    total = jnp.zeros((DIM, D), F32)
    outs = []
    for i in range(STEPS):
        rows = pl.ds(i * BLOCK, BLOCK)
        unit = embed_ref[rows, :].astype(F32)
        delta = jnp.sum(delta_ref[:, rows, :], axis=0)
        radial = jnp.sum(unit * delta, axis=-1, keepdims=True)
        tangent = delta - unit * radial
        scaled = []
        for j in range(BLOCK // DIM):
            b = i * (BLOCK // DIM) + j
            scaled.append(tangent[j * DIM : (j + 1) * DIM] * inverse_ref[:, b : b + 1])
        preact = jnp.concatenate(scaled, axis=0).astype(BF)
        preact_ref[rows, :] = preact
        outs += start_copies(((preact_ref.at[rows], preact_hbm.at[rows]),), out_sems.at[pl.ds(i, 1)])
        for j in range(i * BLOCK // PART, (i + 1) * BLOCK // PART):
            copies[j].wait()
        total = total + dot(preact, hidden_ref[rows, :], ROWS_ROWS)
    head_ref[...] = jnp.transpose(total)
    wait_copies(outs)


def back_kernel(preact_ref, weight_ref, after_ref, grad_ref):
    grad_ref[...] = dot(preact_ref[...], weight_ref[...], COLS_COLS).astype(BF)


def query_back_kernel(preact_ref, weight_hbm, after_ref, grad_ref, weight_ref, sem):
    copy = pltpu.make_async_copy(weight_hbm, weight_ref, sem)
    copy.start()
    copy.wait()
    grad_ref[...] = dot(preact_ref[...], weight_ref[...], COLS_COLS).astype(BF)


def finish_kernel(recv_ref, hidden_hbm, proj_hbm, head_ref, preact_ref, send_ref,
                  hidden_ref, proj_ref, sems):
    copies = start_copies(((proj_hbm, proj_ref), (hidden_hbm, hidden_ref)), sems)
    delta = jnp.sum(recv_ref[...].astype(F32), axis=0)
    copies[0].wait()
    proj = proj_ref[...]
    inverse = lax.rsqrt(jnp.sum(proj * proj, axis=-1, keepdims=True) + EPS)
    unit = proj * inverse
    radial = jnp.sum(unit * delta, axis=-1, keepdims=True)
    preact = ((delta - unit * radial) * inverse).astype(BF)
    preact_ref[...] = preact
    wait_copies(copies[1:])
    head = head_ref[...] + dot(hidden_ref[...], preact, ROWS_ROWS)
    send_ref[0:HEAD_TILES] = head.reshape(HEAD_TILES, 8, DIM).astype(BF)
    send_ref[HEAD_TILES:N_ALL] = jnp.zeros((N_ALL - HEAD_TILES, 8, DIM), BF)


def reduce_kernel(recv_ref, after_ref, send_ref):
    total = jnp.sum(recv_ref[...].astype(F32), axis=0).astype(BF)
    send_ref[...] = jnp.broadcast_to(total[None], (N_ALL, 8, DIM))


def shape(dims, kind):
    return jax.ShapeDtypeStruct(dims, kind)


def in_hbm(x):
    return pltpu.with_memory_space_constraint(x, pltpu.HBM)


def in_vmem(x):
    return pltpu.with_memory_space_constraint(x, pltpu.VMEM)


def exchange(x, axes):
    return lax.all_to_all(x, axes, split_axis=0, concat_axis=0, tiled=True)


def estimate(flops, size):
    return pl.CostEstimate(flops=flops, bytes_accessed=size, transcendentals=0)


def on_device(query_hidden, passage_hidden, head_weight, teacher, candidates, storage, lengths):
    query_flat = in_hbm(query_hidden.reshape(QROWS, D))
    flat_hidden = in_hbm(passage_hidden.reshape(TOKENS, D))
    head_weight = in_hbm(head_weight)
    send, query_proj, const = pl.pallas_call(
        request_kernel,
        out_shape=(
            shape((N_DEV, QROWS + META, DIM), BF),
            pltpu.HBM((QROWS, DIM), F32),
            pltpu.HBM((8, DIM), F32),
        ),
        in_specs=[HBM] * 6,
        out_specs=(VMEM, HBM, HBM),
        scratch_shapes=[
            pltpu.VMEM((QROWS, D), BF),
            pltpu.VMEM((D, DIM), BF),
            pltpu.VMEM((2, PER_QUERY), F32),
            pltpu.VMEM((2, PER_QUERY), jnp.int32),
            pltpu.VMEM((1, N_DEV * STORED), jnp.int32),
            pltpu.VMEM((1, N_DEV * STORED), jnp.int32),
            pltpu.VMEM((N_DEV, DIM), jnp.int32),
            pltpu.VMEM((N_DEV, DIM), jnp.int32),
            pltpu.VMEM((QROWS, DIM), F32),
            pltpu.VMEM((8, DIM), F32),
            pltpu.SemaphoreType.DMA((6,)),
            pltpu.SemaphoreType.DMA((2,)),
        ],
        compiler_params=params(4),
        name="request",
    )(query_flat, head_weight, in_hbm(teacher), in_hbm(candidates), in_hbm(storage), in_hbm(lengths))
    recv = exchange(send, "dev")

    embed, inverse = pl.pallas_call(
        encode_kernel,
        out_shape=(pltpu.VMEM((TOKENS, DIM), BF), pltpu.HBM((DIM, DIM), F32)),
        in_specs=[HBM, HBM],
        out_specs=(VMEM, HBM),
        scratch_shapes=[
            pltpu.VMEM((TOKENS, D), BF),
            pltpu.VMEM((D, DIM), BF),
            pltpu.VMEM((DIM, DIM), F32),
            pltpu.SemaphoreType.DMA((PARTS + 1,)),
            pltpu.SemaphoreType.DMA,
        ],
        cost_estimate=estimate(2 * TOKENS * D * DIM, 15_000_000),
        compiler_params=params(20),
        name="encode",
    )(flat_hidden, head_weight)

    expo, recip, sums, table, second, place, queries = pl.pallas_call(
        score_kernel,
        out_shape=(
            pltpu.HBM((N_DEV * QLEN, WIDE), F32),
            pltpu.HBM((N_DEV * QLEN, DIM), F32),
            shape((N_DEV, 8, DIM), F32),
            pltpu.HBM((3, N_DEV, DIM), F32),
            pltpu.HBM((N_DEV, WIDE), F32),
            pltpu.HBM((N_DEV, DIM), jnp.int32),
            pltpu.HBM((N_DEV, QROWS, DIM), BF),
        ),
        in_specs=[VMEM] * 2,
        out_specs=(HBM, HBM, VMEM, HBM, HBM, HBM, HBM),
        scratch_shapes=[
            pltpu.VMEM((N_DEV * QLEN, DIM), F32),
            pltpu.VMEM((3, N_DEV, DIM), F32),
            pltpu.VMEM((N_DEV, WIDE), F32),
            pltpu.VMEM((N_DEV, DIM), jnp.int32),
            pltpu.VMEM((N_DEV, DIM), F32),
            pltpu.VMEM((N_DEV, WIDE), F32),
            pltpu.VMEM((N_DEV * QLEN, WIDE), F32),
            pltpu.VMEM((N_DEV * QLEN, WIDE), BF),
            pltpu.SMEM((N_DEV, DIM), jnp.int32),
            pltpu.SemaphoreType.DMA,
            pltpu.SemaphoreType.DMA((N_DEV // CHUNK,)),
            pltpu.SemaphoreType.DMA((5,)),
        ],
        compiler_params=params(14),
        name="score",
    )(recv, in_vmem(embed))
    all_sums = exchange(sums, "dev")

    weights = pl.pallas_call(
        ahead_kernel,
        out_shape=pltpu.VMEM((N_DEV * QLEN, WIDE), BF),
        in_specs=[HBM, HBM],
        out_specs=VMEM,
        scratch_shapes=[
            pltpu.VMEM((N_DEV * QLEN, DIM), F32),
            pltpu.VMEM((N_DEV * QLEN, WIDE), F32),
            pltpu.SemaphoreType.DMA((N_DEV // GROUP, 2)),
        ],
        cost_estimate=estimate(2 * TOKENS * D * DIM, 15_000_000),
        compiler_params=params(12),
        name="ahead",
    )(in_hbm(expo), in_hbm(recip))

    me = lax.axis_index("dev").astype(jnp.int32).reshape(1)
    send_delta, mixed, loss = pl.pallas_call(
        query_kernel,
        out_shape=(
            pltpu.HBM((N_DEV, QROWS, DIM), BF),
            pltpu.HBM((N_DEV * QLEN, WIDE), BF),
            pltpu.HBM((2, DIM), F32),
        ),
        in_specs=[VMEM, HBM, SMEM, HBM, HBM, VMEM, VMEM, HBM],
        out_specs=(HBM, HBM, HBM),
        scratch_shapes=[
            pltpu.VMEM((8, DIM), F32),
            pltpu.VMEM((3, N_DEV, DIM), F32),
            pltpu.VMEM((N_DEV, WIDE), F32),
            pltpu.VMEM((2, DIM), F32),
            pltpu.VMEM((N_DEV, WIDE), F32),
            pltpu.VMEM((N_DEV, QROWS, DIM), BF),
            pltpu.VMEM((N_DEV * QLEN, WIDE), BF),
            pltpu.SMEM((N_DEV, DIM), jnp.int32),
            pltpu.SemaphoreType.DMA((4,)),
            pltpu.SemaphoreType.DMA((1,)),
            pltpu.SemaphoreType.DMA((N_DEV // CHUNK, 2)),
        ],
        compiler_params=params(12),
        name="query",
    )(all_sums, in_hbm(const), me, in_hbm(table), in_hbm(second), in_vmem(weights), in_vmem(embed), in_hbm(place))
    recv_delta = exchange(send_delta, "dev")

    preact, head = pl.pallas_call(
        stored_kernel,
        out_shape=(pltpu.HBM((TOKENS, DIM), BF), pltpu.VMEM((D, DIM), F32)),
        in_specs=[HBM] * 6 + [VMEM],
        out_specs=(HBM, VMEM),
        scratch_shapes=[
            pltpu.VMEM((TOKENS, DIM), BF),
            pltpu.VMEM((TOKENS, D), BF),
            pltpu.VMEM((N_DEV, QROWS, DIM), BF),
            pltpu.VMEM((N_DEV, WIDE), F32),
            pltpu.VMEM((N_DEV * QLEN, WIDE), BF),
            pltpu.VMEM((DIM, DIM), F32),
            pltpu.VMEM((LANES, TOKENS, DIM), F32),
            pltpu.SMEM((N_DEV, DIM), jnp.int32),
            pltpu.SemaphoreType.DMA((PARTS,)),
            pltpu.SemaphoreType.DMA((4,)),
            pltpu.SemaphoreType.DMA((N_DEV // GROUP,)),
            pltpu.SemaphoreType.DMA((STEPS,)),
        ],
        cost_estimate=estimate(4 * TOKENS * D * DIM, 20_000_000),
        compiler_params=params(40),
        name="stored",
    )(
        in_hbm(place), in_hbm(queries), in_hbm(second), in_hbm(mixed), in_hbm(inverse), flat_hidden, in_vmem(embed)
    )

    query_preact, send_head = pl.pallas_call(
        finish_kernel,
        out_shape=(pltpu.VMEM((QROWS, DIM), BF), shape((N_ALL, 8, DIM), BF)),
        in_specs=[VMEM, HBM, HBM, VMEM],
        out_specs=(VMEM,) * 2,
        scratch_shapes=[
            pltpu.VMEM((QROWS, D), BF),
            pltpu.VMEM((QROWS, DIM), F32),
            pltpu.SemaphoreType.DMA((2,)),
        ],
        compiler_params=params(8),
        name="finish",
    )(recv_delta, query_flat, in_hbm(query_proj), in_vmem(head))
    recv_head = exchange(send_head, ("group", "dev"))

    passage_grad = pl.pallas_call(
        back_kernel,
        grid=(STEPS,),
        out_shape=pltpu.HBM((TOKENS, D), BF),
        in_specs=[
            pl.BlockSpec((BLOCK, DIM), lambda i: (i, 0)),
            pl.BlockSpec((D, DIM), lambda i: (0, 0)),
            pl.BlockSpec(memory_space=pl.ANY),
        ],
        out_specs=pl.BlockSpec((BLOCK, D), lambda i: (i, 0)),
        cost_estimate=estimate(2 * TOKENS * D * DIM, 15_000_000),
        compiler_params=params(20),
        name="back",
    )(in_hbm(preact), head_weight, query_preact)

    send_total = pl.pallas_call(
        reduce_kernel,
        out_shape=shape((N_ALL, 8, DIM), BF),
        in_specs=[VMEM, pl.BlockSpec(memory_space=pl.ANY)],
        out_specs=VMEM,
        compiler_params=params(4),
        name="reduce",
    )(recv_head, in_hbm(passage_grad))
    query_grad = pl.pallas_call(
        query_back_kernel,
        out_shape=shape((QROWS, D), BF),
        in_specs=[VMEM, HBM, pl.BlockSpec(memory_space=pl.ANY)],
        out_specs=VMEM,
        scratch_shapes=[pltpu.VMEM((D, DIM), BF), pltpu.SemaphoreType.DMA],
        cost_estimate=estimate(2 * QROWS * D * DIM, 400_000),
        compiler_params=params(4),
        name="query_back",
    )(query_preact, head_weight, send_total)
    head_all = exchange(send_total, ("group", "dev"))
    head_grad = head_all[:HEAD_TILES].reshape(D, DIM).astype(F32)
    return (
        loss[:, 0],
        head_grad,
        query_grad.reshape(2, QLEN, D),
        passage_grad.reshape(STORED, PLEN, D),
    )


def solution(mesh):
    return jax.shard_map(
        on_device,
        mesh=mesh,
        in_specs=(
            P(("group", "dev"), None, None),
            P(("group", "dev"), None, None),
            P(),
            P(("group", "dev"), None),
            P(("group", "dev"), None),
            P("group", None),
            P("group", None),
        ),
        out_specs=(
            P(("group", "dev")),
            P(),
            P(("group", "dev"), None, None),
            P(("group", "dev"), None, None),
        ),
        check_vma=False,
    )
```

```python
import jax
import jax.numpy as jnp
from jax import lax
from jax.experimental import pallas as pl
from jax.experimental.pallas import tpu as pltpu
from jax.sharding import PartitionSpec as P

TAU = 0.0625
LOSS_SCALE = 32768.0
EPS = 1e-06

N_DEV = 32
N_ALL = 128
STORED = 128
PLEN = 48
QLEN = 32
D = 768
DIM = 128
PER_QUERY = 64
CAP = 12
SLOTS = 16
WIDE = CAP * PLEN
QROWS = 2 * QLEN
META = 16
CHUNK = 16
GROUP = 16
TOKENS = STORED * PLEN
BLOCK = 1536
STEPS = TOKENS // BLOCK
LANES = 1
PART = 768
PARTS = TOKENS // PART
AHEAD = 4
TILE = 256
HEAD_TILES = D // 8

BF = jnp.bfloat16
F32 = jnp.float32
ROWS_ROWS = (((0,), (0,)), ((), ()))
COLS_COLS = (((1,), (1,)), ((), ()))
VMEM = pl.BlockSpec(memory_space=pltpu.VMEM)
SMEM = pl.BlockSpec(memory_space=pltpu.SMEM)
HBM = pl.BlockSpec(memory_space=pltpu.HBM)


def params(mib):
    return pltpu.CompilerParams(vmem_limit_bytes=mib * 1024 * 1024)


def dot(a, b, dims=(((1,), (0,)), ((), ()))):
    return lax.dot_general(a, b, dims, preferred_element_type=F32)


def iota(shape, axis):
    return lax.broadcasted_iota(jnp.int32, shape, axis)


def start_copies(pairs, sems):
    copies = [pltpu.make_async_copy(a, b, sems.at[i]) for i, (a, b) in enumerate(pairs)]
    for copy in copies:
        copy.start()
    return copies


def wait_copies(copies):
    for copy in copies:
        copy.wait()


def split3(x):
    hi = x.astype(BF).astype(F32)
    mid = (x - hi).astype(BF).astype(F32)
    return hi, mid, (x - hi - mid)


def expander(copies):
    row = iota((DIM, WIDE), 0)
    slot = (row & (SLOTS - 1)) * PLEN
    lane = iota((DIM, WIDE), 1)
    hit = (lane >= slot) & (lane < slot + PLEN) & (row < copies * SLOTS)
    return jnp.where(hit, 1.0, 0.0)


def request_kernel(hidden_hbm, weight_hbm, teacher_hbm, cand_hbm, storage_hbm, lengths_hbm,
                   send_hbm, proj_hbm, const_hbm,
                   hidden_ref, weight_ref, teacher_ref, cand_ref, storage_ref, lengths_ref,
                   place_ref, length_ref, proj_ref, const_ref, embed_ref, meta_ref, sems, out_sems, send_sems):
    small = start_copies(
        (
            (cand_hbm, cand_ref),
            (storage_hbm, storage_ref),
            (lengths_hbm, lengths_ref),
            (teacher_hbm, teacher_ref),
            (weight_hbm, weight_ref),
            (hidden_hbm, hidden_ref),
        ),
        sems,
    )
    wait_copies(small[4:])
    proj = dot(hidden_ref[...], weight_ref[...])
    proj_ref[...] = proj
    inverse = lax.rsqrt(jnp.sum(proj * proj, axis=-1, keepdims=True) + EPS)
    embed_ref[...] = (proj * inverse).astype(BF)
    sends = start_copies(
        [(embed_ref, send_hbm.at[s, pl.ds(0, QROWS)]) for s in range(N_DEV)], send_sems
    )
    wait_copies(small[:4])
    for i in range(N_DEV):
        place_ref[i : i + 1, :] = storage_ref[0:1, i * STORED : (i + 1) * STORED]
        length_ref[i : i + 1, :] = lengths_ref[0:1, i * STORED : (i + 1) * STORED]
    teacher = teacher_ref[...]
    log_t = teacher - jnp.log(jnp.sum(jnp.exp(teacher), axis=-1, keepdims=True))
    prob = jnp.exp(log_t)
    const = jnp.sum(prob * log_t, axis=-1, keepdims=True)
    const_ref[...] = jnp.concatenate(
        [jnp.broadcast_to(const, (2, DIM)), jnp.zeros((6, DIM), F32)], axis=0
    )
    outs = start_copies(((proj_ref, proj_hbm), (const_ref, const_hbm)), out_sems)
    prob_row = jnp.concatenate([prob[0:1], prob[1:2]], axis=1)
    cand = cand_ref[...]
    cand_row = jnp.concatenate([cand[0:1], cand[1:2]], axis=1)

    place = place_ref[...]
    owner_table = (place >> 7).astype(F32).astype(BF)
    slot_table = (place & (STORED - 1)).astype(F32).astype(BF)
    length_table = length_ref[...].astype(F32).astype(BF)
    sub32 = iota((N_DEV, DIM), 0)
    sub128 = iota((DIM, DIM), 0)
    lane128 = iota((DIM, DIM), 1)
    high = jnp.where(sub32 == (cand_row >> 7), 1.0, 0.0).astype(BF)
    low = sub128 == (cand_row & (STORED - 1))
    owner = jnp.sum(jnp.where(low, dot(owner_table, high, ROWS_ROWS), 0.0), axis=0, keepdims=True)
    slot = jnp.sum(jnp.where(low, dot(slot_table, high, ROWS_ROWS), 0.0), axis=0, keepdims=True)
    match = jnp.where(sub32 == owner.astype(jnp.int32), 1.0, 0.0)
    match_bf = match.astype(BF)
    at_slot = sub128 == slot.astype(jnp.int32)
    length = jnp.sum(
        jnp.where(at_slot, dot(length_table, match_bf, ROWS_ROWS), 0.0), axis=0, keepdims=True
    )
    earlier = jnp.where(sub128 < lane128, 1.0, 0.0).astype(BF)
    rank = jnp.sum(match * dot(match_bf, earlier), axis=0, keepdims=True).astype(jnp.int32)
    t_hi, t_mid, t_lo = split3(prob_row)
    which = jnp.where(iota((1, DIM), 1) >= PER_QUERY, 1.0, 0.0)
    fields = (slot, which, length, t_hi, t_mid, t_lo, jnp.ones((1, DIM), F32))
    field_of = sub128 >> 4
    values = jnp.zeros((DIM, DIM), F32)
    for f, row in enumerate(fields):
        values = jnp.where(field_of == f, row, values)
    values = jnp.where((sub128 & (SLOTS - 1)) == rank, values, 0.0).astype(BF)
    meta = dot(match_bf, values, COLS_COLS)
    for s in range(N_DEV):
        meta_ref[s] = jnp.broadcast_to(meta[s : s + 1], (META, DIM)).astype(BF)
    outs += start_copies(((meta_ref, send_hbm.at[:, pl.ds(QROWS, META)]),), out_sems.at[pl.ds(2, 1)])
    wait_copies(sends)
    wait_copies(outs)


def token_copies(hidden_hbm, hidden_ref, sems):
    copies = []
    for i in range(PARTS):
        rows = pl.ds(i * PART, PART)
        copies.append(pltpu.make_async_copy(hidden_hbm.at[rows], hidden_ref.at[rows], sems.at[i]))
    return copies


def encode_kernel(hidden_hbm, weight_hbm, embed_ref, inverse_hbm, hidden_ref, weight_ref, inverse_ref, sems, out_sem):
    weight_copy = pltpu.make_async_copy(weight_hbm, weight_ref, sems.at[PARTS])
    weight_copy.start()
    copies = token_copies(hidden_hbm, hidden_ref, sems)
    for copy in copies[:AHEAD]:
        copy.start()
    weight_copy.wait()
    packed = jnp.zeros((DIM, DIM), F32)
    lane = iota((DIM, DIM), 1)
    begun = AHEAD
    for i in range(STEPS):
        for copy in copies[i * BLOCK // PART : (i + 1) * BLOCK // PART]:
            copy.wait()
            if begun < PARTS:
                copies[begun].start()
                begun += 1

        def tile(t, carry):
            start = i * BLOCK + t * TILE
            rows = pl.ds(pl.multiple_of(start, TILE), TILE)
            proj = dot(hidden_ref[rows, :], weight_ref[...])
            inverse = lax.rsqrt(jnp.sum(proj * proj, axis=-1, keepdims=True) + EPS)
            embed_ref[rows, :] = (proj * inverse).astype(BF)
            for j in range(TILE // DIM):
                carry = jnp.where(lane == start // DIM + j, inverse[j * DIM : (j + 1) * DIM], carry)
            return carry

        packed = lax.fori_loop(0, BLOCK // TILE, tile, packed, unroll=2)
    inverse_ref[...] = packed
    out = pltpu.make_async_copy(inverse_ref, inverse_hbm, out_sem)
    out.start()
    out.wait()


def stored_rows(embed_ref, place_ref, s):
    parts = []
    for k in range(CAP):
        start = pl.multiple_of(place_ref[s, k], 16)
        parts.append(embed_ref[pl.ds(start, PLEN), :])
    return jnp.concatenate(parts, axis=0)


def score_kernel(recv_ref, embed_ref, expo_hbm, recip_hbm, sums_ref, table_hbm, second_hbm, place_hbm, queries_hbm,
                 recip_ref, table_ref, second_ref, place_ref, meta_ref, limit_ref, expo_ref, round_ref,
                 smem_ref, sem, expo_sems, out_sems):
    outs = start_copies(((recv_ref.at[:, pl.ds(0, QROWS)], queries_hbm),), out_sems.at[pl.ds(4, 1)])
    for s in range(N_DEV):
        rows = recv_ref[s, QROWS : QROWS + META, :].astype(F32)
        meta_ref[s : s + 1, :] = rows[0:1, :]
    meta = meta_ref[...]
    place_ref[...] = meta.astype(jnp.int32) * PLEN
    copy = pltpu.make_async_copy(place_ref, smem_ref, sem)
    copy.start()
    outs += start_copies(((place_ref, place_hbm),), out_sems)
    meta_bf = meta.astype(BF)
    spread = expander(1)
    second_ref[...] = dot(pltpu.roll(meta, DIM - SLOTS, 1).astype(BF), spread.astype(BF))
    length = dot(pltpu.roll(meta, DIM - 2 * SLOTS, 1).astype(BF), spread.astype(BF))
    lane = iota((1, WIDE), 1)
    token = lane
    for k in range(1, CAP):
        token = token - jnp.where(lane >= k * PLEN, PLEN, 0)
    limit_ref[...] = jnp.where(token.astype(F32) < length, 1.0, 0.0)
    outs += start_copies(((second_ref, second_hbm),), out_sems.at[pl.ds(1, 1)])
    copy.wait()

    def expo_copy(i):
        rows = pl.ds(i * (CHUNK * QLEN), CHUNK * QLEN)
        return pltpu.make_async_copy(expo_ref.at[rows], expo_hbm.at[rows], expo_sems.at[i])

    def chunk(i, carry):
        for u in range(CHUNK):
            s = i * CHUNK + u
            queries = recv_ref[s, 0:QROWS, :]
            sims = dot(queries, stored_rows(embed_ref, smem_ref, s), COLS_COLS)
            second = second_ref[pl.ds(s, 1), :]
            valid = limit_ref[pl.ds(s, 1), :]
            mine = jnp.where(second > 0.5, sims[QLEN:QROWS], sims[0:QLEN])
            expo = jnp.where(valid > 0.5, jnp.exp(mine * (1.0 / TAU)), 0.0)
            rows = pl.ds(pl.multiple_of(s * QLEN, QLEN), QLEN)
            expo_ref[rows, :] = expo
            round_ref[rows, :] = expo.astype(BF)
        expo_copy(i).start()
        return carry

    lax.fori_loop(0, N_DEV // CHUNK, chunk, 0)
    total = dot(round_ref[...], spread.astype(BF), COLS_COLS)
    total = jnp.where(total > 0.0, total, 1.0)
    recip_ref[...] = 1.0 / total
    outs += start_copies(((recip_ref, recip_hbm),), out_sems.at[pl.ds(2, 1)])
    scores = TAU * jnp.sum(jnp.log(total).reshape(N_DEV, QLEN, DIM), axis=1)
    lane = iota((N_DEV, DIM), 1)
    present = (pltpu.roll(meta, DIM - 6 * SLOTS, 1) > 0.5) & (lane < SLOTS)
    teach = (
        pltpu.roll(meta, DIM - 3 * SLOTS, 1)
        + pltpu.roll(meta, DIM - 4 * SLOTS, 1)
        + pltpu.roll(meta, DIM - 5 * SLOTS, 1)
    )
    teach = jnp.where(present, teach, 0.0)
    student = jnp.where(present, jnp.exp(scores), 0.0)
    which = pltpu.roll(meta, DIM - SLOTS, 1) > 0.5
    table_ref[0] = student
    table_ref[1] = teach
    table_ref[2] = jnp.where(which, 1.0, 0.0)
    outs += start_copies(((table_ref, table_hbm),), out_sems.at[pl.ds(3, 1)])
    gain = teach * scores
    columns = []
    for value in (student, gain):
        columns.append(jnp.sum(jnp.where(which, 0.0, value), axis=-1, keepdims=True))
        columns.append(jnp.sum(jnp.where(which, value, 0.0), axis=-1, keepdims=True))
    mixed = jnp.zeros((N_DEV, DIM), F32)
    for j, column in enumerate(columns):
        mixed = jnp.where(lane == j, column, mixed)
    mixed = jnp.concatenate([mixed, jnp.zeros((DIM - N_DEV, DIM), F32)], axis=0)
    part = jnp.transpose(mixed)[0:8, :]
    for s in range(N_DEV):
        sums_ref[s] = part
    wait_copies(outs)
    wait_copies([expo_copy(i) for i in range(N_DEV // CHUNK)])


def halves(one, second):
    return jnp.concatenate(
        [jnp.where(second, 0.0, one).astype(BF), jnp.where(second, one, 0.0).astype(BF)], axis=0
    )


def ahead_kernel(expo_hbm, recip_hbm, weights_ref, recip_ref, expo_ref, sems):
    steps = N_DEV // GROUP
    span = GROUP * QLEN
    fetch = []
    for i in range(steps):
        rows = pl.ds(i * span, span)
        fetch.append(
            start_copies(
                ((recip_hbm.at[rows], recip_ref.at[rows]), (expo_hbm.at[rows], expo_ref.at[rows])), sems.at[i]
            )
        )
    spread = expander(2).astype(BF)
    lane = iota((span, DIM), 1)
    for i in range(steps):
        rows = pl.ds(i * span, span)
        wait_copies(fetch[i])
        recip = recip_ref[rows, :]
        hi = recip.astype(BF).astype(F32)
        lo = recip - hi
        factor = jnp.where(lane < SLOTS, hi, jnp.where(lane < 2 * SLOTS, pltpu.roll(lo, SLOTS, 1), 0.0))
        weights_ref[rows, :] = (expo_ref[rows, :] * dot(factor.astype(BF), spread)).astype(BF)


def query_kernel(sums_ref, const_hbm, me_ref, table_hbm, second_hbm, weights_ref, embed_ref, place_hbm,
                 send_hbm, mixed_hbm, loss_hbm,
                 const_ref, table_ref, second_ref, loss_ref, wide_ref, send_ref, mixed_ref, smem_ref,
                 sems, out_sems, part_sems):
    small = start_copies(
        ((table_hbm, table_ref), (place_hbm, smem_ref), (const_hbm, const_ref), (second_hbm, second_ref)), sems
    )
    sums = jnp.sum(sums_ref[...], axis=0)
    log_sum = jnp.log(jnp.where(sums > 0.0, sums, 1.0))
    turned = jnp.transpose(jnp.concatenate([sums, jnp.zeros((DIM - 8, DIM), F32)], axis=0))[0:N_DEV, :]
    wait_copies(small)
    loss = const_ref[0:2, :] + log_sum[0:2, :] - sums[2:4, :]
    picked = jnp.where(iota((2, DIM), 1) == me_ref[0], loss, 0.0)
    loss_ref[...] = jnp.broadcast_to(jnp.sum(picked, axis=-1, keepdims=True), (2, DIM))
    normal = jnp.where(table_ref[2] > 0.5, turned[:, 1:2], turned[:, 0:1])
    pull = LOSS_SCALE * (table_ref[0] / normal - table_ref[1])
    outs = start_copies(((loss_ref, loss_hbm),), out_sems)
    hi = pull.astype(BF).astype(F32)
    lo = pull - hi
    lane = iota((N_DEV, DIM), 1)
    factor = jnp.where(lane < SLOTS, hi, jnp.where(lane < 2 * SLOTS, pltpu.roll(lo, SLOTS, 1), 0.0))
    wide_ref[...] = dot(factor.astype(BF), expander(2).astype(BF))

    def part_copies(i):
        some = pl.ds(i * CHUNK, CHUNK)
        rows = pl.ds(i * (CHUNK * QLEN), CHUNK * QLEN)
        return [
            pltpu.make_async_copy(send_ref.at[some], send_hbm.at[some], part_sems.at[i, 0]),
            pltpu.make_async_copy(mixed_ref.at[rows], mixed_hbm.at[rows], part_sems.at[i, 1]),
        ]

    def chunk(i, carry):
        for u in range(CHUNK):
            s = i * CHUNK + u
            rows = pl.ds(pl.multiple_of(s * QLEN, QLEN), QLEN)
            mixed = weights_ref[rows, :].astype(F32) * wide_ref[pl.ds(s, 1), :]
            mixed_ref[rows, :] = mixed.astype(BF)
            both = halves(mixed, second_ref[pl.ds(s, 1), :] > 0.5)
            send_ref[s] = dot(both, stored_rows(embed_ref, smem_ref, s)).astype(BF)
        for copy in part_copies(i):
            copy.start()
        return carry

    lax.fori_loop(0, N_DEV // CHUNK, chunk, 0)
    wait_copies(outs)
    for i in range(N_DEV // CHUNK):
        wait_copies(part_copies(i))


def stored_kernel(place_hbm, queries_hbm, second_hbm, mixed_hbm, inverse_hbm, hidden_hbm, embed_ref,
                  preact_hbm, head_ref,
                  preact_ref, hidden_ref, queries_ref, second_ref, mixed_ref, inverse_ref, delta_ref, place_smem,
                  sems, small_sems, mixed_sems, out_sems):
    steps = N_DEV // GROUP
    small = start_copies(
        ((place_hbm, place_smem), (second_hbm, second_ref), (queries_hbm, queries_ref), (inverse_hbm, inverse_ref)),
        small_sems,
    )
    fetch = []
    for i in range(steps):
        rows = pl.ds(i * GROUP * QLEN, GROUP * QLEN)
        fetch += start_copies(((mixed_hbm.at[rows], mixed_ref.at[rows]),), mixed_sems.at[pl.ds(i, 1)])
    copies = token_copies(hidden_hbm, hidden_ref, sems)
    delta_ref[...] = jnp.zeros_like(delta_ref)
    wait_copies(small)

    for i in range(steps):
        fetch[i].wait()
        for copy in copies[i * PARTS // steps : (i + 1) * PARTS // steps]:
            copy.start()
        for s in range(i * GROUP, (i + 1) * GROUP):
            both = halves(mixed_ref[s * QLEN : (s + 1) * QLEN, :].astype(F32), second_ref[s : s + 1, :] > 0.5)
            part = dot(both, queries_ref[s], ROWS_ROWS)
            for k in range(CAP):
                at = pl.ds(pl.multiple_of(place_smem[s, k], 16), PLEN)
                delta_ref[k % LANES, at, :] += part[k * PLEN : (k + 1) * PLEN]
    total = jnp.zeros((DIM, D), F32)
    outs = []
    for i in range(STEPS):
        rows = pl.ds(i * BLOCK, BLOCK)
        unit = embed_ref[rows, :].astype(F32)
        delta = jnp.sum(delta_ref[:, rows, :], axis=0)
        radial = jnp.sum(unit * delta, axis=-1, keepdims=True)
        tangent = delta - unit * radial
        scaled = []
        for j in range(BLOCK // DIM):
            b = i * (BLOCK // DIM) + j
            scaled.append(tangent[j * DIM : (j + 1) * DIM] * inverse_ref[:, b : b + 1])
        preact = jnp.concatenate(scaled, axis=0).astype(BF)
        preact_ref[rows, :] = preact
        outs += start_copies(((preact_ref.at[rows], preact_hbm.at[rows]),), out_sems.at[pl.ds(i, 1)])
        for j in range(i * BLOCK // PART, (i + 1) * BLOCK // PART):
            copies[j].wait()
        total = total + dot(preact, hidden_ref[rows, :], ROWS_ROWS)
    head_ref[...] = jnp.transpose(total)
    wait_copies(outs)


def back_kernel(preact_ref, weight_ref, query_ref, grad_ref, query_grad_ref):
    grad_ref[...] = dot(preact_ref[...], weight_ref[...], COLS_COLS).astype(BF)

    @pl.when(pl.program_id(0) == 0)
    def _():
        query_grad_ref[...] = dot(query_ref[...], weight_ref[...], COLS_COLS).astype(BF)


def finish_kernel(recv_ref, hidden_hbm, proj_hbm, head_ref, preact_ref, send_ref,
                  hidden_ref, proj_ref, sems):
    copies = start_copies(((proj_hbm, proj_ref), (hidden_hbm, hidden_ref)), sems)
    delta = jnp.sum(recv_ref[...].astype(F32), axis=0)
    copies[0].wait()
    proj = proj_ref[...]
    inverse = lax.rsqrt(jnp.sum(proj * proj, axis=-1, keepdims=True) + EPS)
    unit = proj * inverse
    radial = jnp.sum(unit * delta, axis=-1, keepdims=True)
    preact = ((delta - unit * radial) * inverse).astype(BF)
    preact_ref[...] = preact
    wait_copies(copies[1:])
    head = head_ref[...] + dot(hidden_ref[...], preact, ROWS_ROWS)
    send_ref[0:HEAD_TILES] = head.reshape(HEAD_TILES, 8, DIM).astype(BF)
    send_ref[HEAD_TILES:N_ALL] = jnp.zeros((N_ALL - HEAD_TILES, 8, DIM), BF)


def reduce_kernel(recv_ref, send_ref):
    total = jnp.sum(recv_ref[...].astype(F32), axis=0).astype(BF)
    send_ref[...] = jnp.broadcast_to(total[None], (N_ALL, 8, DIM))


def shape(dims, kind):
    return jax.ShapeDtypeStruct(dims, kind)


def in_hbm(x):
    return pltpu.with_memory_space_constraint(x, pltpu.HBM)


def in_vmem(x):
    return pltpu.with_memory_space_constraint(x, pltpu.VMEM)


def exchange(x, axes):
    return lax.all_to_all(x, axes, split_axis=0, concat_axis=0, tiled=True)


def estimate(flops, size):
    return pl.CostEstimate(flops=flops, bytes_accessed=size, transcendentals=0)


def on_device(query_hidden, passage_hidden, head_weight, teacher, candidates, storage, lengths):
    query_flat = in_hbm(query_hidden.reshape(QROWS, D))
    flat_hidden = in_hbm(passage_hidden.reshape(TOKENS, D))
    head_weight = in_hbm(head_weight)
    send, query_proj, const = pl.pallas_call(
        request_kernel,
        out_shape=(
            pltpu.HBM((N_DEV, QROWS + META, DIM), BF),
            pltpu.HBM((QROWS, DIM), F32),
            pltpu.HBM((8, DIM), F32),
        ),
        in_specs=[HBM] * 6,
        out_specs=(HBM, HBM, HBM),
        scratch_shapes=[
            pltpu.VMEM((QROWS, D), BF),
            pltpu.VMEM((D, DIM), BF),
            pltpu.VMEM((2, PER_QUERY), F32),
            pltpu.VMEM((2, PER_QUERY), jnp.int32),
            pltpu.VMEM((1, N_DEV * STORED), jnp.int32),
            pltpu.VMEM((1, N_DEV * STORED), jnp.int32),
            pltpu.VMEM((N_DEV, DIM), jnp.int32),
            pltpu.VMEM((N_DEV, DIM), jnp.int32),
            pltpu.VMEM((QROWS, DIM), F32),
            pltpu.VMEM((8, DIM), F32),
            pltpu.VMEM((QROWS, DIM), BF),
            pltpu.VMEM((N_DEV, META, DIM), BF),
            pltpu.SemaphoreType.DMA((6,)),
            pltpu.SemaphoreType.DMA((3,)),
            pltpu.SemaphoreType.DMA((N_DEV,)),
        ],
        compiler_params=params(4),
        name="request",
    )(query_flat, head_weight, in_hbm(teacher), in_hbm(candidates), in_hbm(storage), in_hbm(lengths))
    recv = exchange(send, "dev")

    embed, inverse = pl.pallas_call(
        encode_kernel,
        out_shape=(pltpu.VMEM((TOKENS, DIM), BF), pltpu.HBM((DIM, DIM), F32)),
        in_specs=[HBM, HBM],
        out_specs=(VMEM, HBM),
        scratch_shapes=[
            pltpu.VMEM((TOKENS, D), BF),
            pltpu.VMEM((D, DIM), BF),
            pltpu.VMEM((DIM, DIM), F32),
            pltpu.SemaphoreType.DMA((PARTS + 1,)),
            pltpu.SemaphoreType.DMA,
        ],
        cost_estimate=estimate(2 * TOKENS * D * DIM, 15_000_000),
        compiler_params=params(20),
        name="encode",
    )(flat_hidden, head_weight)

    expo, recip, sums, table, second, place, queries = pl.pallas_call(
        score_kernel,
        out_shape=(
            pltpu.HBM((N_DEV * QLEN, WIDE), F32),
            pltpu.HBM((N_DEV * QLEN, DIM), F32),
            shape((N_DEV, 8, DIM), F32),
            pltpu.HBM((3, N_DEV, DIM), F32),
            pltpu.HBM((N_DEV, WIDE), F32),
            pltpu.HBM((N_DEV, DIM), jnp.int32),
            pltpu.HBM((N_DEV, QROWS, DIM), BF),
        ),
        in_specs=[VMEM] * 2,
        out_specs=(HBM, HBM, VMEM, HBM, HBM, HBM, HBM),
        scratch_shapes=[
            pltpu.VMEM((N_DEV * QLEN, DIM), F32),
            pltpu.VMEM((3, N_DEV, DIM), F32),
            pltpu.VMEM((N_DEV, WIDE), F32),
            pltpu.VMEM((N_DEV, DIM), jnp.int32),
            pltpu.VMEM((N_DEV, DIM), F32),
            pltpu.VMEM((N_DEV, WIDE), F32),
            pltpu.VMEM((N_DEV * QLEN, WIDE), F32),
            pltpu.VMEM((N_DEV * QLEN, WIDE), BF),
            pltpu.SMEM((N_DEV, DIM), jnp.int32),
            pltpu.SemaphoreType.DMA,
            pltpu.SemaphoreType.DMA((N_DEV // CHUNK,)),
            pltpu.SemaphoreType.DMA((5,)),
        ],
        compiler_params=params(14),
        name="score",
    )(recv, in_vmem(embed))
    all_sums = exchange(sums, "dev")

    weights = pl.pallas_call(
        ahead_kernel,
        out_shape=pltpu.VMEM((N_DEV * QLEN, WIDE), BF),
        in_specs=[HBM, HBM],
        out_specs=VMEM,
        scratch_shapes=[
            pltpu.VMEM((N_DEV * QLEN, DIM), F32),
            pltpu.VMEM((N_DEV * QLEN, WIDE), F32),
            pltpu.SemaphoreType.DMA((N_DEV // GROUP, 2)),
        ],
        cost_estimate=estimate(2 * TOKENS * D * DIM, 15_000_000),
        compiler_params=params(12),
        name="ahead",
    )(in_hbm(expo), in_hbm(recip))

    me = lax.axis_index("dev").astype(jnp.int32).reshape(1)
    send_delta, mixed, loss = pl.pallas_call(
        query_kernel,
        out_shape=(
            pltpu.HBM((N_DEV, QROWS, DIM), BF),
            pltpu.HBM((N_DEV * QLEN, WIDE), BF),
            pltpu.HBM((2, DIM), F32),
        ),
        in_specs=[VMEM, HBM, SMEM, HBM, HBM, VMEM, VMEM, HBM],
        out_specs=(HBM, HBM, HBM),
        scratch_shapes=[
            pltpu.VMEM((8, DIM), F32),
            pltpu.VMEM((3, N_DEV, DIM), F32),
            pltpu.VMEM((N_DEV, WIDE), F32),
            pltpu.VMEM((2, DIM), F32),
            pltpu.VMEM((N_DEV, WIDE), F32),
            pltpu.VMEM((N_DEV, QROWS, DIM), BF),
            pltpu.VMEM((N_DEV * QLEN, WIDE), BF),
            pltpu.SMEM((N_DEV, DIM), jnp.int32),
            pltpu.SemaphoreType.DMA((4,)),
            pltpu.SemaphoreType.DMA((1,)),
            pltpu.SemaphoreType.DMA((N_DEV // CHUNK, 2)),
        ],
        compiler_params=params(12),
        name="query",
    )(all_sums, in_hbm(const), me, in_hbm(table), in_hbm(second), in_vmem(weights), in_vmem(embed), in_hbm(place))
    recv_delta = exchange(send_delta, "dev")

    preact, head = pl.pallas_call(
        stored_kernel,
        out_shape=(pltpu.HBM((TOKENS, DIM), BF), pltpu.VMEM((D, DIM), F32)),
        in_specs=[HBM] * 6 + [VMEM],
        out_specs=(HBM, VMEM),
        scratch_shapes=[
            pltpu.VMEM((TOKENS, DIM), BF),
            pltpu.VMEM((TOKENS, D), BF),
            pltpu.VMEM((N_DEV, QROWS, DIM), BF),
            pltpu.VMEM((N_DEV, WIDE), F32),
            pltpu.VMEM((N_DEV * QLEN, WIDE), BF),
            pltpu.VMEM((DIM, DIM), F32),
            pltpu.VMEM((LANES, TOKENS, DIM), F32),
            pltpu.SMEM((N_DEV, DIM), jnp.int32),
            pltpu.SemaphoreType.DMA((PARTS,)),
            pltpu.SemaphoreType.DMA((4,)),
            pltpu.SemaphoreType.DMA((N_DEV // GROUP,)),
            pltpu.SemaphoreType.DMA((STEPS,)),
        ],
        cost_estimate=estimate(4 * TOKENS * D * DIM, 20_000_000),
        compiler_params=params(40),
        name="stored",
    )(
        in_hbm(place), in_hbm(queries), in_hbm(second), in_hbm(mixed), in_hbm(inverse), flat_hidden, in_vmem(embed)
    )

    query_preact, send_head = pl.pallas_call(
        finish_kernel,
        out_shape=(pltpu.VMEM((QROWS, DIM), BF), shape((N_ALL, 8, DIM), BF)),
        in_specs=[VMEM, HBM, HBM, VMEM],
        out_specs=(VMEM,) * 2,
        scratch_shapes=[
            pltpu.VMEM((QROWS, D), BF),
            pltpu.VMEM((QROWS, DIM), F32),
            pltpu.SemaphoreType.DMA((2,)),
        ],
        compiler_params=params(8),
        name="finish",
    )(recv_delta, query_flat, in_hbm(query_proj), in_vmem(head))
    recv_head = exchange(send_head, ("group", "dev"))

    passage_grad, query_grad = pl.pallas_call(
        back_kernel,
        grid=(STEPS,),
        out_shape=(pltpu.HBM((TOKENS, D), BF), pltpu.HBM((QROWS, D), BF)),
        in_specs=[
            pl.BlockSpec((BLOCK, DIM), lambda i: (i, 0)),
            pl.BlockSpec((D, DIM), lambda i: (0, 0)),
            pl.BlockSpec((QROWS, DIM), lambda i: (0, 0)),
        ],
        out_specs=(pl.BlockSpec((BLOCK, D), lambda i: (i, 0)), pl.BlockSpec((QROWS, D), lambda i: (0, 0))),
        cost_estimate=estimate(2 * TOKENS * D * DIM, 15_000_000),
        compiler_params=params(20),
        name="back",
    )(in_hbm(preact), head_weight, query_preact)

    send_total = pl.pallas_call(
        reduce_kernel,
        out_shape=shape((N_ALL, 8, DIM), BF),
        in_specs=[VMEM],
        out_specs=VMEM,
        compiler_params=params(4),
        name="reduce",
    )(recv_head)
    head_all = exchange(send_total, ("group", "dev"))
    head_grad = head_all[:HEAD_TILES].reshape(D, DIM).astype(F32)
    return (
        loss[:, 0],
        head_grad,
        query_grad.reshape(2, QLEN, D),
        passage_grad.reshape(STORED, PLEN, D),
    )


def solution(mesh):
    return jax.shard_map(
        on_device,
        mesh=mesh,
        in_specs=(
            P(("group", "dev"), None, None),
            P(("group", "dev"), None, None),
            P(),
            P(("group", "dev"), None),
            P(("group", "dev"), None),
            P("group", None),
            P("group", None),
        ),
        out_specs=(
            P(("group", "dev")),
            P(),
            P(("group", "dev"), None, None),
            P(("group", "dev"), None, None),
        ),
        check_vma=False,
    )
```

```python
import jax
import jax.numpy as jnp
from jax import lax
from jax.experimental import pallas as pl
from jax.experimental.pallas import tpu as pltpu
from jax.sharding import PartitionSpec as P

TAU = 0.0625
LOSS_SCALE = 32768.0
EPS = 1e-06

N_DEV = 32
N_ALL = 128
STORED = 128
PLEN = 48
QLEN = 32
D = 768
DIM = 128
PER_QUERY = 64
CAP = 12
SLOTS = 16
WIDE = CAP * PLEN
QROWS = 2 * QLEN
META = 16
CHUNK = 8
GROUP = 16
TOKENS = STORED * PLEN
BLOCK = 1536
STEPS = TOKENS // BLOCK
LANES = 1
PART = 768
PARTS = TOKENS // PART
AHEAD = 4
TILE = 256
HEAD_TILES = D // 8

BF = jnp.bfloat16
F32 = jnp.float32
ROWS_ROWS = (((0,), (0,)), ((), ()))
COLS_COLS = (((1,), (1,)), ((), ()))
VMEM = pl.BlockSpec(memory_space=pltpu.VMEM)
SMEM = pl.BlockSpec(memory_space=pltpu.SMEM)
HBM = pl.BlockSpec(memory_space=pltpu.HBM)


def params(mib):
    return pltpu.CompilerParams(vmem_limit_bytes=mib * 1024 * 1024)


def dot(a, b, dims=(((1,), (0,)), ((), ()))):
    return lax.dot_general(a, b, dims, preferred_element_type=F32)


def iota(shape, axis):
    return lax.broadcasted_iota(jnp.int32, shape, axis)


def start_copies(pairs, sems):
    copies = [pltpu.make_async_copy(a, b, sems.at[i]) for i, (a, b) in enumerate(pairs)]
    for copy in copies:
        copy.start()
    return copies


def wait_copies(copies):
    for copy in copies:
        copy.wait()


def split3(x):
    hi = x.astype(BF).astype(F32)
    mid = (x - hi).astype(BF).astype(F32)
    return hi, mid, (x - hi - mid)


def expander(copies):
    row = iota((DIM, WIDE), 0)
    slot = (row & (SLOTS - 1)) * PLEN
    lane = iota((DIM, WIDE), 1)
    hit = (lane >= slot) & (lane < slot + PLEN) & (row < copies * SLOTS)
    return jnp.where(hit, 1.0, 0.0)


def request_kernel(hidden_hbm, weight_hbm, teacher_hbm, cand_hbm, storage_hbm, lengths_hbm,
                   send_hbm, proj_hbm, const_hbm,
                   hidden_ref, weight_ref, teacher_ref, cand_ref, storage_ref, lengths_ref,
                   place_ref, length_ref, proj_ref, const_ref, embed_ref, meta_ref, sems, out_sems, send_sems):
    small = start_copies(
        (
            (cand_hbm, cand_ref),
            (storage_hbm, storage_ref),
            (lengths_hbm, lengths_ref),
            (teacher_hbm, teacher_ref),
            (weight_hbm, weight_ref),
            (hidden_hbm, hidden_ref),
        ),
        sems,
    )
    wait_copies(small[4:])
    proj = dot(hidden_ref[...], weight_ref[...])
    proj_ref[...] = proj
    inverse = lax.rsqrt(jnp.sum(proj * proj, axis=-1, keepdims=True) + EPS)
    embed_ref[...] = (proj * inverse).astype(BF)
    sends = start_copies(
        [(embed_ref, send_hbm.at[s, pl.ds(0, QROWS)]) for s in range(N_DEV)], send_sems
    )
    wait_copies(small[:4])
    for i in range(N_DEV):
        place_ref[i : i + 1, :] = storage_ref[0:1, i * STORED : (i + 1) * STORED]
        length_ref[i : i + 1, :] = lengths_ref[0:1, i * STORED : (i + 1) * STORED]
    teacher = teacher_ref[...]
    log_t = teacher - jnp.log(jnp.sum(jnp.exp(teacher), axis=-1, keepdims=True))
    prob = jnp.exp(log_t)
    const = jnp.sum(prob * log_t, axis=-1, keepdims=True)
    const_ref[...] = jnp.concatenate(
        [jnp.broadcast_to(const, (2, DIM)), jnp.zeros((6, DIM), F32)], axis=0
    )
    outs = start_copies(((proj_ref, proj_hbm), (const_ref, const_hbm)), out_sems)
    prob_row = jnp.concatenate([prob[0:1], prob[1:2]], axis=1)
    cand = cand_ref[...]
    cand_row = jnp.concatenate([cand[0:1], cand[1:2]], axis=1)

    place = place_ref[...]
    owner_table = (place >> 7).astype(F32).astype(BF)
    slot_table = (place & (STORED - 1)).astype(F32).astype(BF)
    length_table = length_ref[...].astype(F32).astype(BF)
    sub32 = iota((N_DEV, DIM), 0)
    sub128 = iota((DIM, DIM), 0)
    lane128 = iota((DIM, DIM), 1)
    high = jnp.where(sub32 == (cand_row >> 7), 1.0, 0.0).astype(BF)
    low = sub128 == (cand_row & (STORED - 1))
    owner = jnp.sum(jnp.where(low, dot(owner_table, high, ROWS_ROWS), 0.0), axis=0, keepdims=True)
    slot = jnp.sum(jnp.where(low, dot(slot_table, high, ROWS_ROWS), 0.0), axis=0, keepdims=True)
    match = jnp.where(sub32 == owner.astype(jnp.int32), 1.0, 0.0)
    match_bf = match.astype(BF)
    at_slot = sub128 == slot.astype(jnp.int32)
    length = jnp.sum(
        jnp.where(at_slot, dot(length_table, match_bf, ROWS_ROWS), 0.0), axis=0, keepdims=True
    )
    earlier = jnp.where(sub128 < lane128, 1.0, 0.0).astype(BF)
    rank = jnp.sum(match * dot(match_bf, earlier), axis=0, keepdims=True).astype(jnp.int32)
    t_hi, t_mid, t_lo = split3(prob_row)
    which = jnp.where(iota((1, DIM), 1) >= PER_QUERY, 1.0, 0.0)
    fields = (slot, which, length, t_hi, t_mid, t_lo, jnp.ones((1, DIM), F32))
    field_of = sub128 >> 4
    values = jnp.zeros((DIM, DIM), F32)
    for f, row in enumerate(fields):
        values = jnp.where(field_of == f, row, values)
    values = jnp.where((sub128 & (SLOTS - 1)) == rank, values, 0.0).astype(BF)
    meta = dot(match_bf, values, COLS_COLS)
    for s in range(N_DEV):
        meta_ref[s] = jnp.broadcast_to(meta[s : s + 1], (META, DIM)).astype(BF)
    outs += start_copies(((meta_ref, send_hbm.at[:, pl.ds(QROWS, META)]),), out_sems.at[pl.ds(2, 1)])
    wait_copies(sends)
    wait_copies(outs)


def token_copies(hidden_hbm, hidden_ref, sems):
    copies = []
    for i in range(PARTS):
        rows = pl.ds(i * PART, PART)
        copies.append(pltpu.make_async_copy(hidden_hbm.at[rows], hidden_ref.at[rows], sems.at[i]))
    return copies


def encode_kernel(hidden_hbm, weight_hbm, embed_ref, inverse_hbm, hidden_ref, weight_ref, inverse_ref, sems, out_sem):
    weight_copy = pltpu.make_async_copy(weight_hbm, weight_ref, sems.at[PARTS])
    weight_copy.start()
    copies = token_copies(hidden_hbm, hidden_ref, sems)
    for copy in copies[:AHEAD]:
        copy.start()
    weight_copy.wait()
    packed = jnp.zeros((DIM, DIM), F32)
    lane = iota((DIM, DIM), 1)
    begun = AHEAD
    for i in range(STEPS):
        for copy in copies[i * BLOCK // PART : (i + 1) * BLOCK // PART]:
            copy.wait()
            if begun < PARTS:
                copies[begun].start()
                begun += 1

        def tile(t, carry):
            start = i * BLOCK + t * TILE
            rows = pl.ds(pl.multiple_of(start, TILE), TILE)
            proj = dot(hidden_ref[rows, :], weight_ref[...])
            inverse = lax.rsqrt(jnp.sum(proj * proj, axis=-1, keepdims=True) + EPS)
            embed_ref[rows, :] = (proj * inverse).astype(BF)
            for j in range(TILE // DIM):
                carry = jnp.where(lane == start // DIM + j, inverse[j * DIM : (j + 1) * DIM], carry)
            return carry

        packed = lax.fori_loop(0, BLOCK // TILE, tile, packed, unroll=2)
    inverse_ref[...] = packed
    out = pltpu.make_async_copy(inverse_ref, inverse_hbm, out_sem)
    out.start()
    out.wait()


def stored_rows(embed_ref, place_ref, s):
    parts = []
    for k in range(CAP):
        start = pl.multiple_of(place_ref[s, k], 16)
        parts.append(embed_ref[pl.ds(start, PLEN), :])
    return jnp.concatenate(parts, axis=0)


def score_kernel(recv_ref, embed_ref, expo_hbm, recip_hbm, sums_ref, table_hbm, second_hbm, place_hbm, queries_hbm,
                 recip_ref, table_ref, second_ref, place_ref, meta_ref, limit_ref, expo_ref, round_ref,
                 smem_ref, sem, expo_sems, out_sems):
    outs = start_copies(((recv_ref.at[:, pl.ds(0, QROWS)], queries_hbm),), out_sems.at[pl.ds(4, 1)])
    for s in range(N_DEV):
        rows = recv_ref[s, QROWS : QROWS + META, :].astype(F32)
        meta_ref[s : s + 1, :] = rows[0:1, :]
    meta = meta_ref[...]
    place_ref[...] = meta.astype(jnp.int32) * PLEN
    copy = pltpu.make_async_copy(place_ref, smem_ref, sem)
    copy.start()
    outs += start_copies(((place_ref, place_hbm),), out_sems)
    meta_bf = meta.astype(BF)
    spread = expander(1)
    second_ref[...] = dot(pltpu.roll(meta, DIM - SLOTS, 1).astype(BF), spread.astype(BF))
    length = dot(pltpu.roll(meta, DIM - 2 * SLOTS, 1).astype(BF), spread.astype(BF))
    lane = iota((1, WIDE), 1)
    token = lane
    for k in range(1, CAP):
        token = token - jnp.where(lane >= k * PLEN, PLEN, 0)
    limit_ref[...] = jnp.where(token.astype(F32) < length, 1.0, 0.0)
    outs += start_copies(((second_ref, second_hbm),), out_sems.at[pl.ds(1, 1)])
    copy.wait()

    def expo_copy(i):
        rows = pl.ds(i * (CHUNK * QLEN), CHUNK * QLEN)
        return pltpu.make_async_copy(expo_ref.at[rows], expo_hbm.at[rows], expo_sems.at[i])

    def chunk(i, carry):
        for u in range(CHUNK):
            s = i * CHUNK + u
            queries = recv_ref[s, 0:QROWS, :]
            sims = dot(queries, stored_rows(embed_ref, smem_ref, s), COLS_COLS)
            second = second_ref[pl.ds(s, 1), :]
            valid = limit_ref[pl.ds(s, 1), :]
            mine = jnp.where(second > 0.5, sims[QLEN:QROWS], sims[0:QLEN])
            expo = jnp.where(valid > 0.5, jnp.exp(mine * (1.0 / TAU)), 0.0)
            rows = pl.ds(pl.multiple_of(s * QLEN, QLEN), QLEN)
            expo_ref[rows, :] = expo
            round_ref[rows, :] = expo.astype(BF)
        expo_copy(i).start()
        return carry

    for i in range(N_DEV // CHUNK):
        chunk(i, 0)
    total = dot(round_ref[...], spread.astype(BF), COLS_COLS)
    total = jnp.where(total > 0.0, total, 1.0)
    recip_ref[...] = 1.0 / total
    outs += start_copies(((recip_ref, recip_hbm),), out_sems.at[pl.ds(2, 1)])
    scores = TAU * jnp.sum(jnp.log(total).reshape(N_DEV, QLEN, DIM), axis=1)
    lane = iota((N_DEV, DIM), 1)
    present = (pltpu.roll(meta, DIM - 6 * SLOTS, 1) > 0.5) & (lane < SLOTS)
    teach = (
        pltpu.roll(meta, DIM - 3 * SLOTS, 1)
        + pltpu.roll(meta, DIM - 4 * SLOTS, 1)
        + pltpu.roll(meta, DIM - 5 * SLOTS, 1)
    )
    teach = jnp.where(present, teach, 0.0)
    student = jnp.where(present, jnp.exp(scores), 0.0)
    which = pltpu.roll(meta, DIM - SLOTS, 1) > 0.5
    table_ref[0] = student
    table_ref[1] = teach
    table_ref[2] = jnp.where(which, 1.0, 0.0)
    outs += start_copies(((table_ref, table_hbm),), out_sems.at[pl.ds(3, 1)])
    gain = teach * scores
    columns = []
    for value in (student, gain):
        columns.append(jnp.sum(jnp.where(which, 0.0, value), axis=-1, keepdims=True))
        columns.append(jnp.sum(jnp.where(which, value, 0.0), axis=-1, keepdims=True))
    mixed = jnp.zeros((N_DEV, DIM), F32)
    for j, column in enumerate(columns):
        mixed = jnp.where(lane == j, column, mixed)
    mixed = jnp.concatenate([mixed, jnp.zeros((DIM - N_DEV, DIM), F32)], axis=0)
    part = jnp.transpose(mixed)[0:8, :]
    for s in range(N_DEV):
        sums_ref[s] = part
    wait_copies(outs)
    wait_copies([expo_copy(i) for i in range(N_DEV // CHUNK)])


def halves(one, second):
    return jnp.concatenate(
        [jnp.where(second, 0.0, one).astype(BF), jnp.where(second, one, 0.0).astype(BF)], axis=0
    )


def ahead_kernel(expo_hbm, recip_hbm, weights_ref, recip_ref, expo_ref, sems):
    steps = N_DEV // GROUP
    span = GROUP * QLEN
    fetch = []
    for i in range(steps):
        rows = pl.ds(i * span, span)
        fetch.append(
            start_copies(
                ((recip_hbm.at[rows], recip_ref.at[rows]), (expo_hbm.at[rows], expo_ref.at[rows])), sems.at[i]
            )
        )
    spread = expander(2).astype(BF)
    lane = iota((span, DIM), 1)
    for i in range(steps):
        rows = pl.ds(i * span, span)
        wait_copies(fetch[i])
        recip = recip_ref[rows, :]
        hi = recip.astype(BF).astype(F32)
        lo = recip - hi
        factor = jnp.where(lane < SLOTS, hi, jnp.where(lane < 2 * SLOTS, pltpu.roll(lo, SLOTS, 1), 0.0))
        weights_ref[rows, :] = (expo_ref[rows, :] * dot(factor.astype(BF), spread)).astype(BF)


def query_kernel(sums_ref, const_hbm, me_ref, table_hbm, second_hbm, weights_ref, embed_ref, place_hbm,
                 send_hbm, mixed_hbm, loss_hbm,
                 const_ref, table_ref, second_ref, loss_ref, wide_ref, send_ref, mixed_ref, smem_ref,
                 sems, out_sems, part_sems):
    small = start_copies(
        ((table_hbm, table_ref), (place_hbm, smem_ref), (const_hbm, const_ref), (second_hbm, second_ref)), sems
    )
    sums = jnp.sum(sums_ref[...], axis=0)
    log_sum = jnp.log(jnp.where(sums > 0.0, sums, 1.0))
    turned = jnp.transpose(jnp.concatenate([sums, jnp.zeros((DIM - 8, DIM), F32)], axis=0))[0:N_DEV, :]
    wait_copies(small)
    loss = const_ref[0:2, :] + log_sum[0:2, :] - sums[2:4, :]
    picked = jnp.where(iota((2, DIM), 1) == me_ref[0], loss, 0.0)
    loss_ref[...] = jnp.broadcast_to(jnp.sum(picked, axis=-1, keepdims=True), (2, DIM))
    normal = jnp.where(table_ref[2] > 0.5, turned[:, 1:2], turned[:, 0:1])
    pull = LOSS_SCALE * (table_ref[0] / normal - table_ref[1])
    outs = start_copies(((loss_ref, loss_hbm),), out_sems)
    hi = pull.astype(BF).astype(F32)
    lo = pull - hi
    lane = iota((N_DEV, DIM), 1)
    factor = jnp.where(lane < SLOTS, hi, jnp.where(lane < 2 * SLOTS, pltpu.roll(lo, SLOTS, 1), 0.0))
    wide_ref[...] = dot(factor.astype(BF), expander(2).astype(BF))

    def part_copies(i):
        some = pl.ds(i * CHUNK, CHUNK)
        rows = pl.ds(i * (CHUNK * QLEN), CHUNK * QLEN)
        return [
            pltpu.make_async_copy(send_ref.at[some], send_hbm.at[some], part_sems.at[i, 0]),
            pltpu.make_async_copy(mixed_ref.at[rows], mixed_hbm.at[rows], part_sems.at[i, 1]),
        ]

    def chunk(i, carry):
        for u in range(CHUNK):
            s = i * CHUNK + u
            rows = pl.ds(pl.multiple_of(s * QLEN, QLEN), QLEN)
            mixed = weights_ref[rows, :].astype(F32) * wide_ref[pl.ds(s, 1), :]
            mixed_ref[rows, :] = mixed.astype(BF)
            both = halves(mixed, second_ref[pl.ds(s, 1), :] > 0.5)
            send_ref[s] = dot(both, stored_rows(embed_ref, smem_ref, s)).astype(BF)
        for copy in part_copies(i):
            copy.start()
        return carry

    for i in range(N_DEV // CHUNK):
        chunk(i, 0)
    wait_copies(outs)
    for i in range(N_DEV // CHUNK):
        wait_copies(part_copies(i))


def stored_kernel(place_hbm, queries_hbm, second_hbm, mixed_hbm, inverse_hbm, hidden_hbm, embed_ref,
                  preact_hbm, head_ref,
                  preact_ref, hidden_ref, queries_ref, second_ref, mixed_ref, inverse_ref, delta_ref, place_smem,
                  sems, small_sems, mixed_sems, out_sems):
    steps = N_DEV // GROUP
    small = start_copies(
        ((place_hbm, place_smem), (second_hbm, second_ref), (queries_hbm, queries_ref), (inverse_hbm, inverse_ref)),
        small_sems,
    )
    fetch = []
    for i in range(steps):
        rows = pl.ds(i * GROUP * QLEN, GROUP * QLEN)
        fetch += start_copies(((mixed_hbm.at[rows], mixed_ref.at[rows]),), mixed_sems.at[pl.ds(i, 1)])
    copies = token_copies(hidden_hbm, hidden_ref, sems)
    delta_ref[...] = jnp.zeros_like(delta_ref)
    wait_copies(small)

    for i in range(steps):
        fetch[i].wait()
        for copy in copies[i * PARTS // steps : (i + 1) * PARTS // steps]:
            copy.start()
        for s in range(i * GROUP, (i + 1) * GROUP):
            both = halves(mixed_ref[s * QLEN : (s + 1) * QLEN, :].astype(F32), second_ref[s : s + 1, :] > 0.5)
            part = dot(both, queries_ref[s], ROWS_ROWS)
            for k in range(CAP):
                at = pl.ds(pl.multiple_of(place_smem[s, k], 16), PLEN)
                delta_ref[k % LANES, at, :] += part[k * PLEN : (k + 1) * PLEN]
    total = jnp.zeros((DIM, D), F32)
    outs = []
    for i in range(STEPS):
        rows = pl.ds(i * BLOCK, BLOCK)
        unit = embed_ref[rows, :].astype(F32)
        delta = jnp.sum(delta_ref[:, rows, :], axis=0)
        radial = jnp.sum(unit * delta, axis=-1, keepdims=True)
        tangent = delta - unit * radial
        scaled = []
        for j in range(BLOCK // DIM):
            b = i * (BLOCK // DIM) + j
            scaled.append(tangent[j * DIM : (j + 1) * DIM] * inverse_ref[:, b : b + 1])
        preact = jnp.concatenate(scaled, axis=0).astype(BF)
        preact_ref[rows, :] = preact
        outs += start_copies(((preact_ref.at[rows], preact_hbm.at[rows]),), out_sems.at[pl.ds(i, 1)])
        for j in range(i * BLOCK // PART, (i + 1) * BLOCK // PART):
            copies[j].wait()
        total = total + dot(preact, hidden_ref[rows, :], ROWS_ROWS)
    head_ref[...] = jnp.transpose(total)
    wait_copies(outs)


def back_kernel(preact_hbm, weight_hbm, query_ref, grad_hbm, query_grad_hbm,
                preact_ref, weight_ref, grad_ref, query_grad_ref, sems, out_sems):
    copies = start_copies(((weight_hbm, weight_ref), (preact_hbm, preact_ref)), sems)
    wait_copies(copies)
    outs = []
    for i in range(PARTS):

        def tile(t, carry):
            rows = pl.ds(pl.multiple_of(i * PART + t * TILE, TILE), TILE)
            grad_ref[rows, :] = dot(preact_ref[rows, :], weight_ref[...], COLS_COLS).astype(BF)
            return carry

        lax.fori_loop(0, PART // TILE, tile, 0, unroll=2)
        rows = pl.ds(i * PART, PART)
        outs += start_copies(((grad_ref.at[rows], grad_hbm.at[rows]),), out_sems.at[pl.ds(i, 1)])
    query_grad_ref[...] = dot(query_ref[...], weight_ref[...], COLS_COLS).astype(BF)
    outs += start_copies(((query_grad_ref, query_grad_hbm),), out_sems.at[pl.ds(PARTS, 1)])
    wait_copies(outs)


def finish_kernel(recv_ref, hidden_hbm, proj_hbm, head_ref, preact_ref, send_ref,
                  hidden_ref, proj_ref, sems):
    copies = start_copies(((proj_hbm, proj_ref), (hidden_hbm, hidden_ref)), sems)
    delta = jnp.sum(recv_ref[...].astype(F32), axis=0)
    copies[0].wait()
    proj = proj_ref[...]
    inverse = lax.rsqrt(jnp.sum(proj * proj, axis=-1, keepdims=True) + EPS)
    unit = proj * inverse
    radial = jnp.sum(unit * delta, axis=-1, keepdims=True)
    preact = ((delta - unit * radial) * inverse).astype(BF)
    preact_ref[...] = preact
    wait_copies(copies[1:])
    head = head_ref[...] + dot(hidden_ref[...], preact, ROWS_ROWS)
    send_ref[0:HEAD_TILES] = head.reshape(HEAD_TILES, 8, DIM).astype(BF)
    send_ref[HEAD_TILES:N_ALL] = jnp.zeros((N_ALL - HEAD_TILES, 8, DIM), BF)


def reduce_kernel(recv_ref, send_ref):
    total = jnp.sum(recv_ref[...].astype(F32), axis=0).astype(BF)
    send_ref[...] = jnp.broadcast_to(total[None], (N_ALL, 8, DIM))


def shape(dims, kind):
    return jax.ShapeDtypeStruct(dims, kind)


def in_hbm(x):
    return pltpu.with_memory_space_constraint(x, pltpu.HBM)


def in_vmem(x):
    return pltpu.with_memory_space_constraint(x, pltpu.VMEM)


def exchange(x, axes):
    return lax.all_to_all(x, axes, split_axis=0, concat_axis=0, tiled=True)


def estimate(flops, size):
    return pl.CostEstimate(flops=flops, bytes_accessed=size, transcendentals=0)


def on_device(query_hidden, passage_hidden, head_weight, teacher, candidates, storage, lengths):
    query_flat = in_hbm(query_hidden.reshape(QROWS, D))
    flat_hidden = in_hbm(passage_hidden.reshape(TOKENS, D))
    head_weight = in_hbm(head_weight)
    send, query_proj, const = pl.pallas_call(
        request_kernel,
        out_shape=(
            pltpu.HBM((N_DEV, QROWS + META, DIM), BF),
            pltpu.HBM((QROWS, DIM), F32),
            pltpu.HBM((8, DIM), F32),
        ),
        in_specs=[HBM] * 6,
        out_specs=(HBM, HBM, HBM),
        scratch_shapes=[
            pltpu.VMEM((QROWS, D), BF),
            pltpu.VMEM((D, DIM), BF),
            pltpu.VMEM((2, PER_QUERY), F32),
            pltpu.VMEM((2, PER_QUERY), jnp.int32),
            pltpu.VMEM((1, N_DEV * STORED), jnp.int32),
            pltpu.VMEM((1, N_DEV * STORED), jnp.int32),
            pltpu.VMEM((N_DEV, DIM), jnp.int32),
            pltpu.VMEM((N_DEV, DIM), jnp.int32),
            pltpu.VMEM((QROWS, DIM), F32),
            pltpu.VMEM((8, DIM), F32),
            pltpu.VMEM((QROWS, DIM), BF),
            pltpu.VMEM((N_DEV, META, DIM), BF),
            pltpu.SemaphoreType.DMA((6,)),
            pltpu.SemaphoreType.DMA((3,)),
            pltpu.SemaphoreType.DMA((N_DEV,)),
        ],
        compiler_params=params(4),
        name="request",
    )(query_flat, head_weight, in_hbm(teacher), in_hbm(candidates), in_hbm(storage), in_hbm(lengths))
    recv = exchange(send, "dev")

    embed, inverse = pl.pallas_call(
        encode_kernel,
        out_shape=(pltpu.VMEM((TOKENS, DIM), BF), pltpu.HBM((DIM, DIM), F32)),
        in_specs=[HBM, HBM],
        out_specs=(VMEM, HBM),
        scratch_shapes=[
            pltpu.VMEM((TOKENS, D), BF),
            pltpu.VMEM((D, DIM), BF),
            pltpu.VMEM((DIM, DIM), F32),
            pltpu.SemaphoreType.DMA((PARTS + 1,)),
            pltpu.SemaphoreType.DMA,
        ],
        cost_estimate=estimate(2 * TOKENS * D * DIM, 15_000_000),
        compiler_params=params(20),
        name="encode",
    )(flat_hidden, head_weight)

    expo, recip, sums, table, second, place, queries = pl.pallas_call(
        score_kernel,
        out_shape=(
            pltpu.HBM((N_DEV * QLEN, WIDE), F32),
            pltpu.HBM((N_DEV * QLEN, DIM), F32),
            shape((N_DEV, 8, DIM), F32),
            pltpu.HBM((3, N_DEV, DIM), F32),
            pltpu.HBM((N_DEV, WIDE), F32),
            pltpu.HBM((N_DEV, DIM), jnp.int32),
            pltpu.HBM((N_DEV, QROWS, DIM), BF),
        ),
        in_specs=[VMEM] * 2,
        out_specs=(HBM, HBM, VMEM, HBM, HBM, HBM, HBM),
        scratch_shapes=[
            pltpu.VMEM((N_DEV * QLEN, DIM), F32),
            pltpu.VMEM((3, N_DEV, DIM), F32),
            pltpu.VMEM((N_DEV, WIDE), F32),
            pltpu.VMEM((N_DEV, DIM), jnp.int32),
            pltpu.VMEM((N_DEV, DIM), F32),
            pltpu.VMEM((N_DEV, WIDE), F32),
            pltpu.VMEM((N_DEV * QLEN, WIDE), F32),
            pltpu.VMEM((N_DEV * QLEN, WIDE), BF),
            pltpu.SMEM((N_DEV, DIM), jnp.int32),
            pltpu.SemaphoreType.DMA,
            pltpu.SemaphoreType.DMA((N_DEV // CHUNK,)),
            pltpu.SemaphoreType.DMA((5,)),
        ],
        compiler_params=params(14),
        name="score",
    )(recv, in_vmem(embed))
    all_sums = exchange(sums, "dev")

    weights = pl.pallas_call(
        ahead_kernel,
        out_shape=pltpu.VMEM((N_DEV * QLEN, WIDE), BF),
        in_specs=[HBM, HBM],
        out_specs=VMEM,
        scratch_shapes=[
            pltpu.VMEM((N_DEV * QLEN, DIM), F32),
            pltpu.VMEM((N_DEV * QLEN, WIDE), F32),
            pltpu.SemaphoreType.DMA((N_DEV // GROUP, 2)),
        ],
        cost_estimate=estimate(2 * TOKENS * D * DIM, 15_000_000),
        compiler_params=params(12),
        name="ahead",
    )(in_hbm(expo), in_hbm(recip))

    me = lax.axis_index("dev").astype(jnp.int32).reshape(1)
    send_delta, mixed, loss = pl.pallas_call(
        query_kernel,
        out_shape=(
            pltpu.HBM((N_DEV, QROWS, DIM), BF),
            pltpu.HBM((N_DEV * QLEN, WIDE), BF),
            pltpu.HBM((2, DIM), F32),
        ),
        in_specs=[VMEM, HBM, SMEM, HBM, HBM, VMEM, VMEM, HBM],
        out_specs=(HBM, HBM, HBM),
        scratch_shapes=[
            pltpu.VMEM((8, DIM), F32),
            pltpu.VMEM((3, N_DEV, DIM), F32),
            pltpu.VMEM((N_DEV, WIDE), F32),
            pltpu.VMEM((2, DIM), F32),
            pltpu.VMEM((N_DEV, WIDE), F32),
            pltpu.VMEM((N_DEV, QROWS, DIM), BF),
            pltpu.VMEM((N_DEV * QLEN, WIDE), BF),
            pltpu.SMEM((N_DEV, DIM), jnp.int32),
            pltpu.SemaphoreType.DMA((4,)),
            pltpu.SemaphoreType.DMA((1,)),
            pltpu.SemaphoreType.DMA((N_DEV // CHUNK, 2)),
        ],
        compiler_params=params(12),
        name="query",
    )(all_sums, in_hbm(const), me, in_hbm(table), in_hbm(second), in_vmem(weights), in_vmem(embed), in_hbm(place))
    recv_delta = exchange(send_delta, "dev")

    preact, head = pl.pallas_call(
        stored_kernel,
        out_shape=(pltpu.HBM((TOKENS, DIM), BF), pltpu.VMEM((D, DIM), F32)),
        in_specs=[HBM] * 6 + [VMEM],
        out_specs=(HBM, VMEM),
        scratch_shapes=[
            pltpu.VMEM((TOKENS, DIM), BF),
            pltpu.VMEM((TOKENS, D), BF),
            pltpu.VMEM((N_DEV, QROWS, DIM), BF),
            pltpu.VMEM((N_DEV, WIDE), F32),
            pltpu.VMEM((N_DEV * QLEN, WIDE), BF),
            pltpu.VMEM((DIM, DIM), F32),
            pltpu.VMEM((LANES, TOKENS, DIM), F32),
            pltpu.SMEM((N_DEV, DIM), jnp.int32),
            pltpu.SemaphoreType.DMA((PARTS,)),
            pltpu.SemaphoreType.DMA((4,)),
            pltpu.SemaphoreType.DMA((N_DEV // GROUP,)),
            pltpu.SemaphoreType.DMA((STEPS,)),
        ],
        cost_estimate=estimate(4 * TOKENS * D * DIM, 20_000_000),
        compiler_params=params(40),
        name="stored",
    )(
        in_hbm(place), in_hbm(queries), in_hbm(second), in_hbm(mixed), in_hbm(inverse), flat_hidden, in_vmem(embed)
    )

    query_preact, send_head = pl.pallas_call(
        finish_kernel,
        out_shape=(pltpu.VMEM((QROWS, DIM), BF), shape((N_ALL, 8, DIM), BF)),
        in_specs=[VMEM, HBM, HBM, VMEM],
        out_specs=(VMEM,) * 2,
        scratch_shapes=[
            pltpu.VMEM((QROWS, D), BF),
            pltpu.VMEM((QROWS, DIM), F32),
            pltpu.SemaphoreType.DMA((2,)),
        ],
        compiler_params=params(8),
        name="finish",
    )(recv_delta, query_flat, in_hbm(query_proj), in_vmem(head))
    recv_head = exchange(send_head, ("group", "dev"))

    passage_grad, query_grad = pl.pallas_call(
        back_kernel,
        out_shape=(pltpu.HBM((TOKENS, D), BF), pltpu.HBM((QROWS, D), BF)),
        in_specs=[HBM, HBM, VMEM],
        out_specs=(HBM, HBM),
        scratch_shapes=[
            pltpu.VMEM((TOKENS, DIM), BF),
            pltpu.VMEM((D, DIM), BF),
            pltpu.VMEM((TOKENS, D), BF),
            pltpu.VMEM((QROWS, D), BF),
            pltpu.SemaphoreType.DMA((2,)),
            pltpu.SemaphoreType.DMA((PARTS + 1,)),
        ],
        cost_estimate=estimate(2 * TOKENS * D * DIM, 15_000_000),
        compiler_params=params(20),
        name="back",
    )(in_hbm(preact), head_weight, in_vmem(query_preact))

    send_total = pl.pallas_call(
        reduce_kernel,
        out_shape=shape((N_ALL, 8, DIM), BF),
        in_specs=[VMEM],
        out_specs=VMEM,
        compiler_params=params(4),
        name="reduce",
    )(recv_head)
    head_all = exchange(send_total, ("group", "dev"))
    head_grad = head_all[:HEAD_TILES].reshape(D, DIM).astype(F32)
    return (
        loss[:, 0],
        head_grad,
        query_grad.reshape(2, QLEN, D),
        passage_grad.reshape(STORED, PLEN, D),
    )


def solution(mesh):
    return jax.shard_map(
        on_device,
        mesh=mesh,
        in_specs=(
            P(("group", "dev"), None, None),
            P(("group", "dev"), None, None),
            P(),
            P(("group", "dev"), None),
            P(("group", "dev"), None),
            P("group", None),
            P("group", None),
        ),
        out_specs=(
            P(("group", "dev")),
            P(),
            P(("group", "dev"), None, None),
            P(("group", "dev"), None, None),
        ),
        check_vma=False,
    )
```

```python
import jax
import jax.numpy as jnp
from jax import lax
from jax.experimental import pallas as pl
from jax.experimental.pallas import tpu as pltpu
from jax.sharding import PartitionSpec as P

TAU = 0.0625
LOSS_SCALE = 32768.0
EPS = 1e-06

N_DEV = 32
N_ALL = 128
STORED = 128
PLEN = 48
QLEN = 32
D = 768
DIM = 128
PER_QUERY = 64
CAP = 12
SLOTS = 16
WIDE = CAP * PLEN
QROWS = 2 * QLEN
META = 16
CHUNK = 8
GROUP = 16
TOKENS = STORED * PLEN
BLOCK = 1536
STEPS = TOKENS // BLOCK
LANES = 1
PART = 768
PARTS = TOKENS // PART
AHEAD = 4
TILE = 256
HEAD_TILES = D // 8

BF = jnp.bfloat16
F32 = jnp.float32
ROWS_ROWS = (((0,), (0,)), ((), ()))
COLS_COLS = (((1,), (1,)), ((), ()))
VMEM = pl.BlockSpec(memory_space=pltpu.VMEM)
SMEM = pl.BlockSpec(memory_space=pltpu.SMEM)
HBM = pl.BlockSpec(memory_space=pltpu.HBM)


def params(mib):
    return pltpu.CompilerParams(vmem_limit_bytes=mib * 1024 * 1024)


def dot(a, b, dims=(((1,), (0,)), ((), ()))):
    return lax.dot_general(a, b, dims, preferred_element_type=F32)


def iota(shape, axis):
    return lax.broadcasted_iota(jnp.int32, shape, axis)


def start_copies(pairs, sems):
    copies = [pltpu.make_async_copy(a, b, sems.at[i]) for i, (a, b) in enumerate(pairs)]
    for copy in copies:
        copy.start()
    return copies


def wait_copies(copies):
    for copy in copies:
        copy.wait()


def split3(x):
    hi = x.astype(BF).astype(F32)
    mid = (x - hi).astype(BF).astype(F32)
    return hi, mid, (x - hi - mid)


def expander(copies):
    row = iota((DIM, WIDE), 0)
    slot = (row & (SLOTS - 1)) * PLEN
    lane = iota((DIM, WIDE), 1)
    hit = (lane >= slot) & (lane < slot + PLEN) & (row < copies * SLOTS)
    return jnp.where(hit, 1.0, 0.0)


def request_kernel(hidden_hbm, weight_hbm, teacher_hbm, cand_hbm, storage_hbm, lengths_hbm,
                   send_hbm, proj_hbm, const_hbm,
                   hidden_ref, weight_ref, teacher_ref, cand_ref, storage_ref, lengths_ref,
                   place_ref, length_ref, proj_ref, const_ref, embed_ref, meta_ref, sems, out_sems, send_sems):
    small = start_copies(
        (
            (cand_hbm, cand_ref),
            (storage_hbm, storage_ref),
            (lengths_hbm, lengths_ref),
            (teacher_hbm, teacher_ref),
            (weight_hbm, weight_ref),
            (hidden_hbm, hidden_ref),
        ),
        sems,
    )
    wait_copies(small[:4])
    for i in range(N_DEV):
        place_ref[i : i + 1, :] = storage_ref[0:1, i * STORED : (i + 1) * STORED]
        length_ref[i : i + 1, :] = lengths_ref[0:1, i * STORED : (i + 1) * STORED]
    teacher = teacher_ref[...]
    log_t = teacher - jnp.log(jnp.sum(jnp.exp(teacher), axis=-1, keepdims=True))
    prob = jnp.exp(log_t)
    const = jnp.sum(prob * log_t, axis=-1, keepdims=True)
    const_ref[...] = jnp.concatenate(
        [jnp.broadcast_to(const, (2, DIM)), jnp.zeros((6, DIM), F32)], axis=0
    )
    outs = start_copies(((const_ref, const_hbm),), out_sems)
    prob_row = jnp.concatenate([prob[0:1], prob[1:2]], axis=1)
    cand = cand_ref[...]
    cand_row = jnp.concatenate([cand[0:1], cand[1:2]], axis=1)

    place = place_ref[...]
    owner_table = (place >> 7).astype(F32).astype(BF)
    slot_table = (place & (STORED - 1)).astype(F32).astype(BF)
    length_table = length_ref[...].astype(F32).astype(BF)
    sub32 = iota((N_DEV, DIM), 0)
    sub128 = iota((DIM, DIM), 0)
    lane128 = iota((DIM, DIM), 1)
    high = jnp.where(sub32 == (cand_row >> 7), 1.0, 0.0).astype(BF)
    low = sub128 == (cand_row & (STORED - 1))
    owner = jnp.sum(jnp.where(low, dot(owner_table, high, ROWS_ROWS), 0.0), axis=0, keepdims=True)
    slot = jnp.sum(jnp.where(low, dot(slot_table, high, ROWS_ROWS), 0.0), axis=0, keepdims=True)
    match = jnp.where(sub32 == owner.astype(jnp.int32), 1.0, 0.0)
    match_bf = match.astype(BF)
    at_slot = sub128 == slot.astype(jnp.int32)
    length = jnp.sum(
        jnp.where(at_slot, dot(length_table, match_bf, ROWS_ROWS), 0.0), axis=0, keepdims=True
    )
    earlier = jnp.where(sub128 < lane128, 1.0, 0.0).astype(BF)
    rank = jnp.sum(match * dot(match_bf, earlier), axis=0, keepdims=True).astype(jnp.int32)
    t_hi, t_mid, t_lo = split3(prob_row)
    which = jnp.where(iota((1, DIM), 1) >= PER_QUERY, 1.0, 0.0)
    fields = (slot, which, length, t_hi, t_mid, t_lo, jnp.ones((1, DIM), F32))
    field_of = sub128 >> 4
    values = jnp.zeros((DIM, DIM), F32)
    for f, row in enumerate(fields):
        values = jnp.where(field_of == f, row, values)
    values = jnp.where((sub128 & (SLOTS - 1)) == rank, values, 0.0).astype(BF)
    meta = dot(match_bf, values, COLS_COLS)
    for s in range(N_DEV):
        meta_ref[s] = jnp.broadcast_to(meta[s : s + 1], (META, DIM)).astype(BF)
    outs += start_copies(((meta_ref, send_hbm.at[:, pl.ds(QROWS, META)]),), out_sems.at[pl.ds(2, 1)])
    wait_copies(small[4:])
    proj = dot(hidden_ref[...], weight_ref[...])
    proj_ref[...] = proj
    inverse = lax.rsqrt(jnp.sum(proj * proj, axis=-1, keepdims=True) + EPS)
    embed_ref[...] = (proj * inverse).astype(BF)
    sends = start_copies(
        [(embed_ref, send_hbm.at[s, pl.ds(0, QROWS)]) for s in range(N_DEV)], send_sems
    )
    outs += start_copies(((proj_ref, proj_hbm),), out_sems.at[pl.ds(1, 1)])
    wait_copies(sends)
    wait_copies(outs)


def token_copies(hidden_hbm, hidden_ref, sems):
    copies = []
    for i in range(PARTS):
        rows = pl.ds(i * PART, PART)
        copies.append(pltpu.make_async_copy(hidden_hbm.at[rows], hidden_ref.at[rows], sems.at[i]))
    return copies


def encode_kernel(hidden_hbm, weight_hbm, embed_ref, inverse_hbm, hidden_ref, weight_ref, inverse_ref, sems, out_sem):
    weight_copy = pltpu.make_async_copy(weight_hbm, weight_ref, sems.at[PARTS])
    weight_copy.start()
    copies = token_copies(hidden_hbm, hidden_ref, sems)
    for copy in copies[:AHEAD]:
        copy.start()
    weight_copy.wait()
    packed = jnp.zeros((DIM, DIM), F32)
    lane = iota((DIM, DIM), 1)
    begun = AHEAD
    for i in range(STEPS):
        for copy in copies[i * BLOCK // PART : (i + 1) * BLOCK // PART]:
            copy.wait()
            if begun < PARTS:
                copies[begun].start()
                begun += 1

        def tile(t, carry):
            start = i * BLOCK + t * TILE
            rows = pl.ds(pl.multiple_of(start, TILE), TILE)
            proj = dot(hidden_ref[rows, :], weight_ref[...])
            inverse = lax.rsqrt(jnp.sum(proj * proj, axis=-1, keepdims=True) + EPS)
            embed_ref[rows, :] = (proj * inverse).astype(BF)
            for j in range(TILE // DIM):
                carry = jnp.where(lane == start // DIM + j, inverse[j * DIM : (j + 1) * DIM], carry)
            return carry

        packed = lax.fori_loop(0, BLOCK // TILE, tile, packed, unroll=2)
    inverse_ref[...] = packed
    out = pltpu.make_async_copy(inverse_ref, inverse_hbm, out_sem)
    out.start()
    out.wait()


def stored_rows(embed_ref, place_ref, s):
    parts = []
    for k in range(CAP):
        start = pl.multiple_of(place_ref[s, k], 16)
        parts.append(embed_ref[pl.ds(start, PLEN), :])
    return jnp.concatenate(parts, axis=0)


def score_kernel(recv_ref, embed_ref, expo_hbm, recip_hbm, sums_ref, table_hbm, second_hbm, place_hbm, queries_hbm,
                 recip_ref, table_ref, second_ref, place_ref, meta_ref, limit_ref, expo_ref, round_ref,
                 smem_ref, sem, expo_sems, out_sems):
    outs = start_copies(((recv_ref.at[:, pl.ds(0, QROWS)], queries_hbm),), out_sems.at[pl.ds(4, 1)])
    for s in range(N_DEV):
        rows = recv_ref[s, QROWS : QROWS + META, :].astype(F32)
        meta_ref[s : s + 1, :] = rows[0:1, :]
    meta = meta_ref[...]
    place_ref[...] = meta.astype(jnp.int32) * PLEN
    copy = pltpu.make_async_copy(place_ref, smem_ref, sem)
    copy.start()
    outs += start_copies(((place_ref, place_hbm),), out_sems)
    meta_bf = meta.astype(BF)
    spread = expander(1)
    second_ref[...] = dot(pltpu.roll(meta, DIM - SLOTS, 1).astype(BF), spread.astype(BF))
    length = dot(pltpu.roll(meta, DIM - 2 * SLOTS, 1).astype(BF), spread.astype(BF))
    lane = iota((1, WIDE), 1)
    token = lane
    for k in range(1, CAP):
        token = token - jnp.where(lane >= k * PLEN, PLEN, 0)
    limit_ref[...] = jnp.where(token.astype(F32) < length, 1.0, 0.0)
    outs += start_copies(((second_ref, second_hbm),), out_sems.at[pl.ds(1, 1)])
    copy.wait()

    def expo_copy(i):
        rows = pl.ds(i * (CHUNK * QLEN), CHUNK * QLEN)
        return pltpu.make_async_copy(expo_ref.at[rows], expo_hbm.at[rows], expo_sems.at[i])

    def chunk(i, carry):
        for u in range(CHUNK):
            s = i * CHUNK + u
            queries = recv_ref[s, 0:QROWS, :]
            sims = dot(queries, stored_rows(embed_ref, smem_ref, s), COLS_COLS)
            second = second_ref[pl.ds(s, 1), :]
            valid = limit_ref[pl.ds(s, 1), :]
            mine = jnp.where(second > 0.5, sims[QLEN:QROWS], sims[0:QLEN])
            expo = jnp.where(valid > 0.5, jnp.exp(mine * (1.0 / TAU)), 0.0)
            rows = pl.ds(pl.multiple_of(s * QLEN, QLEN), QLEN)
            expo_ref[rows, :] = expo
            round_ref[rows, :] = expo.astype(BF)
        expo_copy(i).start()
        return carry

    for i in range(N_DEV // CHUNK):
        chunk(i, 0)
    total = dot(round_ref[...], spread.astype(BF), COLS_COLS)
    total = jnp.where(total > 0.0, total, 1.0)
    recip_ref[...] = 1.0 / total
    outs += start_copies(((recip_ref, recip_hbm),), out_sems.at[pl.ds(2, 1)])
    scores = TAU * jnp.sum(jnp.log(total).reshape(N_DEV, QLEN, DIM), axis=1)
    lane = iota((N_DEV, DIM), 1)
    present = (pltpu.roll(meta, DIM - 6 * SLOTS, 1) > 0.5) & (lane < SLOTS)
    teach = (
        pltpu.roll(meta, DIM - 3 * SLOTS, 1)
        + pltpu.roll(meta, DIM - 4 * SLOTS, 1)
        + pltpu.roll(meta, DIM - 5 * SLOTS, 1)
    )
    teach = jnp.where(present, teach, 0.0)
    student = jnp.where(present, jnp.exp(scores), 0.0)
    which = pltpu.roll(meta, DIM - SLOTS, 1) > 0.5
    table_ref[0] = student
    table_ref[1] = teach
    table_ref[2] = jnp.where(which, 1.0, 0.0)
    outs += start_copies(((table_ref, table_hbm),), out_sems.at[pl.ds(3, 1)])
    gain = teach * scores
    columns = []
    for value in (student, gain):
        columns.append(jnp.sum(jnp.where(which, 0.0, value), axis=-1, keepdims=True))
        columns.append(jnp.sum(jnp.where(which, value, 0.0), axis=-1, keepdims=True))
    mixed = jnp.zeros((N_DEV, DIM), F32)
    for j, column in enumerate(columns):
        mixed = jnp.where(lane == j, column, mixed)
    mixed = jnp.concatenate([mixed, jnp.zeros((DIM - N_DEV, DIM), F32)], axis=0)
    part = jnp.transpose(mixed)[0:8, :]
    for s in range(N_DEV):
        sums_ref[s] = part
    wait_copies(outs)
    wait_copies([expo_copy(i) for i in range(N_DEV // CHUNK)])


def halves(one, second):
    return jnp.concatenate(
        [jnp.where(second, 0.0, one).astype(BF), jnp.where(second, one, 0.0).astype(BF)], axis=0
    )


def ahead_kernel(expo_hbm, recip_hbm, table_hbm, second_hbm, weights_ref, table_ref, second_ref,
                 recip_ref, expo_ref, sems, small_sems):
    steps = N_DEV // GROUP
    span = GROUP * QLEN
    fetch = []
    for i in range(steps):
        rows = pl.ds(i * span, span)
        fetch.append(
            start_copies(
                ((recip_hbm.at[rows], recip_ref.at[rows]), (expo_hbm.at[rows], expo_ref.at[rows])), sems.at[i]
            )
        )
    small = start_copies(((table_hbm, table_ref), (second_hbm, second_ref)), small_sems)
    spread = expander(2).astype(BF)
    lane = iota((span, DIM), 1)
    for i in range(steps):
        rows = pl.ds(i * span, span)
        wait_copies(fetch[i])
        recip = recip_ref[rows, :]
        hi = recip.astype(BF).astype(F32)
        lo = recip - hi
        factor = jnp.where(lane < SLOTS, hi, jnp.where(lane < 2 * SLOTS, pltpu.roll(lo, SLOTS, 1), 0.0))
        weights_ref[rows, :] = (expo_ref[rows, :] * dot(factor.astype(BF), spread)).astype(BF)
    wait_copies(small)


def query_kernel(sums_ref, const_hbm, me_ref, table_ref, second_ref, weights_ref, embed_ref, place_hbm,
                 send_hbm, mixed_hbm, loss_hbm,
                 const_ref, loss_ref, wide_ref, send_ref, mixed_ref, smem_ref,
                 sems, out_sems, part_sems):
    small = start_copies(
        ((place_hbm, smem_ref), (const_hbm, const_ref)), sems
    )
    sums = jnp.sum(sums_ref[...], axis=0)
    log_sum = jnp.log(jnp.where(sums > 0.0, sums, 1.0))
    turned = jnp.transpose(jnp.concatenate([sums, jnp.zeros((DIM - 8, DIM), F32)], axis=0))[0:N_DEV, :]
    normal = jnp.where(table_ref[2] > 0.5, turned[:, 1:2], turned[:, 0:1])
    pull = LOSS_SCALE * (table_ref[0] / normal - table_ref[1])
    hi = pull.astype(BF).astype(F32)
    lo = pull - hi
    lane = iota((N_DEV, DIM), 1)
    factor = jnp.where(lane < SLOTS, hi, jnp.where(lane < 2 * SLOTS, pltpu.roll(lo, SLOTS, 1), 0.0))
    wide_ref[...] = dot(factor.astype(BF), expander(2).astype(BF))
    wait_copies(small)
    loss = const_ref[0:2, :] + log_sum[0:2, :] - sums[2:4, :]
    picked = jnp.where(iota((2, DIM), 1) == me_ref[0], loss, 0.0)
    loss_ref[...] = jnp.broadcast_to(jnp.sum(picked, axis=-1, keepdims=True), (2, DIM))
    outs = start_copies(((loss_ref, loss_hbm),), out_sems)

    def part_copies(i):
        some = pl.ds(i * CHUNK, CHUNK)
        rows = pl.ds(i * (CHUNK * QLEN), CHUNK * QLEN)
        return [
            pltpu.make_async_copy(send_ref.at[some], send_hbm.at[some], part_sems.at[i, 0]),
            pltpu.make_async_copy(mixed_ref.at[rows], mixed_hbm.at[rows], part_sems.at[i, 1]),
        ]

    def chunk(i, carry):
        for u in range(CHUNK):
            s = i * CHUNK + u
            rows = pl.ds(pl.multiple_of(s * QLEN, QLEN), QLEN)
            mixed = weights_ref[rows, :].astype(F32) * wide_ref[pl.ds(s, 1), :]
            mixed_ref[rows, :] = mixed.astype(BF)
            both = halves(mixed, second_ref[pl.ds(s, 1), :] > 0.5)
            send_ref[s] = dot(both, stored_rows(embed_ref, smem_ref, s)).astype(BF)
        for copy in part_copies(i):
            copy.start()
        return carry

    for i in range(N_DEV // CHUNK):
        chunk(i, 0)
    wait_copies(outs)
    for i in range(N_DEV // CHUNK):
        wait_copies(part_copies(i))


def stored_kernel(place_hbm, queries_hbm, second_hbm, mixed_hbm, inverse_hbm, hidden_hbm, embed_ref,
                  preact_hbm, head_ref,
                  preact_ref, hidden_ref, queries_ref, second_ref, mixed_ref, inverse_ref, delta_ref, place_smem,
                  sems, small_sems, mixed_sems, out_sems):
    steps = N_DEV // GROUP
    small = start_copies(
        ((place_hbm, place_smem), (second_hbm, second_ref), (queries_hbm, queries_ref), (inverse_hbm, inverse_ref)),
        small_sems,
    )
    fetch = []
    for i in range(steps):
        rows = pl.ds(i * GROUP * QLEN, GROUP * QLEN)
        fetch += start_copies(((mixed_hbm.at[rows], mixed_ref.at[rows]),), mixed_sems.at[pl.ds(i, 1)])
    copies = token_copies(hidden_hbm, hidden_ref, sems)
    delta_ref[...] = jnp.zeros_like(delta_ref)
    wait_copies(small)

    for i in range(steps):
        fetch[i].wait()
        for copy in copies[i * PARTS // steps : (i + 1) * PARTS // steps]:
            copy.start()
        for s in range(i * GROUP, (i + 1) * GROUP):
            both = halves(mixed_ref[s * QLEN : (s + 1) * QLEN, :].astype(F32), second_ref[s : s + 1, :] > 0.5)
            part = dot(both, queries_ref[s], ROWS_ROWS)
            for k in range(CAP):
                at = pl.ds(pl.multiple_of(place_smem[s, k], 16), PLEN)
                delta_ref[k % LANES, at, :] += part[k * PLEN : (k + 1) * PLEN]
    total = jnp.zeros((DIM, D), F32)
    outs = []
    for i in range(STEPS):
        rows = pl.ds(i * BLOCK, BLOCK)
        unit = embed_ref[rows, :].astype(F32)
        delta = jnp.sum(delta_ref[:, rows, :], axis=0)
        radial = jnp.sum(unit * delta, axis=-1, keepdims=True)
        tangent = delta - unit * radial
        scaled = []
        for j in range(BLOCK // DIM):
            b = i * (BLOCK // DIM) + j
            scaled.append(tangent[j * DIM : (j + 1) * DIM] * inverse_ref[:, b : b + 1])
        preact = jnp.concatenate(scaled, axis=0).astype(BF)
        preact_ref[rows, :] = preact
        outs += start_copies(((preact_ref.at[rows], preact_hbm.at[rows]),), out_sems.at[pl.ds(i, 1)])
        for j in range(i * BLOCK // PART, (i + 1) * BLOCK // PART):
            copies[j].wait()
        total = total + dot(preact, hidden_ref[rows, :], ROWS_ROWS)
    head_ref[...] = jnp.transpose(total)
    wait_copies(outs)


def back_kernel(preact_hbm, weight_hbm, query_ref, grad_hbm, query_grad_hbm,
                preact_ref, weight_ref, grad_ref, query_grad_ref, sems, out_sems):
    copies = start_copies(((weight_hbm, weight_ref), (preact_hbm, preact_ref)), sems)
    wait_copies(copies)
    outs = []
    for i in range(PARTS):

        def tile(t, carry):
            rows = pl.ds(pl.multiple_of(i * PART + t * TILE, TILE), TILE)
            grad_ref[rows, :] = dot(preact_ref[rows, :], weight_ref[...], COLS_COLS).astype(BF)
            return carry

        lax.fori_loop(0, PART // TILE, tile, 0, unroll=2)
        rows = pl.ds(i * PART, PART)
        outs += start_copies(((grad_ref.at[rows], grad_hbm.at[rows]),), out_sems.at[pl.ds(i, 1)])
    query_grad_ref[...] = dot(query_ref[...], weight_ref[...], COLS_COLS).astype(BF)
    outs += start_copies(((query_grad_ref, query_grad_hbm),), out_sems.at[pl.ds(PARTS, 1)])
    wait_copies(outs)


def finish_kernel(recv_ref, hidden_hbm, proj_hbm, head_ref, preact_ref, send_ref,
                  hidden_ref, proj_ref, sems):
    copies = start_copies(((proj_hbm, proj_ref), (hidden_hbm, hidden_ref)), sems)
    delta = jnp.sum(recv_ref[...].astype(F32), axis=0)
    copies[0].wait()
    proj = proj_ref[...]
    inverse = lax.rsqrt(jnp.sum(proj * proj, axis=-1, keepdims=True) + EPS)
    unit = proj * inverse
    radial = jnp.sum(unit * delta, axis=-1, keepdims=True)
    preact = ((delta - unit * radial) * inverse).astype(BF)
    preact_ref[...] = preact
    wait_copies(copies[1:])
    head = head_ref[...] + dot(hidden_ref[...], preact, ROWS_ROWS)
    send_ref[0:HEAD_TILES] = head.reshape(HEAD_TILES, 8, DIM).astype(BF)
    send_ref[HEAD_TILES:N_ALL] = jnp.zeros((N_ALL - HEAD_TILES, 8, DIM), BF)


def reduce_kernel(recv_ref, send_ref):
    total = jnp.sum(recv_ref[...].astype(F32), axis=0).astype(BF)
    send_ref[...] = jnp.broadcast_to(total[None], (N_ALL, 8, DIM))


def shape(dims, kind):
    return jax.ShapeDtypeStruct(dims, kind)


def in_hbm(x):
    return pltpu.with_memory_space_constraint(x, pltpu.HBM)


def in_vmem(x):
    return pltpu.with_memory_space_constraint(x, pltpu.VMEM)


def exchange(x, axes):
    return lax.all_to_all(x, axes, split_axis=0, concat_axis=0, tiled=True)


def estimate(flops, size):
    return pl.CostEstimate(flops=flops, bytes_accessed=size, transcendentals=0)


def on_device(query_hidden, passage_hidden, head_weight, teacher, candidates, storage, lengths):
    query_flat = in_hbm(query_hidden.reshape(QROWS, D))
    flat_hidden = in_hbm(passage_hidden.reshape(TOKENS, D))
    head_weight = in_hbm(head_weight)
    send, query_proj, const = pl.pallas_call(
        request_kernel,
        out_shape=(
            pltpu.HBM((N_DEV, QROWS + META, DIM), BF),
            pltpu.HBM((QROWS, DIM), F32),
            pltpu.HBM((8, DIM), F32),
        ),
        in_specs=[HBM] * 6,
        out_specs=(HBM, HBM, HBM),
        scratch_shapes=[
            pltpu.VMEM((QROWS, D), BF),
            pltpu.VMEM((D, DIM), BF),
            pltpu.VMEM((2, PER_QUERY), F32),
            pltpu.VMEM((2, PER_QUERY), jnp.int32),
            pltpu.VMEM((1, N_DEV * STORED), jnp.int32),
            pltpu.VMEM((1, N_DEV * STORED), jnp.int32),
            pltpu.VMEM((N_DEV, DIM), jnp.int32),
            pltpu.VMEM((N_DEV, DIM), jnp.int32),
            pltpu.VMEM((QROWS, DIM), F32),
            pltpu.VMEM((8, DIM), F32),
            pltpu.VMEM((QROWS, DIM), BF),
            pltpu.VMEM((N_DEV, META, DIM), BF),
            pltpu.SemaphoreType.DMA((6,)),
            pltpu.SemaphoreType.DMA((3,)),
            pltpu.SemaphoreType.DMA((N_DEV,)),
        ],
        compiler_params=params(4),
        name="request",
    )(query_flat, head_weight, in_hbm(teacher), in_hbm(candidates), in_hbm(storage), in_hbm(lengths))
    recv = exchange(send, "dev")

    embed, inverse = pl.pallas_call(
        encode_kernel,
        out_shape=(pltpu.VMEM((TOKENS, DIM), BF), pltpu.HBM((DIM, DIM), F32)),
        in_specs=[HBM, HBM],
        out_specs=(VMEM, HBM),
        scratch_shapes=[
            pltpu.VMEM((TOKENS, D), BF),
            pltpu.VMEM((D, DIM), BF),
            pltpu.VMEM((DIM, DIM), F32),
            pltpu.SemaphoreType.DMA((PARTS + 1,)),
            pltpu.SemaphoreType.DMA,
        ],
        cost_estimate=estimate(2 * TOKENS * D * DIM, 15_000_000),
        compiler_params=params(20),
        name="encode",
    )(flat_hidden, head_weight)

    expo, recip, sums, table, second, place, queries = pl.pallas_call(
        score_kernel,
        out_shape=(
            pltpu.HBM((N_DEV * QLEN, WIDE), F32),
            pltpu.HBM((N_DEV * QLEN, DIM), F32),
            shape((N_DEV, 8, DIM), F32),
            pltpu.HBM((3, N_DEV, DIM), F32),
            pltpu.HBM((N_DEV, WIDE), F32),
            pltpu.HBM((N_DEV, DIM), jnp.int32),
            pltpu.HBM((N_DEV, QROWS, DIM), BF),
        ),
        in_specs=[VMEM] * 2,
        out_specs=(HBM, HBM, VMEM, HBM, HBM, HBM, HBM),
        scratch_shapes=[
            pltpu.VMEM((N_DEV * QLEN, DIM), F32),
            pltpu.VMEM((3, N_DEV, DIM), F32),
            pltpu.VMEM((N_DEV, WIDE), F32),
            pltpu.VMEM((N_DEV, DIM), jnp.int32),
            pltpu.VMEM((N_DEV, DIM), F32),
            pltpu.VMEM((N_DEV, WIDE), F32),
            pltpu.VMEM((N_DEV * QLEN, WIDE), F32),
            pltpu.VMEM((N_DEV * QLEN, WIDE), BF),
            pltpu.SMEM((N_DEV, DIM), jnp.int32),
            pltpu.SemaphoreType.DMA,
            pltpu.SemaphoreType.DMA((N_DEV // CHUNK,)),
            pltpu.SemaphoreType.DMA((5,)),
        ],
        compiler_params=params(14),
        name="score",
    )(recv, in_vmem(embed))
    all_sums = exchange(sums, "dev")

    weights, near_table, near_second = pl.pallas_call(
        ahead_kernel,
        out_shape=(
            pltpu.VMEM((N_DEV * QLEN, WIDE), BF),
            pltpu.VMEM((3, N_DEV, DIM), F32),
            pltpu.VMEM((N_DEV, WIDE), F32),
        ),
        in_specs=[HBM] * 4,
        out_specs=(VMEM,) * 3,
        scratch_shapes=[
            pltpu.VMEM((N_DEV * QLEN, DIM), F32),
            pltpu.VMEM((N_DEV * QLEN, WIDE), F32),
            pltpu.SemaphoreType.DMA((N_DEV // GROUP, 2)),
            pltpu.SemaphoreType.DMA((2,)),
        ],
        cost_estimate=estimate(2 * TOKENS * D * DIM, 15_000_000),
        compiler_params=params(12),
        name="ahead",
    )(in_hbm(expo), in_hbm(recip), in_hbm(table), in_hbm(second))

    me = lax.axis_index("dev").astype(jnp.int32).reshape(1)
    send_delta, mixed, loss = pl.pallas_call(
        query_kernel,
        out_shape=(
            pltpu.HBM((N_DEV, QROWS, DIM), BF),
            pltpu.HBM((N_DEV * QLEN, WIDE), BF),
            pltpu.HBM((2, DIM), F32),
        ),
        in_specs=[VMEM, HBM, SMEM, VMEM, VMEM, VMEM, VMEM, HBM],
        out_specs=(HBM, HBM, HBM),
        scratch_shapes=[
            pltpu.VMEM((8, DIM), F32),
            pltpu.VMEM((2, DIM), F32),
            pltpu.VMEM((N_DEV, WIDE), F32),
            pltpu.VMEM((N_DEV, QROWS, DIM), BF),
            pltpu.VMEM((N_DEV * QLEN, WIDE), BF),
            pltpu.SMEM((N_DEV, DIM), jnp.int32),
            pltpu.SemaphoreType.DMA((2,)),
            pltpu.SemaphoreType.DMA((1,)),
            pltpu.SemaphoreType.DMA((N_DEV // CHUNK, 2)),
        ],
        compiler_params=params(12),
        name="query",
    )(all_sums, in_hbm(const), me, in_vmem(near_table), in_vmem(near_second), in_vmem(weights), in_vmem(embed), in_hbm(place))
    recv_delta = exchange(send_delta, "dev")

    preact, head = pl.pallas_call(
        stored_kernel,
        out_shape=(pltpu.HBM((TOKENS, DIM), BF), pltpu.VMEM((D, DIM), F32)),
        in_specs=[HBM] * 6 + [VMEM],
        out_specs=(HBM, VMEM),
        scratch_shapes=[
            pltpu.VMEM((TOKENS, DIM), BF),
            pltpu.VMEM((TOKENS, D), BF),
            pltpu.VMEM((N_DEV, QROWS, DIM), BF),
            pltpu.VMEM((N_DEV, WIDE), F32),
            pltpu.VMEM((N_DEV * QLEN, WIDE), BF),
            pltpu.VMEM((DIM, DIM), F32),
            pltpu.VMEM((LANES, TOKENS, DIM), F32),
            pltpu.SMEM((N_DEV, DIM), jnp.int32),
            pltpu.SemaphoreType.DMA((PARTS,)),
            pltpu.SemaphoreType.DMA((4,)),
            pltpu.SemaphoreType.DMA((N_DEV // GROUP,)),
            pltpu.SemaphoreType.DMA((STEPS,)),
        ],
        cost_estimate=estimate(4 * TOKENS * D * DIM, 20_000_000),
        compiler_params=params(40),
        name="stored",
    )(
        in_hbm(place), in_hbm(queries), in_hbm(second), in_hbm(mixed), in_hbm(inverse), flat_hidden, in_vmem(embed)
    )

    query_preact, send_head = pl.pallas_call(
        finish_kernel,
        out_shape=(pltpu.VMEM((QROWS, DIM), BF), shape((N_ALL, 8, DIM), BF)),
        in_specs=[VMEM, HBM, HBM, VMEM],
        out_specs=(VMEM,) * 2,
        scratch_shapes=[
            pltpu.VMEM((QROWS, D), BF),
            pltpu.VMEM((QROWS, DIM), F32),
            pltpu.SemaphoreType.DMA((2,)),
        ],
        compiler_params=params(8),
        name="finish",
    )(recv_delta, query_flat, in_hbm(query_proj), in_vmem(head))
    recv_head = exchange(send_head, ("group", "dev"))

    passage_grad, query_grad = pl.pallas_call(
        back_kernel,
        out_shape=(pltpu.HBM((TOKENS, D), BF), pltpu.HBM((QROWS, D), BF)),
        in_specs=[HBM, HBM, VMEM],
        out_specs=(HBM, HBM),
        scratch_shapes=[
            pltpu.VMEM((TOKENS, DIM), BF),
            pltpu.VMEM((D, DIM), BF),
            pltpu.VMEM((TOKENS, D), BF),
            pltpu.VMEM((QROWS, D), BF),
            pltpu.SemaphoreType.DMA((2,)),
            pltpu.SemaphoreType.DMA((PARTS + 1,)),
        ],
        cost_estimate=estimate(2 * TOKENS * D * DIM, 15_000_000),
        compiler_params=params(20),
        name="back",
    )(in_hbm(preact), head_weight, in_vmem(query_preact))

    send_total = pl.pallas_call(
        reduce_kernel,
        out_shape=shape((N_ALL, 8, DIM), BF),
        in_specs=[VMEM],
        out_specs=VMEM,
        compiler_params=params(4),
        name="reduce",
    )(recv_head)
    head_all = exchange(send_total, ("group", "dev"))
    head_grad = head_all[:HEAD_TILES].reshape(D, DIM).astype(F32)
    return (
        loss[:, 0],
        head_grad,
        query_grad.reshape(2, QLEN, D),
        passage_grad.reshape(STORED, PLEN, D),
    )


def solution(mesh):
    return jax.shard_map(
        on_device,
        mesh=mesh,
        in_specs=(
            P(("group", "dev"), None, None),
            P(("group", "dev"), None, None),
            P(),
            P(("group", "dev"), None),
            P(("group", "dev"), None),
            P("group", None),
            P("group", None),
        ),
        out_specs=(
            P(("group", "dev")),
            P(),
            P(("group", "dev"), None, None),
            P(("group", "dev"), None, None),
        ),
        check_vma=False,
    )
```

```python
import jax
import jax.numpy as jnp
from jax import lax
from jax.experimental import pallas as pl
from jax.experimental.pallas import tpu as pltpu
from jax.sharding import PartitionSpec as P

TAU = 0.0625
LOSS_SCALE = 32768.0
EPS = 1e-06

N_DEV = 32
N_ALL = 128
STORED = 128
PLEN = 48
QLEN = 32
D = 768
DIM = 128
PER_QUERY = 64
CAP = 12
SLOTS = 16
WIDE = CAP * PLEN
QROWS = 2 * QLEN
META = 16
CHUNK = 8
GROUP = 16
TOKENS = STORED * PLEN
BLOCK = 1536
STEPS = TOKENS // BLOCK
LANES = 1
PART = 768
PARTS = TOKENS // PART
AHEAD = 4
TILE = 256
HEAD_TILES = D // 8

BF = jnp.bfloat16
F32 = jnp.float32
ROWS_ROWS = (((0,), (0,)), ((), ()))
COLS_COLS = (((1,), (1,)), ((), ()))
VMEM = pl.BlockSpec(memory_space=pltpu.VMEM)
SMEM = pl.BlockSpec(memory_space=pltpu.SMEM)
HBM = pl.BlockSpec(memory_space=pltpu.HBM)


def params(mib):
    return pltpu.CompilerParams(vmem_limit_bytes=mib * 1024 * 1024)


def dot(a, b, dims=(((1,), (0,)), ((), ()))):
    return lax.dot_general(a, b, dims, preferred_element_type=F32)


def iota(shape, axis):
    return lax.broadcasted_iota(jnp.int32, shape, axis)


def start_copies(pairs, sems):
    copies = [pltpu.make_async_copy(a, b, sems.at[i]) for i, (a, b) in enumerate(pairs)]
    for copy in copies:
        copy.start()
    return copies


def wait_copies(copies):
    for copy in copies:
        copy.wait()


def split3(x):
    hi = x.astype(BF).astype(F32)
    mid = (x - hi).astype(BF).astype(F32)
    return hi, mid, (x - hi - mid)


def expander(copies):
    row = iota((DIM, WIDE), 0)
    slot = (row & (SLOTS - 1)) * PLEN
    lane = iota((DIM, WIDE), 1)
    hit = (lane >= slot) & (lane < slot + PLEN) & (row < copies * SLOTS)
    return jnp.where(hit, 1.0, 0.0)


def request_kernel(hidden_hbm, weight_hbm, teacher_hbm, cand_hbm, storage_hbm, lengths_hbm,
                   send_hbm, proj_hbm, const_hbm,
                   hidden_ref, weight_ref, teacher_ref, cand_ref, storage_ref, lengths_ref,
                   place_ref, length_ref, proj_ref, const_ref, embed_ref, meta_ref, sems, out_sems, send_sems):
    small = start_copies(
        (
            (cand_hbm, cand_ref),
            (storage_hbm, storage_ref),
            (lengths_hbm, lengths_ref),
            (teacher_hbm, teacher_ref),
            (weight_hbm, weight_ref),
            (hidden_hbm, hidden_ref),
        ),
        sems,
    )
    wait_copies(small[:4])
    for i in range(N_DEV):
        place_ref[i : i + 1, :] = storage_ref[0:1, i * STORED : (i + 1) * STORED]
        length_ref[i : i + 1, :] = lengths_ref[0:1, i * STORED : (i + 1) * STORED]
    teacher = teacher_ref[...]
    log_t = teacher - jnp.log(jnp.sum(jnp.exp(teacher), axis=-1, keepdims=True))
    prob = jnp.exp(log_t)
    const = jnp.sum(prob * log_t, axis=-1, keepdims=True)
    const_ref[...] = jnp.concatenate(
        [jnp.broadcast_to(const, (2, DIM)), jnp.zeros((6, DIM), F32)], axis=0
    )
    outs = start_copies(((const_ref, const_hbm),), out_sems)
    prob_row = jnp.concatenate([prob[0:1], prob[1:2]], axis=1)
    cand = cand_ref[...]
    cand_row = jnp.concatenate([cand[0:1], cand[1:2]], axis=1)

    place = place_ref[...]
    owner_table = (place >> 7).astype(F32).astype(BF)
    slot_table = (place & (STORED - 1)).astype(F32).astype(BF)
    length_table = length_ref[...].astype(F32).astype(BF)
    sub32 = iota((N_DEV, DIM), 0)
    sub128 = iota((DIM, DIM), 0)
    lane128 = iota((DIM, DIM), 1)
    high = jnp.where(sub32 == (cand_row >> 7), 1.0, 0.0).astype(BF)
    low = sub128 == (cand_row & (STORED - 1))
    owner = jnp.sum(jnp.where(low, dot(owner_table, high, ROWS_ROWS), 0.0), axis=0, keepdims=True)
    slot = jnp.sum(jnp.where(low, dot(slot_table, high, ROWS_ROWS), 0.0), axis=0, keepdims=True)
    match = jnp.where(sub32 == owner.astype(jnp.int32), 1.0, 0.0)
    match_bf = match.astype(BF)
    at_slot = sub128 == slot.astype(jnp.int32)
    length = jnp.sum(
        jnp.where(at_slot, dot(length_table, match_bf, ROWS_ROWS), 0.0), axis=0, keepdims=True
    )
    earlier = jnp.where(sub128 < lane128, 1.0, 0.0).astype(BF)
    rank = jnp.sum(match * dot(match_bf, earlier), axis=0, keepdims=True).astype(jnp.int32)
    t_hi, t_mid, t_lo = split3(prob_row)
    which = jnp.where(iota((1, DIM), 1) >= PER_QUERY, 1.0, 0.0)
    fields = (slot, which, length, t_hi, t_mid, t_lo, jnp.ones((1, DIM), F32))
    field_of = sub128 >> 4
    values = jnp.zeros((DIM, DIM), F32)
    for f, row in enumerate(fields):
        values = jnp.where(field_of == f, row, values)
    values = jnp.where((sub128 & (SLOTS - 1)) == rank, values, 0.0).astype(BF)
    meta = dot(match_bf, values, COLS_COLS)
    for s in range(N_DEV):
        meta_ref[s] = jnp.broadcast_to(meta[s : s + 1], (META, DIM)).astype(BF)
    outs += start_copies(((meta_ref, send_hbm.at[:, pl.ds(QROWS, META)]),), out_sems.at[pl.ds(2, 1)])
    wait_copies(small[4:])
    proj = dot(hidden_ref[...], weight_ref[...])
    proj_ref[...] = proj
    inverse = lax.rsqrt(jnp.sum(proj * proj, axis=-1, keepdims=True) + EPS)
    embed_ref[...] = (proj * inverse).astype(BF)
    sends = start_copies(
        [(embed_ref, send_hbm.at[s, pl.ds(0, QROWS)]) for s in range(N_DEV)], send_sems
    )
    outs += start_copies(((proj_ref, proj_hbm),), out_sems.at[pl.ds(1, 1)])
    wait_copies(sends)
    wait_copies(outs)


def token_copies(hidden_hbm, hidden_ref, sems):
    copies = []
    for i in range(PARTS):
        rows = pl.ds(i * PART, PART)
        copies.append(pltpu.make_async_copy(hidden_hbm.at[rows], hidden_ref.at[rows], sems.at[i]))
    return copies


def encode_kernel(hidden_hbm, weight_hbm, embed_ref, inverse_hbm, hidden_ref, weight_ref, inverse_ref, sems, out_sem):
    weight_copy = pltpu.make_async_copy(weight_hbm, weight_ref, sems.at[PARTS])
    weight_copy.start()
    copies = token_copies(hidden_hbm, hidden_ref, sems)
    for copy in copies[:AHEAD]:
        copy.start()
    weight_copy.wait()
    packed = jnp.zeros((DIM, DIM), F32)
    lane = iota((DIM, DIM), 1)
    begun = AHEAD
    for i in range(STEPS):
        for copy in copies[i * BLOCK // PART : (i + 1) * BLOCK // PART]:
            copy.wait()
            if begun < PARTS:
                copies[begun].start()
                begun += 1

        def tile(t, carry):
            start = i * BLOCK + t * TILE
            rows = pl.ds(pl.multiple_of(start, TILE), TILE)
            proj = dot(hidden_ref[rows, :], weight_ref[...])
            inverse = lax.rsqrt(jnp.sum(proj * proj, axis=-1, keepdims=True) + EPS)
            embed_ref[rows, :] = (proj * inverse).astype(BF)
            for j in range(TILE // DIM):
                carry = jnp.where(lane == start // DIM + j, inverse[j * DIM : (j + 1) * DIM], carry)
            return carry

        packed = lax.fori_loop(0, BLOCK // TILE, tile, packed, unroll=2)
    inverse_ref[...] = packed
    out = pltpu.make_async_copy(inverse_ref, inverse_hbm, out_sem)
    out.start()
    out.wait()


def stored_rows(embed_ref, place_ref, s):
    parts = []
    for k in range(CAP):
        start = pl.multiple_of(place_ref[s, k], 16)
        parts.append(embed_ref[pl.ds(start, PLEN), :])
    return jnp.concatenate(parts, axis=0)


def score_kernel(recv_ref, embed_ref, expo_hbm, recip_hbm, sums_ref, table_hbm, second_hbm, place_hbm, queries_hbm,
                 recip_ref, table_ref, second_ref, place_ref, meta_ref, limit_ref, expo_ref, round_ref,
                 smem_ref, sem, expo_sems, out_sems):
    outs = start_copies(((recv_ref.at[:, pl.ds(0, QROWS)], queries_hbm),), out_sems.at[pl.ds(4, 1)])
    for s in range(N_DEV):
        rows = recv_ref[s, QROWS : QROWS + META, :].astype(F32)
        meta_ref[s : s + 1, :] = rows[0:1, :]
    meta = meta_ref[...]
    place_ref[...] = meta.astype(jnp.int32) * PLEN
    copy = pltpu.make_async_copy(place_ref, smem_ref, sem)
    copy.start()
    outs += start_copies(((place_ref, place_hbm),), out_sems)
    meta_bf = meta.astype(BF)
    spread = expander(1)
    second_ref[...] = dot(pltpu.roll(meta, DIM - SLOTS, 1).astype(BF), spread.astype(BF))
    length = dot(pltpu.roll(meta, DIM - 2 * SLOTS, 1).astype(BF), spread.astype(BF))
    lane = iota((1, WIDE), 1)
    token = lane
    for k in range(1, CAP):
        token = token - jnp.where(lane >= k * PLEN, PLEN, 0)
    limit_ref[...] = jnp.where(token.astype(F32) < length, 1.0, 0.0)
    outs += start_copies(((second_ref, second_hbm),), out_sems.at[pl.ds(1, 1)])
    copy.wait()

    def expo_copy(i):
        rows = pl.ds(i * (CHUNK * QLEN), CHUNK * QLEN)
        return pltpu.make_async_copy(expo_ref.at[rows], expo_hbm.at[rows], expo_sems.at[i])

    def chunk(i, carry):
        for u in range(CHUNK):
            s = i * CHUNK + u
            queries = recv_ref[s, 0:QROWS, :]
            sims = dot(queries, stored_rows(embed_ref, smem_ref, s), COLS_COLS)
            second = second_ref[pl.ds(s, 1), :]
            valid = limit_ref[pl.ds(s, 1), :]
            mine = jnp.where(second > 0.5, sims[QLEN:QROWS], sims[0:QLEN])
            expo = jnp.where(valid > 0.5, jnp.exp(mine * (1.0 / TAU)), 0.0)
            rows = pl.ds(pl.multiple_of(s * QLEN, QLEN), QLEN)
            expo_ref[rows, :] = expo
            round_ref[rows, :] = expo.astype(BF)
        expo_copy(i).start()
        return carry

    for i in range(N_DEV // CHUNK):
        chunk(i, 0)
    total = dot(round_ref[...], spread.astype(BF), COLS_COLS)
    total = jnp.where(total > 0.0, total, 1.0)
    recip_ref[...] = 1.0 / total
    outs += start_copies(((recip_ref, recip_hbm),), out_sems.at[pl.ds(2, 1)])
    scores = TAU * jnp.sum(jnp.log(total).reshape(N_DEV, QLEN, DIM), axis=1)
    lane = iota((N_DEV, DIM), 1)
    present = (pltpu.roll(meta, DIM - 6 * SLOTS, 1) > 0.5) & (lane < SLOTS)
    teach = (
        pltpu.roll(meta, DIM - 3 * SLOTS, 1)
        + pltpu.roll(meta, DIM - 4 * SLOTS, 1)
        + pltpu.roll(meta, DIM - 5 * SLOTS, 1)
    )
    teach = jnp.where(present, teach, 0.0)
    student = jnp.where(present, jnp.exp(scores), 0.0)
    which = pltpu.roll(meta, DIM - SLOTS, 1) > 0.5
    table_ref[0] = student
    table_ref[1] = teach
    table_ref[2] = jnp.where(which, 1.0, 0.0)
    outs += start_copies(((table_ref, table_hbm),), out_sems.at[pl.ds(3, 1)])
    gain = teach * scores
    columns = []
    for value in (student, gain):
        columns.append(jnp.sum(jnp.where(which, 0.0, value), axis=-1, keepdims=True))
        columns.append(jnp.sum(jnp.where(which, value, 0.0), axis=-1, keepdims=True))
    mixed = jnp.zeros((N_DEV, DIM), F32)
    for j, column in enumerate(columns):
        mixed = jnp.where(lane == j, column, mixed)
    mixed = jnp.concatenate([mixed, jnp.zeros((DIM - N_DEV, DIM), F32)], axis=0)
    part = jnp.transpose(mixed)[0:8, :]
    for s in range(N_DEV):
        sums_ref[s] = part
    wait_copies(outs)
    wait_copies([expo_copy(i) for i in range(N_DEV // CHUNK)])


def halves(one, second):
    return jnp.concatenate(
        [jnp.where(second, 0.0, one).astype(BF), jnp.where(second, one, 0.0).astype(BF)], axis=0
    )


def ahead_kernel(expo_hbm, recip_hbm, table_hbm, second_hbm, weights_ref, table_ref, second_ref,
                 recip_ref, expo_ref, sems, small_sems):
    steps = N_DEV // GROUP
    span = GROUP * QLEN
    fetch = []
    for i in range(steps):
        rows = pl.ds(i * span, span)
        fetch.append(
            start_copies(
                ((recip_hbm.at[rows], recip_ref.at[rows]), (expo_hbm.at[rows], expo_ref.at[rows])), sems.at[i]
            )
        )
    small = start_copies(((table_hbm, table_ref), (second_hbm, second_ref)), small_sems)
    spread = expander(2).astype(BF)
    lane = iota((span, DIM), 1)
    for i in range(steps):
        rows = pl.ds(i * span, span)
        wait_copies(fetch[i])
        recip = recip_ref[rows, :]
        hi = recip.astype(BF).astype(F32)
        lo = recip - hi
        factor = jnp.where(lane < SLOTS, hi, jnp.where(lane < 2 * SLOTS, pltpu.roll(lo, SLOTS, 1), 0.0))
        weights_ref[rows, :] = (expo_ref[rows, :] * dot(factor.astype(BF), spread)).astype(BF)
    wait_copies(small)


def query_kernel(sums_ref, const_hbm, me_ref, table_ref, second_ref, weights_ref, embed_ref, place_hbm,
                 send_hbm, mixed_hbm, loss_hbm,
                 const_ref, loss_ref, wide_ref, send_ref, mixed_ref, smem_ref,
                 sems, out_sems, part_sems):
    small = start_copies(
        ((place_hbm, smem_ref), (const_hbm, const_ref)), sems
    )
    sums = jnp.sum(sums_ref[...], axis=0)
    log_sum = jnp.log(jnp.where(sums > 0.0, sums, 1.0))
    turned = jnp.transpose(jnp.concatenate([sums, jnp.zeros((DIM - 8, DIM), F32)], axis=0))[0:N_DEV, :]
    normal = jnp.where(table_ref[2] > 0.5, turned[:, 1:2], turned[:, 0:1])
    pull = LOSS_SCALE * (table_ref[0] / normal - table_ref[1])
    hi = pull.astype(BF).astype(F32)
    lo = pull - hi
    lane = iota((N_DEV, DIM), 1)
    factor = jnp.where(lane < SLOTS, hi, jnp.where(lane < 2 * SLOTS, pltpu.roll(lo, SLOTS, 1), 0.0))
    wide_ref[...] = dot(factor.astype(BF), expander(2).astype(BF))
    wait_copies(small)
    loss = const_ref[0:2, :] + log_sum[0:2, :] - sums[2:4, :]
    picked = jnp.where(iota((2, DIM), 1) == me_ref[0], loss, 0.0)
    loss_ref[...] = jnp.broadcast_to(jnp.sum(picked, axis=-1, keepdims=True), (2, DIM))
    outs = start_copies(((loss_ref, loss_hbm),), out_sems)

    def part_copies(i):
        some = pl.ds(i * CHUNK, CHUNK)
        rows = pl.ds(i * (CHUNK * QLEN), CHUNK * QLEN)
        return [
            pltpu.make_async_copy(send_ref.at[some], send_hbm.at[some], part_sems.at[i, 0]),
            pltpu.make_async_copy(mixed_ref.at[rows], mixed_hbm.at[rows], part_sems.at[i, 1]),
        ]

    def chunk(i, carry):
        blocks = []
        for u in range(CHUNK):
            s = i * CHUNK + u
            rows = pl.ds(pl.multiple_of(s * QLEN, QLEN), QLEN)
            mixed = weights_ref[rows, :].astype(F32) * wide_ref[pl.ds(s, 1), :]
            mixed_ref[rows, :] = mixed.astype(BF)
            blocks.append(halves(mixed, second_ref[pl.ds(s, 1), :] > 0.5))
        send_copy, mixed_copy = part_copies(i)
        mixed_copy.start()
        for u, both in enumerate(blocks):
            s = i * CHUNK + u
            send_ref[s] = dot(both, stored_rows(embed_ref, smem_ref, s)).astype(BF)
        send_copy.start()
        return carry

    for i in range(N_DEV // CHUNK):
        chunk(i, 0)
    wait_copies(outs)
    for i in range(N_DEV // CHUNK):
        wait_copies(part_copies(i))


def stored_kernel(place_hbm, queries_hbm, second_hbm, mixed_hbm, inverse_hbm, hidden_hbm, embed_ref,
                  preact_hbm, head_ref,
                  preact_ref, hidden_ref, queries_ref, second_ref, mixed_ref, inverse_ref, delta_ref, place_smem,
                  sems, small_sems, mixed_sems, out_sems):
    steps = N_DEV // GROUP
    small = start_copies(
        ((place_hbm, place_smem), (second_hbm, second_ref), (queries_hbm, queries_ref), (inverse_hbm, inverse_ref)),
        small_sems,
    )
    fetch = []
    for i in range(steps):
        rows = pl.ds(i * GROUP * QLEN, GROUP * QLEN)
        fetch += start_copies(((mixed_hbm.at[rows], mixed_ref.at[rows]),), mixed_sems.at[pl.ds(i, 1)])
    copies = token_copies(hidden_hbm, hidden_ref, sems)
    delta_ref[...] = jnp.zeros_like(delta_ref)
    wait_copies(small)

    for i in range(steps):
        fetch[i].wait()
        for copy in copies[i * PARTS // steps : (i + 1) * PARTS // steps]:
            copy.start()
        for s in range(i * GROUP, (i + 1) * GROUP):
            both = halves(mixed_ref[s * QLEN : (s + 1) * QLEN, :].astype(F32), second_ref[s : s + 1, :] > 0.5)
            part = dot(both, queries_ref[s], ROWS_ROWS)
            for k in range(CAP):
                at = pl.ds(pl.multiple_of(place_smem[s, k], 16), PLEN)
                delta_ref[k % LANES, at, :] += part[k * PLEN : (k + 1) * PLEN]
    total = jnp.zeros((DIM, D), F32)
    outs = []
    for i in range(STEPS):
        rows = pl.ds(i * BLOCK, BLOCK)
        unit = embed_ref[rows, :].astype(F32)
        delta = jnp.sum(delta_ref[:, rows, :], axis=0)
        radial = jnp.sum(unit * delta, axis=-1, keepdims=True)
        tangent = delta - unit * radial
        scaled = []
        for j in range(BLOCK // DIM):
            b = i * (BLOCK // DIM) + j
            scaled.append(tangent[j * DIM : (j + 1) * DIM] * inverse_ref[:, b : b + 1])
        preact = jnp.concatenate(scaled, axis=0).astype(BF)
        preact_ref[rows, :] = preact
        outs += start_copies(((preact_ref.at[rows], preact_hbm.at[rows]),), out_sems.at[pl.ds(i, 1)])
        for j in range(i * BLOCK // PART, (i + 1) * BLOCK // PART):
            copies[j].wait()
        total = total + dot(preact, hidden_ref[rows, :], ROWS_ROWS)
    head_ref[...] = jnp.transpose(total)
    wait_copies(outs)


def back_kernel(preact_hbm, weight_hbm, query_ref, grad_hbm, query_grad_hbm,
                preact_ref, weight_ref, grad_ref, query_grad_ref, sems, out_sems):
    copies = start_copies(((weight_hbm, weight_ref), (preact_hbm, preact_ref)), sems)
    wait_copies(copies)
    outs = []
    for i in range(PARTS):

        def tile(t, carry):
            rows = pl.ds(pl.multiple_of(i * PART + t * TILE, TILE), TILE)
            grad_ref[rows, :] = dot(preact_ref[rows, :], weight_ref[...], COLS_COLS).astype(BF)
            return carry

        lax.fori_loop(0, PART // TILE, tile, 0, unroll=2)
        rows = pl.ds(i * PART, PART)
        outs += start_copies(((grad_ref.at[rows], grad_hbm.at[rows]),), out_sems.at[pl.ds(i, 1)])
    query_grad_ref[...] = dot(query_ref[...], weight_ref[...], COLS_COLS).astype(BF)
    outs += start_copies(((query_grad_ref, query_grad_hbm),), out_sems.at[pl.ds(PARTS, 1)])
    wait_copies(outs)


def finish_kernel(recv_ref, hidden_hbm, proj_hbm, head_ref, preact_ref, send_ref,
                  hidden_ref, proj_ref, sems):
    copies = start_copies(((proj_hbm, proj_ref), (hidden_hbm, hidden_ref)), sems)
    delta = jnp.sum(recv_ref[...].astype(F32), axis=0)
    copies[0].wait()
    proj = proj_ref[...]
    inverse = lax.rsqrt(jnp.sum(proj * proj, axis=-1, keepdims=True) + EPS)
    unit = proj * inverse
    radial = jnp.sum(unit * delta, axis=-1, keepdims=True)
    preact = ((delta - unit * radial) * inverse).astype(BF)
    preact_ref[...] = preact
    wait_copies(copies[1:])
    head = head_ref[...] + dot(hidden_ref[...], preact, ROWS_ROWS)
    send_ref[0:HEAD_TILES] = head.reshape(HEAD_TILES, 8, DIM).astype(BF)
    send_ref[HEAD_TILES:N_ALL] = jnp.zeros((N_ALL - HEAD_TILES, 8, DIM), BF)


def reduce_kernel(recv_ref, send_ref):
    total = jnp.sum(recv_ref[...].astype(F32), axis=0).astype(BF)
    send_ref[...] = jnp.broadcast_to(total[None], (N_ALL, 8, DIM))


def shape(dims, kind):
    return jax.ShapeDtypeStruct(dims, kind)


def in_hbm(x):
    return pltpu.with_memory_space_constraint(x, pltpu.HBM)


def in_vmem(x):
    return pltpu.with_memory_space_constraint(x, pltpu.VMEM)


def exchange(x, axes):
    return lax.all_to_all(x, axes, split_axis=0, concat_axis=0, tiled=True)


def estimate(flops, size):
    return pl.CostEstimate(flops=flops, bytes_accessed=size, transcendentals=0)


def on_device(query_hidden, passage_hidden, head_weight, teacher, candidates, storage, lengths):
    query_flat = in_hbm(query_hidden.reshape(QROWS, D))
    flat_hidden = in_hbm(passage_hidden.reshape(TOKENS, D))
    head_weight = in_hbm(head_weight)
    send, query_proj, const = pl.pallas_call(
        request_kernel,
        out_shape=(
            pltpu.HBM((N_DEV, QROWS + META, DIM), BF),
            pltpu.HBM((QROWS, DIM), F32),
            pltpu.HBM((8, DIM), F32),
        ),
        in_specs=[HBM] * 6,
        out_specs=(HBM, HBM, HBM),
        scratch_shapes=[
            pltpu.VMEM((QROWS, D), BF),
            pltpu.VMEM((D, DIM), BF),
            pltpu.VMEM((2, PER_QUERY), F32),
            pltpu.VMEM((2, PER_QUERY), jnp.int32),
            pltpu.VMEM((1, N_DEV * STORED), jnp.int32),
            pltpu.VMEM((1, N_DEV * STORED), jnp.int32),
            pltpu.VMEM((N_DEV, DIM), jnp.int32),
            pltpu.VMEM((N_DEV, DIM), jnp.int32),
            pltpu.VMEM((QROWS, DIM), F32),
            pltpu.VMEM((8, DIM), F32),
            pltpu.VMEM((QROWS, DIM), BF),
            pltpu.VMEM((N_DEV, META, DIM), BF),
            pltpu.SemaphoreType.DMA((6,)),
            pltpu.SemaphoreType.DMA((3,)),
            pltpu.SemaphoreType.DMA((N_DEV,)),
        ],
        compiler_params=params(4),
        name="request",
    )(query_flat, head_weight, in_hbm(teacher), in_hbm(candidates), in_hbm(storage), in_hbm(lengths))
    recv = exchange(send, "dev")

    embed, inverse = pl.pallas_call(
        encode_kernel,
        out_shape=(pltpu.VMEM((TOKENS, DIM), BF), pltpu.HBM((DIM, DIM), F32)),
        in_specs=[HBM, HBM],
        out_specs=(VMEM, HBM),
        scratch_shapes=[
            pltpu.VMEM((TOKENS, D), BF),
            pltpu.VMEM((D, DIM), BF),
            pltpu.VMEM((DIM, DIM), F32),
            pltpu.SemaphoreType.DMA((PARTS + 1,)),
            pltpu.SemaphoreType.DMA,
        ],
        cost_estimate=estimate(2 * TOKENS * D * DIM, 15_000_000),
        compiler_params=params(20),
        name="encode",
    )(flat_hidden, head_weight)

    expo, recip, sums, table, second, place, queries = pl.pallas_call(
        score_kernel,
        out_shape=(
            pltpu.HBM((N_DEV * QLEN, WIDE), F32),
            pltpu.HBM((N_DEV * QLEN, DIM), F32),
            shape((N_DEV, 8, DIM), F32),
            pltpu.HBM((3, N_DEV, DIM), F32),
            pltpu.HBM((N_DEV, WIDE), F32),
            pltpu.HBM((N_DEV, DIM), jnp.int32),
            pltpu.HBM((N_DEV, QROWS, DIM), BF),
        ),
        in_specs=[VMEM] * 2,
        out_specs=(HBM, HBM, VMEM, HBM, HBM, HBM, HBM),
        scratch_shapes=[
            pltpu.VMEM((N_DEV * QLEN, DIM), F32),
            pltpu.VMEM((3, N_DEV, DIM), F32),
            pltpu.VMEM((N_DEV, WIDE), F32),
            pltpu.VMEM((N_DEV, DIM), jnp.int32),
            pltpu.VMEM((N_DEV, DIM), F32),
            pltpu.VMEM((N_DEV, WIDE), F32),
            pltpu.VMEM((N_DEV * QLEN, WIDE), F32),
            pltpu.VMEM((N_DEV * QLEN, WIDE), BF),
            pltpu.SMEM((N_DEV, DIM), jnp.int32),
            pltpu.SemaphoreType.DMA,
            pltpu.SemaphoreType.DMA((N_DEV // CHUNK,)),
            pltpu.SemaphoreType.DMA((5,)),
        ],
        compiler_params=params(14),
        name="score",
    )(recv, in_vmem(embed))
    all_sums = exchange(sums, "dev")

    weights, near_table, near_second = pl.pallas_call(
        ahead_kernel,
        out_shape=(
            pltpu.VMEM((N_DEV * QLEN, WIDE), BF),
            pltpu.VMEM((3, N_DEV, DIM), F32),
            pltpu.VMEM((N_DEV, WIDE), F32),
        ),
        in_specs=[HBM] * 4,
        out_specs=(VMEM,) * 3,
        scratch_shapes=[
            pltpu.VMEM((N_DEV * QLEN, DIM), F32),
            pltpu.VMEM((N_DEV * QLEN, WIDE), F32),
            pltpu.SemaphoreType.DMA((N_DEV // GROUP, 2)),
            pltpu.SemaphoreType.DMA((2,)),
        ],
        cost_estimate=estimate(2 * TOKENS * D * DIM, 15_000_000),
        compiler_params=params(12),
        name="ahead",
    )(in_hbm(expo), in_hbm(recip), in_hbm(table), in_hbm(second))

    me = lax.axis_index("dev").astype(jnp.int32).reshape(1)
    send_delta, mixed, loss = pl.pallas_call(
        query_kernel,
        out_shape=(
            pltpu.HBM((N_DEV, QROWS, DIM), BF),
            pltpu.HBM((N_DEV * QLEN, WIDE), BF),
            pltpu.HBM((2, DIM), F32),
        ),
        in_specs=[VMEM, HBM, SMEM, VMEM, VMEM, VMEM, VMEM, HBM],
        out_specs=(HBM, HBM, HBM),
        scratch_shapes=[
            pltpu.VMEM((8, DIM), F32),
            pltpu.VMEM((2, DIM), F32),
            pltpu.VMEM((N_DEV, WIDE), F32),
            pltpu.VMEM((N_DEV, QROWS, DIM), BF),
            pltpu.VMEM((N_DEV * QLEN, WIDE), BF),
            pltpu.SMEM((N_DEV, DIM), jnp.int32),
            pltpu.SemaphoreType.DMA((2,)),
            pltpu.SemaphoreType.DMA((1,)),
            pltpu.SemaphoreType.DMA((N_DEV // CHUNK, 2)),
        ],
        compiler_params=params(12),
        name="query",
    )(all_sums, in_hbm(const), me, in_vmem(near_table), in_vmem(near_second), in_vmem(weights), in_vmem(embed), in_hbm(place))
    recv_delta = exchange(send_delta, "dev")

    preact, head = pl.pallas_call(
        stored_kernel,
        out_shape=(pltpu.HBM((TOKENS, DIM), BF), pltpu.VMEM((D, DIM), F32)),
        in_specs=[HBM] * 6 + [VMEM],
        out_specs=(HBM, VMEM),
        scratch_shapes=[
            pltpu.VMEM((TOKENS, DIM), BF),
            pltpu.VMEM((TOKENS, D), BF),
            pltpu.VMEM((N_DEV, QROWS, DIM), BF),
            pltpu.VMEM((N_DEV, WIDE), F32),
            pltpu.VMEM((N_DEV * QLEN, WIDE), BF),
            pltpu.VMEM((DIM, DIM), F32),
            pltpu.VMEM((LANES, TOKENS, DIM), F32),
            pltpu.SMEM((N_DEV, DIM), jnp.int32),
            pltpu.SemaphoreType.DMA((PARTS,)),
            pltpu.SemaphoreType.DMA((4,)),
            pltpu.SemaphoreType.DMA((N_DEV // GROUP,)),
            pltpu.SemaphoreType.DMA((STEPS,)),
        ],
        cost_estimate=estimate(4 * TOKENS * D * DIM, 20_000_000),
        compiler_params=params(40),
        name="stored",
    )(
        in_hbm(place), in_hbm(queries), in_hbm(second), in_hbm(mixed), in_hbm(inverse), flat_hidden, in_vmem(embed)
    )

    query_preact, send_head = pl.pallas_call(
        finish_kernel,
        out_shape=(pltpu.VMEM((QROWS, DIM), BF), shape((N_ALL, 8, DIM), BF)),
        in_specs=[VMEM, HBM, HBM, VMEM],
        out_specs=(VMEM,) * 2,
        scratch_shapes=[
            pltpu.VMEM((QROWS, D), BF),
            pltpu.VMEM((QROWS, DIM), F32),
            pltpu.SemaphoreType.DMA((2,)),
        ],
        compiler_params=params(8),
        name="finish",
    )(recv_delta, query_flat, in_hbm(query_proj), in_vmem(head))
    recv_head = exchange(send_head, ("group", "dev"))

    passage_grad, query_grad = pl.pallas_call(
        back_kernel,
        out_shape=(pltpu.HBM((TOKENS, D), BF), pltpu.HBM((QROWS, D), BF)),
        in_specs=[HBM, HBM, VMEM],
        out_specs=(HBM, HBM),
        scratch_shapes=[
            pltpu.VMEM((TOKENS, DIM), BF),
            pltpu.VMEM((D, DIM), BF),
            pltpu.VMEM((TOKENS, D), BF),
            pltpu.VMEM((QROWS, D), BF),
            pltpu.SemaphoreType.DMA((2,)),
            pltpu.SemaphoreType.DMA((PARTS + 1,)),
        ],
        cost_estimate=estimate(2 * TOKENS * D * DIM, 15_000_000),
        compiler_params=params(20),
        name="back",
    )(in_hbm(preact), head_weight, in_vmem(query_preact))

    send_total = pl.pallas_call(
        reduce_kernel,
        out_shape=shape((N_ALL, 8, DIM), BF),
        in_specs=[VMEM],
        out_specs=VMEM,
        compiler_params=params(4),
        name="reduce",
    )(recv_head)
    head_all = exchange(send_total, ("group", "dev"))
    head_grad = head_all[:HEAD_TILES].reshape(D, DIM).astype(F32)
    return (
        loss[:, 0],
        head_grad,
        query_grad.reshape(2, QLEN, D),
        passage_grad.reshape(STORED, PLEN, D),
    )


def solution(mesh):
    return jax.shard_map(
        on_device,
        mesh=mesh,
        in_specs=(
            P(("group", "dev"), None, None),
            P(("group", "dev"), None, None),
            P(),
            P(("group", "dev"), None),
            P(("group", "dev"), None),
            P("group", None),
            P("group", None),
        ),
        out_specs=(
            P(("group", "dev")),
            P(),
            P(("group", "dev"), None, None),
            P(("group", "dev"), None, None),
        ),
        check_vma=False,
    )
```
